32 devices in a mesh: dp: 4 (over z), fsdp: 8 (over y, x, core).
Axes of the slice: x: 2, y: 2, z: 4, core: 2. Of those that a mesh axis runs over, the one named last changes fastest.
Arguments:
- layer_input: bfloat16 [4, 1536, 2048], P('dp', 'fsdp'), may hold values from -6 to 6
- output_grad: bfloat16 [4, 1536, 2048], P('dp', 'fsdp'), may hold values from -6 to 6
- layer_keep: int32 [4], P('dp'), may hold values 0 or 1
- group_ids: int32 [4], P('dp'), may hold values from 0 to 1
- exit_scale: float32 [2], replicated, may hold values from 0.5 to 2
- doc_lengths: int32 [4, 4], P('dp'), may hold values from 1 to 1392, 1536 in all within a row
- attention_gain: bfloat16 [2048], P(('dp', 'fsdp')), may hold values from 0.25 to 1.75
- query_weight: bfloat16 [2048, 2048], P(('dp', 'fsdp')), may hold values from -0.125 to 0.125
- key_weight: bfloat16 [2048, 512], P(('dp', 'fsdp')), may hold values from -0.125 to 0.125
- value_weight: bfloat16 [2048, 512], P(('dp', 'fsdp')), may hold values from -0.125 to 0.125
- output_weight: bfloat16 [2048, 2048], P(('dp', 'fsdp')), may hold values from -4 to 4
- feedforward_gain: bfloat16 [2048], P(('dp', 'fsdp')), may hold values from 0.25 to 1.75
- gate_weight: bfloat16 [2048, 5632], P('fsdp', 'dp'), may hold values from -0.125 to 0.125
- up_weight: bfloat16 [2048, 5632], P('fsdp', 'dp'), may hold values from -0.125 to 0.125
- down_weight: bfloat16 [5632, 2048], P(('dp', 'fsdp')), may hold values from -0.078125 to 0.078125
Outputs:
- layer_output: bfloat16 [4, 1536, 2048], P('dp', 'fsdp')
- input_gradient: float32 [4, 1536, 2048], P('dp', 'fsdp')
- attention_gain_gradient: float32 [2048], P(('dp', 'fsdp'))
- query_gradient: float32 [2048, 2048], P(('dp', 'fsdp'))
- key_gradient: float32 [2048, 512], P(('dp', 'fsdp'))
- value_gradient: float32 [2048, 512], P(('dp', 'fsdp'))
- output_gradient: float32 [2048, 2048], P(('dp', 'fsdp'))
- feedforward_gain_gradient: float32 [2048], P(('dp', 'fsdp'))
- gate_gradient: float32 [2048, 5632], P('fsdp', 'dp')
- up_gradient: float32 [2048, 5632], P('fsdp', 'dp')
- down_gradient: float32 [5632, 2048], P(('dp', 'fsdp'))
The draws below stay inside these ranges and needn't reach their ends.
Inputs may be any that keep to these rules, and one draw needn't show every extreme that they name: `layer_keep`: 1 applies the layer to the sequence, 0 skips it. `doc_lengths`: each row sums to 1536; its longest document has exactly 1392 tokens.
All inputs are finite; a program needn't handle non-finite values. No bound on the sum of `layer_keep` on one device may be relied on, other than what follows from the above.
Results may differ from the reference program's by a relative error of at most 0.019.
Values may be sent and summed in bfloat16 or wider, within the bound.
No kernel may reach another device: no remote copies, remote signals or barrier semaphores. Data moves between devices by JAX's collectives and lax.ppermute only.
A program may use at most 512 MiB of HBM per device.

```python
import math
import jax
import jax.numpy as jnp
import numpy as np
from jax import lax

D = 2048
HEADS = 16
KV_HEADS = 4
HEAD_DIM = 128
FF = 5632
TOK_DEV = 192
NDOC = 4
GROUPS = 2
KV_WIDTH = 512
LENGTH = 1536
SEQS = 4


def plant(result, own_key, low, largest):
    longest = result.shape.index(max(result.shape))
    spots = []
    for shift in (0, 1):
        where = [jax.random.randint(jax.random.fold_in(own_key, axis), (), 0, length) for axis, length in enumerate(result.shape)]
        where[longest] = (where[longest] + shift) % result.shape[longest]
        spots.append(tuple(where))
    return result.at[spots[0]].set(low).at[spots[1]].set(largest)


def shard_levels(key, dims, shards, smallest, largest):
    level, own = 1.0, jax.random.fold_in(key, 6)
    for axis_at, shards_of in shards:
        draws = jnp.exp(jax.random.uniform(jax.random.fold_in(own, axis_at), (shards_of,), jnp.float32, smallest / len(shards), largest / len(shards)))
        level = level * jnp.repeat(draws, dims[axis_at] // shards_of).reshape([-1 if axis == axis_at else 1 for axis in range(len(dims))])
    return level


def length_profile(count, total, most, skew):
    loads = [(1 << 20) // math.isqrt(rank ** skew) + 1 for rank in range(2, count + 1)]
    rest, holding = total - most - (count - 1), [1] * (count - 1)
    while rest > 0:
        movable = [i for i in range(count - 1) if holding[i] < most]
        mass, budget = sum([loads[i] for i in movable]), rest
        for i in movable:
            more = min(most - holding[i], max(1, budget * loads[i] // mass), rest)
            holding[i] = holding[i] + more
            rest = rest - more
    return np.array([most] + holding)


def ragged_sizes(key, number_of, total, most, slope):
    if number_of == 2:
        one = jax.random.randint(key, (), max(1, total - most), min(most, total - 1) + 1)
        return jnp.stack([one, total - one])
    sizes = jnp.asarray(length_profile(number_of, total, most, slope), jnp.int32)
    twos = (number_of - 1) // 2
    giver, sink = sizes[1:1 + 2 * twos:2], sizes[2:2 + 2 * twos:2]
    room = jnp.minimum(giver - 1, most - sink)
    moved = jax.random.randint(jax.random.fold_in(key, 1), (twos,), 0, 1 << 20) % (room + 1)
    sizes = sizes.at[1:1 + 2 * twos:2].set(giver - moved).at[2:2 + 2 * twos:2].set(sink + moved)
    return sizes[jax.random.permutation(jax.random.fold_in(key, 2), number_of)]


def gaussian(own_key, shape, deviation, reach, split=(), held_as=jnp.bfloat16):
    entries = jax.random.normal(own_key, shape, jnp.float32) * deviation
    if len(split) > 0:
        entries = shard_levels(own_key, shape, split, -0.22, 0.18) * entries
    return jnp.clip(entries, min=-reach, max=reach).astype(held_as)


def setup_inputs(seed: int = 0) -> dict:
    streams_of = jax.random.split(jax.random.key(seed), 16)
    layer_input = gaussian(streams_of[0], (SEQS, LENGTH, D), 1.0, 6.0, ((0, 4), (1, 8)))
    output_grad = gaussian(streams_of[1], (SEQS, LENGTH, D), 1.0, 6.0, ((0, 4), (1, 8)))
    layer_keep = plant((jax.random.randint(streams_of[2], (SEQS,), 0, 4) < 3).astype(jnp.int32), jax.random.fold_in(streams_of[2], 1), 0, 1)
    group_ids = plant(jax.random.randint(streams_of[3], (SEQS,), 0, GROUPS), jax.random.fold_in(streams_of[3], 1), 0, GROUPS - 1).astype(jnp.int32)
    exit_scale = jnp.clip(jnp.exp(jax.random.uniform(streams_of[4], (GROUPS,), jnp.float32, math.log(0.5), math.log(2.0))), 0.5, 2.0)
    doc_lengths = jax.vmap(lambda own: ragged_sizes(own, NDOC, LENGTH, LENGTH - 3 * TOK_DEV // 4, 0))(jax.random.split(streams_of[5], SEQS)).reshape((SEQS, NDOC)).astype(jnp.int32)
    attention_gain = jnp.clip(1.0 + 0.15 * jax.random.normal(streams_of[6], (D,), jnp.float32), 0.25, 1.75).astype(jnp.bfloat16)
    query_weight = gaussian(streams_of[7], (D, D), D ** -0.5, 0.125, ((0, 32),))
    key_weight = gaussian(streams_of[8], (D, KV_WIDTH), D ** -0.5, 0.125, ((0, 32),))
    value_weight = gaussian(streams_of[9], (D, KV_WIDTH), D ** -0.5, 0.125, ((0, 32),))
    output_weight = gaussian(streams_of[10], (D, D), (max(1, 2 * D // LENGTH)) ** -0.5, 4.0, ((0, 32),))
    feedforward_gain = jnp.clip(1.0 + 0.15 * jax.random.normal(streams_of[11], (D,), jnp.float32), 0.25, 1.75).astype(jnp.bfloat16)
    gate_weight = gaussian(streams_of[12], (D, FF), D ** -0.5, 0.125, ((0, 8), (1, 4)))
    up_weight = gaussian(streams_of[13], (D, FF), D ** -0.5, 0.125, ((0, 8), (1, 4)))
    down_weight = gaussian(streams_of[14], (FF, D), FF ** -0.5, 0.078125, ((0, 32),))
    return dict(layer_input=layer_input, output_grad=output_grad, layer_keep=layer_keep, group_ids=group_ids, exit_scale=exit_scale, doc_lengths=doc_lengths, attention_gain=attention_gain, query_weight=query_weight, key_weight=key_weight, value_weight=value_weight, output_weight=output_weight, feedforward_gain=feedforward_gain, gate_weight=gate_weight, up_weight=up_weight, down_weight=down_weight)


@jax.custom_vjp
def low(v):
    return lax.optimization_barrier(v.astype(jnp.bfloat16)).astype(jnp.float32)

@jax.custom_vjp
def low_back(v):
    return v

def low_keep(v):
    return (low(v), None)

def low_pass(kept, grad):
    return (grad,)

def back_keep(v):
    return (v, None)

def back_low(kept, grad):
    return (low(grad),)
low.defvjp(low_keep, low_pass)
low_back.defvjp(back_keep, back_low)
norm_eps = 1e-05
rope_base = 10000.0
mask_fill = -1e+30

def matmul_high(left, right):
    return jnp.dot(left, right, precision=lax.Precision.HIGHEST, preferred_element_type=jnp.float32)

def rotate(vectors, cosine, sine_part):
    half_dim = vectors.shape[-1] // 2
    lower_half = vectors[..., :half_dim]
    upper_half = vectors[..., half_dim:]
    return jnp.concatenate([lower_half * cosine - upper_half * sine_part, upper_half * cosine + lower_half * sine_part], -1)

def rms_normed(rows, gain):
    inv_rms = lax.rsqrt(lax.optimization_barrier(jnp.mean(rows * rows, -1, keepdims=True)) + norm_eps)
    return rows * inv_rms * gain

def sequence_layer(rows, keep, lengths, params):
    attention_gain, query_weight, key_weight, value_weight, output_weight, feedforward_gain, gate_weight, up_weight, down_weight = params
    seq_length = rows.shape[0]
    group_size = HEADS // KV_HEADS
    positions = jnp.arange(seq_length, dtype=jnp.int32)
    ends = jnp.cumsum(lengths.astype(jnp.int32))
    documents = lax.optimization_barrier(jnp.sum((positions[:, None] >= ends[None, :]).astype(jnp.int32), 1))
    half_dim = HEAD_DIM // 2
    frequency = rope_base ** (-(2.0 * jnp.arange(half_dim, dtype=jnp.float32)) / HEAD_DIM)
    angles = positions.astype(jnp.float32)[:, None] * frequency[None, :]
    cosine = jnp.cos(angles)[:, None, :]
    sine_part = jnp.sin(angles)[:, None, :]
    normed = low(rms_normed(rows, attention_gain))
    query_raw = low_back(matmul_high(normed, query_weight)).reshape(seq_length, HEADS, HEAD_DIM)
    queries = low(rotate(query_raw, cosine, sine_part)).reshape(seq_length, KV_HEADS, group_size, HEAD_DIM)
    key_raw = low_back(matmul_high(normed, key_weight)).reshape(seq_length, KV_HEADS, HEAD_DIM)
    keys = low(rotate(key_raw, cosine, sine_part))
    values = low_back(low(matmul_high(normed, value_weight))).reshape(seq_length, KV_HEADS, HEAD_DIM)
    block_rows = math.gcd(seq_length, 512)
    score_scale = 1.0 / math.sqrt(HEAD_DIM)

    def query_block(index):
        offset = index * block_rows
        block_queries = lax.dynamic_slice_in_dim(queries, offset, block_rows, 0)
        block_pos = lax.dynamic_slice_in_dim(positions, offset, block_rows, 0)
        block_doc = lax.dynamic_slice_in_dim(documents, offset, block_rows, 0)
        scores = low_back(jnp.einsum('tkgd,skd->kgts', block_queries, keys, precision=lax.Precision.HIGHEST) * score_scale)
        allowed = (positions[None, :] <= block_pos[:, None]) & (documents[None, :] == block_doc[:, None])
        scores = jnp.where(allowed[None, None], scores, mask_fill)
        shifted = jnp.exp(scores - lax.optimization_barrier(jnp.max(scores, -1, keepdims=True)))
        probability = low(shifted / lax.optimization_barrier(jnp.sum(shifted, -1, keepdims=True)))
        mixed = jnp.einsum('kgts,skd->tkgd', probability, values, precision=lax.Precision.HIGHEST)
        return mixed.reshape(block_rows, HEADS * HEAD_DIM)
    attended = lax.map(jax.checkpoint(query_block), jnp.arange(seq_length // block_rows, dtype=jnp.int32))
    attended = low_back(low(attended.reshape(seq_length, HEADS * HEAD_DIM)))
    branch_attention = low_back(matmul_high(attended, output_weight))
    middle = rows + branch_attention
    normed_second = low(rms_normed(middle, feedforward_gain))
    gate_pre = low_back(matmul_high(normed_second, gate_weight))
    upward = low_back(matmul_high(normed_second, up_weight))
    hidden = low(gate_pre * (1.0 / (1.0 + jnp.exp(-gate_pre))) * upward)
    branch_feed = low_back(matmul_high(hidden, down_weight))
    return rows + keep * (branch_attention + branch_feed)

def forward(inputs, keep_all, lengths_all, params):

    def per_sequence(carry, sliced):
        rows, keep, lengths = sliced
        return (carry, jax.checkpoint(sequence_layer)(rows, keep, lengths, params))
    _, outputs = lax.scan(per_sequence, jnp.zeros((), jnp.float32), (inputs, keep_all, lengths_all))
    return outputs

def reference(layer_input, output_grad, layer_keep, group_ids, exit_scale, doc_lengths, attention_gain, query_weight, key_weight, value_weight, output_weight, feedforward_gain, gate_weight, up_weight, down_weight):
    params = tuple((weight.astype(jnp.float32) for weight in (attention_gain, query_weight, key_weight, value_weight, output_weight, feedforward_gain, gate_weight, up_weight, down_weight)))
    keep_all = layer_keep.astype(jnp.float32)

    def wrapped(inputs, *weights):
        return forward(inputs, keep_all, doc_lengths, weights)
    outputs, pullback = jax.vjp(wrapped, layer_input.astype(jnp.float32), *params)
    picked = lax.optimization_barrier(jnp.sum(jnp.where(jnp.arange(GROUPS, dtype=jnp.int32)[None, :] == group_ids[:, None], exit_scale[None, :].astype(jnp.float32), 0.0), 1))
    cotangent = output_grad.astype(jnp.float32) * picked[:, None, None]
    grads = pullback(cotangent)
    return (outputs.astype(jnp.bfloat16), grads[0], grads[1], grads[2], grads[3], grads[4], grads[5], grads[6], grads[7], grads[8], grads[9])
```

```python
import math

import jax
import jax.numpy as jnp
from jax import lax
from jax.sharding import PartitionSpec as P

HEADS = 16
KV_HEADS = 4
HEAD_DIM = 128


norm_eps = 1e-05
rope_base = 10000.0
mask_fill = -1e30


def dot_plain(left, right):
    return jnp.dot(left, right, preferred_element_type=jnp.float32)


def dot_right_t(left, right):
    return lax.dot_general(
        left, right, (((1,), (1,)), ((), ())), preferred_element_type=jnp.float32
    )


def dot_left_t(left, right):
    return lax.dot_general(
        left, right, (((0,), (0,)), ((), ())), preferred_element_type=jnp.float32
    )


def rotary_tables(positions):
    half_dim = HEAD_DIM // 2
    frequency = rope_base ** (-(2.0 * jnp.arange(half_dim, dtype=jnp.float32)) / HEAD_DIM)
    angles = positions.astype(jnp.float32)[:, None] * frequency[None, :]
    return (jnp.cos(angles)[:, None, :], jnp.sin(angles)[:, None, :])


def rotate(vectors, cosine, sine_part):
    half_dim = vectors.shape[-1] // 2
    lower_half = vectors[..., :half_dim]
    upper_half = vectors[..., half_dim:]
    return jnp.concatenate(
        [
            lower_half * cosine - upper_half * sine_part,
            upper_half * cosine + lower_half * sine_part,
        ],
        -1,
    )


def rms_scale(rows):
    return lax.rsqrt(jnp.mean(rows * rows, -1, keepdims=True) + norm_eps)


def norm_back(grad_normed, rows, inv_rms, gain):
    weighted = grad_normed * gain.astype(jnp.float32)
    gain_grad = jnp.sum(grad_normed * rows * inv_rms, 0)
    grad_rows = inv_rms * weighted - rows * inv_rms**3 * jnp.mean(
        weighted * rows, -1, keepdims=True
    )
    return (gain_grad, grad_rows)


def allowed_mask(query_pos, query_doc, key_pos, key_doc):
    return (key_pos[None, :] <= query_pos[:, None]) & (key_doc[None, :] == query_doc[:, None])


def block_scores(queries, key_block, allowed):
    scores = jnp.einsum(
        "tkgd,skd->kgts", queries, key_block, preferred_element_type=jnp.float32
    ) * (1.0 / math.sqrt(HEAD_DIM))
    return jnp.where(allowed[None, None], scores, mask_fill)


def log_normalizer(queries, layout):
    query_pos, query_doc, key_blocks, value_blocks, key_pos_blocks, key_doc_blocks = layout
    shape_rows = (queries.shape[1], queries.shape[2], queries.shape[0])
    initial = (jnp.full(shape_rows, mask_fill, jnp.float32), jnp.zeros(shape_rows, jnp.float32))

    def advance(carry, sliced):
        run_max, run_sum = carry
        key_block, key_pos, key_doc = sliced
        allowed = allowed_mask(query_pos, query_doc, key_pos, key_doc)
        scores = block_scores(queries, key_block, allowed)
        new_max = jnp.maximum(run_max, jnp.max(scores, -1))
        expo = jnp.where(allowed[None, None], jnp.exp(scores - new_max[..., None]), 0.0)
        run_sum = run_sum * jnp.exp(run_max - new_max) + jnp.sum(expo, -1)
        return ((new_max, run_sum), None)

    (run_max, run_sum), _ = lax.scan(advance, initial, (key_blocks, key_pos_blocks, key_doc_blocks))
    return run_max + jnp.log(run_sum)


def attend_values(queries, layout, normalizer):
    query_pos, query_doc, key_blocks, value_blocks, key_pos_blocks, key_doc_blocks = layout
    initial = jnp.zeros(queries.shape, jnp.float32)

    def advance(carry, sliced):
        key_block, value_block, key_pos, key_doc = sliced
        allowed = allowed_mask(query_pos, query_doc, key_pos, key_doc)
        scores = block_scores(queries, key_block, allowed)
        probs_low = jnp.where(
            allowed[None, None], jnp.exp(scores - normalizer[..., None]), 0.0
        ).astype(jnp.bfloat16)
        return (
            carry
            + jnp.einsum(
                "kgts,skd->tkgd", probs_low, value_block, preferred_element_type=jnp.float32
            ),
            None,
        )

    summed, _ = lax.scan(
        advance, initial, (key_blocks, value_blocks, key_pos_blocks, key_doc_blocks)
    )
    return summed


def attend_back(queries, layout, normalizer, grad_out_low, delta):
    query_pos, query_doc, key_blocks, value_blocks, key_pos_blocks, key_doc_blocks = layout
    initial = jnp.zeros(queries.shape, jnp.float32)

    def advance(carry, sliced):
        key_block, value_block, key_pos, key_doc = sliced
        allowed = allowed_mask(query_pos, query_doc, key_pos, key_doc)
        scores = block_scores(queries, key_block, allowed)
        probs = jnp.where(allowed[None, None], jnp.exp(scores - normalizer[..., None]), 0.0)
        probs_low = probs.astype(jnp.bfloat16)
        grad_prob = jnp.einsum(
            "tkgd,skd->kgts", grad_out_low, value_block, preferred_element_type=jnp.float32
        )
        grad_score = (probs * (grad_prob - delta[..., None])).astype(jnp.bfloat16)
        carry = carry + jnp.einsum(
            "kgts,skd->tkgd", grad_score, key_block, preferred_element_type=jnp.float32
        )
        key_part = jnp.einsum(
            "kgts,tkgd->skd", grad_score, queries, preferred_element_type=jnp.float32
        )
        value_part = jnp.einsum(
            "kgts,tkgd->skd", probs_low, grad_out_low, preferred_element_type=jnp.float32
        )
        return (carry, (key_part, value_part))

    query_acc, (key_parts, value_parts) = lax.scan(
        advance, initial, (key_blocks, value_blocks, key_pos_blocks, key_doc_blocks)
    )
    seq_length = key_parts.shape[0] * key_parts.shape[1]
    return (
        query_acc,
        key_parts.reshape(seq_length, KV_HEADS * HEAD_DIM),
        value_parts.reshape(seq_length, KV_HEADS * HEAD_DIM),
    )


def front(rows, attention_set, cosine, sine_part):
    attention_gain, query_weight, key_weight, value_weight = attention_set
    tokens = rows.shape[0]
    inv_first = rms_scale(rows)
    normed = (rows * inv_first * attention_gain.astype(jnp.float32)).astype(jnp.bfloat16)
    query_raw = dot_plain(normed, query_weight).reshape(tokens, HEADS, HEAD_DIM)
    query_rot = (
        rotate(query_raw, cosine, sine_part)
        .astype(jnp.bfloat16)
        .reshape(tokens, KV_HEADS, HEADS // KV_HEADS, HEAD_DIM)
    )
    key_raw = dot_plain(normed, key_weight).reshape(tokens, KV_HEADS, HEAD_DIM)
    key_rot = (
        rotate(key_raw, cosine, sine_part).astype(jnp.bfloat16).reshape(tokens, KV_HEADS * HEAD_DIM)
    )
    value_low = dot_plain(normed, value_weight).astype(jnp.bfloat16)
    return (inv_first, normed, query_rot, key_rot, value_low)


def make_layout(query_pos, query_doc, all_doc, keys_all, values_all):
    seq_length = keys_all.shape[0]
    block_rows = math.gcd(seq_length, 512)
    count = seq_length // block_rows
    key_blocks = keys_all.reshape(count, block_rows, KV_HEADS, HEAD_DIM)
    value_blocks = values_all.reshape(count, block_rows, KV_HEADS, HEAD_DIM)
    key_pos_blocks = jnp.arange(seq_length, dtype=jnp.int32).reshape(count, block_rows)
    key_doc_blocks = all_doc.reshape(count, block_rows)
    return (query_pos, query_doc, key_blocks, value_blocks, key_pos_blocks, key_doc_blocks)


def per_device(
    layer_input,
    output_grad,
    layer_keep,
    group_ids,
    exit_scale,
    doc_lengths,
    attention_gain,
    query_weight,
    key_weight,
    value_weight,
    output_weight,
    feedforward_gain,
    gate_weight,
    up_weight,
    down_weight,
):
    tokens = layer_input.shape[1]
    rows = layer_input[0].astype(jnp.float32)
    seq_length = tokens * lax.axis_size("fsdp")
    all_pos = jnp.arange(seq_length, dtype=jnp.int32)
    first_row = lax.axis_index("fsdp") * tokens
    query_pos = first_row + jnp.arange(tokens, dtype=jnp.int32)
    order = jnp.arange(doc_lengths.shape[1], dtype=jnp.int32)
    ends = jnp.sum(jnp.where(order[None, :] <= order[:, None], doc_lengths[0][None, :], 0), 1)
    all_doc = jnp.sum((all_pos[:, None] >= ends[None, :]).astype(jnp.int32), 1)
    query_doc = lax.dynamic_slice_in_dim(all_doc, first_row, tokens)
    cosine, sine_part = rotary_tables(query_pos)
    keep = layer_keep[0].astype(jnp.float32)
    gathered = (
        lax.all_gather(attention_gain, ("dp", "fsdp"), axis=0, tiled=True),
        lax.all_gather(feedforward_gain, ("dp", "fsdp"), axis=0, tiled=True),
        lax.all_gather(query_weight, ("dp", "fsdp"), axis=0, tiled=True),
        lax.all_gather(key_weight, ("dp", "fsdp"), axis=0, tiled=True),
        lax.all_gather(value_weight, ("dp", "fsdp"), axis=0, tiled=True),
        lax.all_gather(output_weight, ("dp", "fsdp"), axis=0, tiled=True),
    )
    gain_first, gain_second, query_full, key_full, value_full, output_full = gathered
    feed_block = (
        lax.all_gather(gate_weight, "fsdp", axis=0, tiled=True),
        lax.all_gather(up_weight, "fsdp", axis=0, tiled=True),
        lax.all_gather(down_weight, "fsdp", axis=0, tiled=True),
    )
    gate_use, up_use = (
        lax.all_gather(feed_block[0], "dp", axis=1, tiled=True),
        lax.all_gather(feed_block[1], "dp", axis=1, tiled=True),
    )
    down_use = lax.all_gather(feed_block[2], "dp", axis=0, tiled=True)
    front_parts = front(rows, (gain_first, query_full, key_full, value_full), cosine, sine_part)
    inv_first, normed, query_rot, key_rot, value_low = front_parts
    keys_all, values_all = (
        lax.all_gather(key_rot, "fsdp", axis=0, tiled=True),
        lax.all_gather(value_low, "fsdp", axis=0, tiled=True),
    )
    layout = make_layout(query_pos, query_doc, all_doc, keys_all, values_all)
    normalizer = log_normalizer(query_rot, layout)
    attended = attend_values(query_rot, layout, normalizer)
    attended_low = attended.reshape(tokens, HEADS * HEAD_DIM).astype(jnp.bfloat16)
    branch_attention = dot_plain(attended_low, output_full)
    middle = rows + branch_attention
    inv_second = rms_scale(middle)
    normed_second = (middle * inv_second * gain_second.astype(jnp.float32)).astype(jnp.bfloat16)
    gate_pre = dot_plain(normed_second, gate_use)
    upward = dot_plain(normed_second, up_use)
    sigmoid_gate = 1.0 / (1.0 + jnp.exp(-gate_pre))
    silu_gate = gate_pre * sigmoid_gate
    hidden_low = (silu_gate * upward).astype(jnp.bfloat16)
    branch_feed = dot_plain(hidden_low, down_use)
    output = (rows + keep * (branch_attention + branch_feed)).astype(jnp.bfloat16)
    picked = jnp.sum(
        jnp.where(jnp.arange(exit_scale.shape[0], dtype=jnp.int32) == group_ids[0], exit_scale, 0.0)
    )
    cotangent = output_grad[0].astype(jnp.float32) * picked
    direct = keep * cotangent
    direct_low = direct.astype(jnp.bfloat16)
    grad_hidden = dot_right_t(direct_low, down_use)
    down_term = dot_left_t(hidden_low, direct_low)
    grad_gate_low = (
        grad_hidden * upward * sigmoid_gate * (1.0 + gate_pre * (1.0 - sigmoid_gate))
    ).astype(jnp.bfloat16)
    grad_up_low = (grad_hidden * silu_gate).astype(jnp.bfloat16)
    normed_term = dot_right_t(grad_gate_low, gate_use) + dot_right_t(grad_up_low, up_use)
    gate_term = dot_left_t(normed_second, grad_gate_low)
    up_term = dot_left_t(normed_second, grad_up_low)
    gate_part, up_part = (
        lax.psum_scatter(
            gate_term.astype(jnp.bfloat16), "dp", scatter_dimension=1, tiled=True
        ).astype(jnp.float32),
        lax.psum_scatter(
            up_term.astype(jnp.bfloat16), "dp", scatter_dimension=1, tiled=True
        ).astype(jnp.float32),
    )
    down_part = lax.psum_scatter(
        down_term.astype(jnp.bfloat16), "dp", scatter_dimension=0, tiled=True
    )
    feed_grads = (
        lax.psum_scatter(
            gate_part.astype(jnp.bfloat16), "fsdp", scatter_dimension=0, tiled=True
        ).astype(jnp.float32),
        lax.psum_scatter(
            up_part.astype(jnp.bfloat16), "fsdp", scatter_dimension=0, tiled=True
        ).astype(jnp.float32),
        lax.psum_scatter(down_part, "fsdp", scatter_dimension=0, tiled=True).astype(jnp.float32),
    )
    second_gain_grad, grad_middle = norm_back(normed_term, middle, inv_second, gain_second)
    grad_branch_low = (direct + grad_middle).astype(jnp.bfloat16)
    grad_attended_low = dot_right_t(grad_branch_low, output_full).astype(jnp.bfloat16)
    output_grad_weight = dot_left_t(attended_low, grad_branch_low)
    grad_heads = grad_attended_low.reshape(attended.shape)
    delta = jnp.transpose(jnp.sum(grad_heads.astype(jnp.float32) * attended, -1), (1, 2, 0))
    query_acc, key_grad_all, value_grad_all = attend_back(
        query_rot, layout, normalizer, grad_heads, delta
    )
    key_grad_mine, value_grad_mine = (
        lax.psum_scatter(
            key_grad_all.astype(jnp.bfloat16), "fsdp", scatter_dimension=0, tiled=True
        ).astype(jnp.float32),
        lax.psum_scatter(
            value_grad_all.astype(jnp.bfloat16), "fsdp", scatter_dimension=0, tiled=True
        ).astype(jnp.float32),
    )
    score_scale = 1.0 / math.sqrt(HEAD_DIM)
    grad_query_low = (
        rotate((query_acc * score_scale).reshape(tokens, HEADS, HEAD_DIM), cosine, -sine_part)
        .astype(jnp.bfloat16)
        .reshape(tokens, HEADS * HEAD_DIM)
    )
    grad_key_low = (
        rotate(
            (key_grad_mine * score_scale).reshape(tokens, KV_HEADS, HEAD_DIM), cosine, -sine_part
        )
        .astype(jnp.bfloat16)
        .reshape(tokens, KV_HEADS * HEAD_DIM)
    )
    grad_value_low = value_grad_mine.astype(jnp.bfloat16)
    grad_normed = (
        dot_right_t(grad_query_low, query_full)
        + dot_right_t(grad_key_low, key_full)
        + dot_right_t(grad_value_low, value_full)
    )
    query_grad = dot_left_t(normed, grad_query_low)
    key_grad = dot_left_t(normed, grad_key_low)
    value_grad = dot_left_t(normed, grad_value_low)
    first_gain_grad, grad_rows = norm_back(grad_normed, rows, inv_first, gain_first)
    input_grad = cotangent + grad_middle + grad_rows
    attention_grads = (
        lax.psum_scatter(first_gain_grad, ("dp", "fsdp"), scatter_dimension=0, tiled=True),
        lax.psum_scatter(query_grad, ("dp", "fsdp"), scatter_dimension=0, tiled=True),
        lax.psum_scatter(key_grad, ("dp", "fsdp"), scatter_dimension=0, tiled=True),
        lax.psum_scatter(value_grad, ("dp", "fsdp"), scatter_dimension=0, tiled=True),
        lax.psum_scatter(output_grad_weight, ("dp", "fsdp"), scatter_dimension=0, tiled=True),
        lax.psum_scatter(second_gain_grad, ("dp", "fsdp"), scatter_dimension=0, tiled=True),
    )
    return (
        output[None],
        input_grad[None],
        attention_grads[0],
        attention_grads[1],
        attention_grads[2],
        attention_grads[3],
        attention_grads[4],
        attention_grads[5],
        feed_grads[0],
        feed_grads[1],
        feed_grads[2],
    )


def solution(mesh):
    placed = (
        P("dp", "fsdp", None),
        P("dp", "fsdp", None),
        P("dp"),
        P("dp"),
        P(),
        P("dp", None),
        P(("dp", "fsdp")),
        P(("dp", "fsdp"), None),
        P(("dp", "fsdp"), None),
        P(("dp", "fsdp"), None),
        P(("dp", "fsdp"), None),
        P(("dp", "fsdp")),
        P("fsdp", "dp"),
        P("fsdp", "dp"),
        P(("dp", "fsdp"), None),
    )
    return jax.shard_map(
        per_device,
        mesh=mesh,
        in_specs=placed,
        out_specs=(
            P("dp", "fsdp", None),
            P("dp", "fsdp", None),
            P(("dp", "fsdp")),
            P(("dp", "fsdp"), None),
            P(("dp", "fsdp"), None),
            P(("dp", "fsdp"), None),
            P(("dp", "fsdp"), None),
            P(("dp", "fsdp")),
            P("fsdp", "dp"),
            P("fsdp", "dp"),
            P(("dp", "fsdp"), None),
        ),
        check_vma=False,
    )
```

```python
import functools
import math

import jax
import jax.numpy as jnp
from jax import lax
from jax.experimental import pallas as pl
from jax.experimental.pallas import tpu as pltpu
from jax.sharding import PartitionSpec as P

HEADS = 16
KV_HEADS = 4
HEAD_DIM = 128

norm_eps = 1e-05
rope_base = 10000.0
mask_fill = -1e30
score_scale = 1.0 / math.sqrt(HEAD_DIM)
f32 = jnp.float32
bf16 = jnp.bfloat16


def dot_plain(left, right):
    return jnp.dot(left, right, preferred_element_type=f32)


def dot_right_t(left, right):
    return lax.dot_general(left, right, (((1,), (1,)), ((), ())), preferred_element_type=f32)


def dot_left_t(left, right):
    return lax.dot_general(left, right, (((0,), (0,)), ((), ())), preferred_element_type=f32)


def rotary_tables(length):
    half_dim = HEAD_DIM // 2
    frequency = rope_base ** (-(2.0 * jnp.arange(half_dim, dtype=f32)) / HEAD_DIM)
    angles = jnp.arange(length, dtype=jnp.int32).astype(f32)[:, None] * frequency[None, :]
    return (jnp.cos(angles)[:, None, :], jnp.sin(angles)[:, None, :])


def rotate(vectors, cosine, sine_part):
    half_dim = vectors.shape[-1] // 2
    lower_half = vectors[..., :half_dim]
    upper_half = vectors[..., half_dim:]
    return jnp.concatenate(
        [
            lower_half * cosine - upper_half * sine_part,
            upper_half * cosine + lower_half * sine_part,
        ],
        -1,
    )


def rms_scale(rows):
    return lax.rsqrt(jnp.mean(rows * rows, -1, keepdims=True) + norm_eps)


def after(value, *earlier):
    return lax.optimization_barrier((value, *earlier))[0]


UP = [(0, 1), (1, 2), (2, 3)]
DOWN = [(3, 2), (2, 1), (1, 0)]


def pick(plane, options):
    return lax.select_n(plane, *options)


def plane_gather(block):
    count = lax.axis_size("dp")
    plane = lax.axis_index("dp")
    if count != 4:
        whole = lax.all_gather(block, "dp", axis=0)
        return [whole[i] for i in range(count)], [jnp.int32(i) for i in range(count)]
    up1 = lax.ppermute(block, "dp", UP)
    down1 = lax.ppermute(block, "dp", DOWN)
    up2 = lax.ppermute(up1, "dp", UP[1:])
    down2 = lax.ppermute(down1, "dp", DOWN[1:])
    up3 = lax.ppermute(up2, "dp", UP[2:])
    down3 = lax.ppermute(down2, "dp", DOWN[2:])
    blocks = [
        block,
        pick(plane, [down1, down1, up1, up1]),
        pick(plane, [down2, up1, down1, up2]),
        pick(plane, [down3, down2, up2, up3]),
    ]
    table = jnp.array([[0, 1, 2, 3], [1, 2, 0, 3], [2, 1, 3, 0], [3, 2, 1, 0]], jnp.int32)
    mine = lax.dynamic_index_in_dim(table, plane, 0, keepdims=False)
    return blocks, [mine[i] for i in range(4)]


def add_low(left, right):
    return (left.astype(f32) + right.astype(f32)).astype(left.dtype)


def plane_scatter(parts):
    count = lax.axis_size("dp")
    plane = lax.axis_index("dp")
    if count != 4:
        return lax.psum_scatter(jnp.stack(parts), "dp", scatter_dimension=0, tiled=False).astype(f32)
    own, first, second, third = parts
    up3 = lax.ppermute(third, "dp", UP[:1])
    down3 = lax.ppermute(third, "dp", DOWN[:1])
    middle = pick(plane, [second, third, third, second])
    up2 = lax.ppermute(add_low(middle, up3), "dp", UP[:2])
    down2 = lax.ppermute(add_low(middle, down3), "dp", DOWN[:2])
    up1 = lax.ppermute(add_low(pick(plane, [first, first, second, second]), up2), "dp", UP)
    down1 = lax.ppermute(add_low(pick(plane, [second, second, first, first]), down2), "dp", DOWN)
    return own.astype(f32) + up1.astype(f32) + down1.astype(f32)


def slots_of(whole):
    count = lax.axis_size("dp")
    if count != 4:
        return [whole[i] for i in range(count)]
    plane = lax.axis_index("dp")
    table = jnp.array([[0, 1, 2, 3], [1, 2, 0, 3], [2, 1, 3, 0], [3, 2, 1, 0]], jnp.int32)
    mine = lax.dynamic_index_in_dim(table, plane, 0, keepdims=False)
    return [lax.dynamic_index_in_dim(whole, mine[i], 0, keepdims=False) for i in range(4)]


def in_order(blocks, planes):
    if lax.axis_size("dp") != 4:
        return jnp.stack(blocks)
    whole = jnp.zeros((4, *blocks[0].shape), blocks[0].dtype)
    for block, plane in zip(blocks, planes):
        whole = lax.dynamic_update_index_in_dim(whole, block, plane, 0)
    return whole


def block_rows_of(length):
    return math.gcd(length, 256)


def transposed_scores(keys, queries, starts, low, high, width):
    scores = dot_right_t(keys, queries) * score_scale
    key_pos = lax.broadcasted_iota(jnp.int32, (width, high - low), 0)
    query_pos = lax.broadcasted_iota(jnp.int32, (width, high - low), 1) + low
    allowed = (key_pos <= query_pos) & (key_pos >= starts)
    return scores, allowed


def attend_kernel(rows_of, q_ref, k_ref, vt_ref, starts_ref, out_ref, norm_ref):
    length = q_ref.shape[0]
    for low in range(0, length, rows_of):
        high = low + rows_of
        starts = starts_ref[:, low:high]
        scores, allowed = transposed_scores(
            k_ref[:high, :], q_ref[low:high, :], starts, low, high, high
        )
        scores = jnp.where(allowed, scores, mask_fill)
        top = jnp.max(scores, 0, keepdims=True)
        expo = jnp.exp(scores - top)
        total = jnp.sum(expo, 0, keepdims=True)
        probs = (expo * (1.0 / total)).astype(bf16)
        mixed = dot_plain(vt_ref[:, :high], probs)
        out_ref[low:high, :] = jnp.transpose(mixed).astype(out_ref.dtype)
        norm_ref[0, :, low:high] = top + jnp.log(total)


def attend(queries, keys, values, starts):
    length, width = queries.shape
    heads = width // HEAD_DIM
    return pl.pallas_call(
        functools.partial(attend_kernel, block_rows_of(length)),
        grid=(heads,),
        in_specs=[
            pl.BlockSpec((length, HEAD_DIM), lambda h: (0, h)),
            pl.BlockSpec((length, HEAD_DIM), lambda h: (0, 0)),
            pl.BlockSpec((HEAD_DIM, length), lambda h: (0, 0)),
            pl.BlockSpec((1, length), lambda h: (0, 0)),
        ],
        out_specs=[
            pl.BlockSpec((length, HEAD_DIM), lambda h: (0, h)),
            pl.BlockSpec((1, 1, length), lambda h: (h, 0, 0)),
        ],
        out_shape=[
            jax.ShapeDtypeStruct((length, width), bf16),
            jax.ShapeDtypeStruct((heads, 1, length), f32),
        ],
        compiler_params=pltpu.CompilerParams(vmem_limit_bytes=48 << 20),
        cost_estimate=pl.CostEstimate(
            flops=3 * heads * length * length * HEAD_DIM,
            bytes_accessed=8 * length * width,
            transcendentals=heads * length * length,
        ),
        name="attend",
    )(queries, keys, jnp.transpose(values), starts)


def attend_back_kernel(
    rows_of, q_ref, k_ref, kt_ref, v_ref, starts_ref, norm_ref, out_ref, grad_ref, dq_ref, dk_ref, dv_ref
):
    length = q_ref.shape[0]

    @pl.when(pl.program_id(0) == 0)
    def _():
        dk_ref[...] = jnp.zeros_like(dk_ref)
        dv_ref[...] = jnp.zeros_like(dv_ref)

    for low in range(0, length, rows_of):
        high = low + rows_of
        starts = starts_ref[:, low:high]
        queries = q_ref[low:high, :]
        grads = grad_ref[low:high, :]
        scores, allowed = transposed_scores(k_ref[:high, :], queries, starts, low, high, high)
        probs = jnp.where(allowed, jnp.exp(scores - norm_ref[0, :, low:high]), 0.0)
        grad_prob = dot_right_t(v_ref[:high, :], grads)
        weighed = jnp.transpose(grads.astype(f32) * out_ref[low:high, :].astype(f32))
        delta = jnp.sum(weighed, 0, keepdims=True)
        grad_score = (probs * (grad_prob - delta)).astype(bf16)
        dv_ref[:high, :] += dot_plain(probs.astype(bf16), grads)
        dk_ref[:high, :] += dot_plain(grad_score, queries)
        dq_ref[low:high, :] = jnp.transpose(dot_plain(kt_ref[:, :high], grad_score))


def attend_back(queries, keys, values, starts, norm, out, grads):
    length, width = queries.shape
    heads = width // HEAD_DIM
    by_head = pl.BlockSpec((length, HEAD_DIM), lambda h: (0, h))
    shared = pl.BlockSpec((length, HEAD_DIM), lambda h: (0, 0))
    return pl.pallas_call(
        functools.partial(attend_back_kernel, block_rows_of(length)),
        grid=(heads,),
        in_specs=[
            by_head,
            shared,
            pl.BlockSpec((HEAD_DIM, length), lambda h: (0, 0)),
            shared,
            pl.BlockSpec((1, length), lambda h: (0, 0)),
            pl.BlockSpec((1, 1, length), lambda h: (h, 0, 0)),
            by_head,
            by_head,
        ],
        out_specs=[by_head, shared, shared],
        out_shape=[
            jax.ShapeDtypeStruct((length, width), f32),
            jax.ShapeDtypeStruct((length, HEAD_DIM), f32),
            jax.ShapeDtypeStruct((length, HEAD_DIM), f32),
        ],
        compiler_params=pltpu.CompilerParams(vmem_limit_bytes=56 << 20),
        cost_estimate=pl.CostEstimate(
            flops=7 * heads * length * length * HEAD_DIM,
            bytes_accessed=16 * length * width,
            transcendentals=heads * length * length,
        ),
        name="attend_back",
    )(queries, keys, jnp.transpose(keys), values, starts, norm, out, grads)


def per_device(
    layer_input,
    output_grad,
    layer_keep,
    group_ids,
    exit_scale,
    doc_lengths,
    attention_gain,
    query_weight,
    key_weight,
    value_weight,
    output_weight,
    feedforward_gain,
    gate_weight,
    up_weight,
    down_weight,
):
    tokens, width = layer_input.shape[1:]
    ring = lax.axis_size("fsdp")
    planes = lax.axis_size("dp")
    place = lax.axis_index("fsdp")
    length = tokens * ring
    own_rows = query_weight.shape[0]
    heads = HEADS // ring
    own_width = heads * HEAD_DIM
    ff_own = gate_weight.shape[1]
    rows = layer_input[0].astype(f32)
    keep = layer_keep[0].astype(f32)

    inv_first = rms_scale(rows)
    normed = lax.all_gather((rows * inv_first).astype(bf16), "fsdp", axis=0, tiled=True)

    gain_mine = attention_gain.astype(f32)[:, None]
    sharers = ring // KV_HEADS
    cols = own_width + 2 * HEAD_DIM

    def spread(weight):
        heads_of = (weight.astype(f32) * gain_mine).astype(bf16).reshape(own_rows, KV_HEADS, 1, HEAD_DIM)
        return jnp.broadcast_to(heads_of, (own_rows, KV_HEADS, sharers, HEAD_DIM)).reshape(
            own_rows, ring, HEAD_DIM
        )

    query_scaled = (query_weight.astype(f32) * gain_mine).astype(bf16).reshape(own_rows, ring, own_width)
    sent = jnp.concatenate([query_scaled, spread(key_weight), spread(value_weight)], -1)
    sent = jnp.transpose(sent, (1, 0, 2)).reshape(ring * own_rows, cols)
    plane_cols = lax.all_to_all(sent, "fsdp", split_axis=0, concat_axis=0, tiled=True)
    project = in_order(*plane_gather(plane_cols)).reshape(width, cols)

    picked = jnp.sum(
        jnp.where(jnp.arange(exit_scale.shape[0], dtype=jnp.int32) == group_ids[0], exit_scale, 0.0)
    )
    cotangent = output_grad[0].astype(f32) * picked
    direct = keep * cotangent
    direct_all = plane_gather(after(direct.astype(bf16), plane_cols))[0]
    direct_all = jnp.concatenate(direct_all, 0)

    gain_second = lax.all_gather(
        lax.all_gather(feedforward_gain, "fsdp", axis=0, tiled=False), "dp", axis=0, tiled=False
    ).reshape(width).astype(f32)

    output_full = lax.all_gather(after(output_weight, normed), ("dp", "fsdp"), axis=0, tiled=True)
    gate_up = jnp.concatenate([gate_weight, up_weight], 1)
    gate_up = lax.all_gather(after(gate_up, output_full), "fsdp", axis=0, tiled=True)
    down_use = lax.all_gather(after(down_weight, gate_up), "fsdp", axis=0, tiled=True)

    cosine, sine_part = rotary_tables(length)
    ends = jnp.sum(
        jnp.where(
            jnp.arange(doc_lengths.shape[1])[None, :] <= jnp.arange(doc_lengths.shape[1])[:, None],
            doc_lengths[0][None, :],
            0,
        ),
        1,
    )
    positions = jnp.arange(length, dtype=jnp.int32)
    starts = jnp.max(jnp.where(positions[None, :] >= ends[:, None], ends[:, None], 0), 0)[None, :]
    raw = dot_plain(normed, project)
    rotated = rotate(
        raw[:, : own_width + HEAD_DIM].reshape(length, heads + 1, HEAD_DIM), cosine, sine_part
    ).astype(bf16)
    queries = rotated[:, :heads].reshape(length, own_width)
    keys = rotated[:, heads]
    values = raw[:, own_width + HEAD_DIM :].astype(bf16)
    mixed, norm = attend(queries, keys, values, starts)
    attended_low = lax.all_to_all(mixed, "fsdp", split_axis=0, concat_axis=1, tiled=True)
    branch_attention = dot_plain(attended_low, output_full)
    middle = rows + branch_attention
    inv_second = rms_scale(middle)
    second_mine = (middle * inv_second * gain_second).astype(bf16)

    second_all = jnp.concatenate(plane_gather(second_mine)[0], 0)
    gate_use, up_use = gate_up[:, :ff_own], gate_up[:, ff_own:]
    gate_pre = dot_plain(second_all, gate_use)
    upward = dot_plain(second_all, up_use)
    sigmoid_gate = 1.0 / (1.0 + jnp.exp(-gate_pre))
    silu_gate = gate_pre * sigmoid_gate
    hidden_low = (silu_gate * upward).astype(bf16)
    grad_hidden = dot_right_t(direct_all, down_use)
    grad_gate_low = (
        grad_hidden * upward * sigmoid_gate * (1.0 + gate_pre * (1.0 - sigmoid_gate))
    ).astype(bf16)
    grad_up_low = (grad_hidden * silu_gate).astype(bf16)
    grad_both = jnp.concatenate([grad_gate_low, grad_up_low], 1)
    second_terms = dot_right_t(grad_both, gate_up).astype(bf16).reshape(planes, tokens, width)
    grad_second = plane_scatter([second_terms[i] for i in range(planes)])

    down_term = dot_left_t(hidden_low, direct_all).astype(bf16)
    gate_up_term = dot_left_t(second_all, grad_both).astype(bf16)
    gate_up_grad = lax.psum_scatter(gate_up_term, "fsdp", scatter_dimension=0, tiled=True).astype(f32)
    down_grad = lax.psum_scatter(
        after(down_term, gate_up_grad), "fsdp", scatter_dimension=0, tiled=True
    ).astype(f32)
    branch_terms = dot_plain(hidden_low, down_use).astype(bf16).reshape(planes, tokens, width)
    branch_feed = plane_scatter(
        [after(branch_terms, grad_second)[i] for i in range(planes)]
    )
    output = (rows + keep * (branch_attention + branch_feed)).astype(bf16)

    second_gain_term = jnp.sum(grad_second * middle * inv_second, 0)
    weighted = grad_second * gain_second
    grad_middle = inv_second * weighted - middle * inv_second**3 * jnp.mean(
        weighted * middle, -1, keepdims=True
    )
    grad_branch_low = (direct + grad_middle).astype(bf16)
    grad_attended_low = dot_right_t(grad_branch_low, output_full).astype(bf16)
    grad_heads = lax.all_to_all(grad_attended_low, "fsdp", split_axis=1, concat_axis=0, tiled=True)
    attended_by_owner = jnp.transpose(
        attended_low.reshape(tokens, planes, ring, own_rows), (0, 2, 1, 3)
    ).reshape(tokens, width)
    output_term = dot_left_t(attended_by_owner, grad_branch_low).astype(bf16)
    output_plane = lax.psum_scatter(
        after(output_term, down_grad), "fsdp", scatter_dimension=0, tiled=True
    )

    dq, dk, dv = attend_back(queries, keys, values, starts, norm, mixed, grad_heads)
    turned = rotate(
        (jnp.concatenate([dq, dk], 1) * score_scale).reshape(length, heads + 1, HEAD_DIM),
        cosine,
        -sine_part,
    ).astype(bf16)
    grad_cols = jnp.concatenate([turned.reshape(length, own_width + HEAD_DIM), dv.astype(bf16)], 1)
    normed_terms = dot_right_t(grad_cols, project).astype(bf16)
    weighted_first = lax.psum_scatter(normed_terms, "fsdp", scatter_dimension=0, tiled=True).astype(f32)
    grad_rows = inv_first * weighted_first - rows * inv_first**3 * jnp.mean(
        weighted_first * rows, -1, keepdims=True
    )
    input_grad = cotangent + grad_middle + grad_rows

    project_term = dot_left_t(normed, grad_cols).astype(bf16).reshape(planes, ring * own_rows, cols)
    project_plane = plane_scatter(slots_of(project_term)).astype(bf16)
    back = lax.all_to_all(project_plane, "fsdp", split_axis=0, concat_axis=0, tiled=True)
    back = back.reshape(ring, own_rows, cols).astype(f32)

    def collect(low):
        parts = back[:, :, low : low + HEAD_DIM].reshape(KV_HEADS, sharers, own_rows, HEAD_DIM)
        return jnp.transpose(jnp.sum(parts, 1), (1, 0, 2)).reshape(own_rows, KV_HEADS * HEAD_DIM)

    query_plain = jnp.transpose(back[:, :, :own_width], (1, 0, 2)).reshape(own_rows, width)
    key_plain = collect(own_width)
    value_plain = collect(own_width + HEAD_DIM)
    first_gain_grad = (
        jnp.sum(query_plain * query_weight.astype(f32), 1)
        + jnp.sum(key_plain * key_weight.astype(f32), 1)
        + jnp.sum(value_plain * value_weight.astype(f32), 1)
    )
    output_grad_weight = plane_scatter(slots_of(output_plane.reshape(planes, own_rows, width)))
    second_gain_all = lax.psum(lax.psum(second_gain_term, "fsdp"), "dp")
    mine = (lax.axis_index("dp") * ring + place) * own_rows
    second_gain_grad = lax.dynamic_slice_in_dim(second_gain_all, mine, own_rows)
    return (
        output[None],
        input_grad[None],
        first_gain_grad,
        query_plain * gain_mine,
        key_plain * gain_mine,
        value_plain * gain_mine,
        output_grad_weight,
        second_gain_grad,
        gate_up_grad[:, :ff_own],
        gate_up_grad[:, ff_own:],
        down_grad,
    )


def solution(mesh):
    both = ("dp", "fsdp")
    return jax.shard_map(
        per_device,
        mesh=mesh,
        in_specs=(
            P("dp", "fsdp", None),
            P("dp", "fsdp", None),
            P("dp"),
            P("dp"),
            P(),
            P("dp", None),
            P(both),
            P(both, None),
            P(both, None),
            P(both, None),
            P(both, None),
            P(both),
            P("fsdp", "dp"),
            P("fsdp", "dp"),
            P(both, None),
        ),
        out_specs=(
            P("dp", "fsdp", None),
            P("dp", "fsdp", None),
            P(both),
            P(both, None),
            P(both, None),
            P(both, None),
            P(both, None),
            P(both),
            P("fsdp", "dp"),
            P("fsdp", "dp"),
            P(both, None),
        ),
        check_vma=False,
    )
```

```python
import functools
import math

import jax
import jax.numpy as jnp
from jax import lax
from jax.experimental import pallas as pl
from jax.experimental.pallas import tpu as pltpu
from jax.sharding import PartitionSpec as P

HEADS = 16
KV_HEADS = 4
HEAD_DIM = 128

norm_eps = 1e-05
rope_base = 10000.0
mask_fill = -1e30
score_scale = 1.0 / math.sqrt(HEAD_DIM)
f32 = jnp.float32
bf16 = jnp.bfloat16


def dot_plain(left, right):
    return jnp.dot(left, right, preferred_element_type=f32)


def dot_right_t(left, right):
    return lax.dot_general(left, right, (((1,), (1,)), ((), ())), preferred_element_type=f32)


def dot_left_t(left, right):
    return lax.dot_general(left, right, (((0,), (0,)), ((), ())), preferred_element_type=f32)


def rotary_tables(length):
    half_dim = HEAD_DIM // 2
    frequency = rope_base ** (-(2.0 * jnp.arange(half_dim, dtype=f32)) / HEAD_DIM)
    angles = jnp.arange(length, dtype=jnp.int32).astype(f32)[:, None] * frequency[None, :]
    return (jnp.cos(angles)[:, None, :], jnp.sin(angles)[:, None, :])


def rotate(vectors, cosine, sine_part):
    half_dim = vectors.shape[-1] // 2
    lower_half = vectors[..., :half_dim]
    upper_half = vectors[..., half_dim:]
    return jnp.concatenate(
        [
            lower_half * cosine - upper_half * sine_part,
            upper_half * cosine + lower_half * sine_part,
        ],
        -1,
    )


def rms_scale(rows):
    return lax.rsqrt(jnp.mean(rows * rows, -1, keepdims=True) + norm_eps)


def after(value, *earlier):
    return lax.optimization_barrier((value, *earlier))[0]


UP = [(0, 1), (1, 2), (2, 3)]
DOWN = [(3, 2), (2, 1), (1, 0)]


def pick(plane, options):
    return lax.select_n(plane, *options)


def plane_gather(block):
    count = lax.axis_size("dp")
    plane = lax.axis_index("dp")
    if count != 4:
        whole = lax.all_gather(block, "dp", axis=0)
        return [whole[i] for i in range(count)], [jnp.int32(i) for i in range(count)]
    up1 = lax.ppermute(block, "dp", UP)
    down1 = lax.ppermute(block, "dp", DOWN)
    up2 = lax.ppermute(up1, "dp", UP[1:])
    down2 = lax.ppermute(down1, "dp", DOWN[1:])
    up3 = lax.ppermute(up2, "dp", UP[2:])
    down3 = lax.ppermute(down2, "dp", DOWN[2:])
    blocks = [
        block,
        pick(plane, [down1, down1, up1, up1]),
        pick(plane, [down2, up1, down1, up2]),
        pick(plane, [down3, down2, up2, up3]),
    ]
    table = jnp.array([[0, 1, 2, 3], [1, 2, 0, 3], [2, 1, 3, 0], [3, 2, 1, 0]], jnp.int32)
    mine = lax.dynamic_index_in_dim(table, plane, 0, keepdims=False)
    return blocks, [mine[i] for i in range(4)]


def add_low(left, right):
    return (left.astype(f32) + right.astype(f32)).astype(left.dtype)


def plane_scatter(parts):
    count = lax.axis_size("dp")
    plane = lax.axis_index("dp")
    if count != 4:
        return lax.psum_scatter(jnp.stack(parts), "dp", scatter_dimension=0, tiled=False).astype(f32)
    own, first, second, third = parts
    up3 = lax.ppermute(third, "dp", UP[:1])
    down3 = lax.ppermute(third, "dp", DOWN[:1])
    middle = pick(plane, [second, third, third, second])
    up2 = lax.ppermute(add_low(middle, up3), "dp", UP[:2])
    down2 = lax.ppermute(add_low(middle, down3), "dp", DOWN[:2])
    up1 = lax.ppermute(add_low(pick(plane, [first, first, second, second]), up2), "dp", UP)
    down1 = lax.ppermute(add_low(pick(plane, [second, second, first, first]), down2), "dp", DOWN)
    return own.astype(f32) + up1.astype(f32) + down1.astype(f32)


def slots_of(whole):
    count = lax.axis_size("dp")
    if count != 4:
        return [whole[i] for i in range(count)]
    plane = lax.axis_index("dp")
    table = jnp.array([[0, 1, 2, 3], [1, 2, 0, 3], [2, 1, 3, 0], [3, 2, 1, 0]], jnp.int32)
    mine = lax.dynamic_index_in_dim(table, plane, 0, keepdims=False)
    return [lax.dynamic_index_in_dim(whole, mine[i], 0, keepdims=False) for i in range(4)]


def in_order(blocks, planes):
    if lax.axis_size("dp") != 4:
        return jnp.stack(blocks)
    whole = jnp.zeros((4, *blocks[0].shape), blocks[0].dtype)
    for block, plane in zip(blocks, planes):
        whole = lax.dynamic_update_index_in_dim(whole, block, plane, 0)
    return whole


FLIP = {bit: [(i, i ^ bit) for i in range(8)] for bit in (1, 2, 4, 6)}


def flip(block, bit):
    return lax.ppermute(block, "fsdp", FLIP[bit])


def output_rows(term):
    place = lax.axis_index("fsdp")
    plane = lax.axis_index("dp")
    rows = term.shape[0] // 4
    blocks = term.reshape(4, rows, term.shape[1])
    y, x, core = place // 4, (place // 2) % 2, place % 2
    by_group = jnp.zeros_like(blocks)
    for a in (0, 1):
        for b in (0, 1):
            sent = lax.dynamic_index_in_dim(blocks, 2 * (x ^ a) + (y ^ b), 0, keepdims=False)
            moves = [
                (i, 4 * (i % 2) + 2 * ((i // 2) % 2 ^ a) + ((i // 4) ^ b)) for i in range(8)
            ]
            got = lax.ppermute(sent, "fsdp", moves)
            by_group = lax.dynamic_update_index_in_dim(by_group, got, 2 * (core ^ b) + (x ^ a), 0)
    return plane_scatter(slots_of(by_group))


def block_rows_of(length):
    return math.gcd(length, 256)


def transposed_scores(keys, queries, starts, low, high, width):
    scores = dot_right_t(keys, queries) * score_scale
    key_pos = lax.broadcasted_iota(jnp.int32, (width, high - low), 0)
    query_pos = lax.broadcasted_iota(jnp.int32, (width, high - low), 1) + low
    allowed = (key_pos <= query_pos) & (key_pos >= starts)
    return scores, allowed


def attend_kernel(rows_of, q_ref, k_ref, vt_ref, starts_ref, out_ref, norm_ref):
    length = q_ref.shape[0]
    for low in range(0, length, rows_of):
        high = low + rows_of
        starts = starts_ref[:, low:high]
        scores, allowed = transposed_scores(
            k_ref[:high, :], q_ref[low:high, :], starts, low, high, high
        )
        scores = jnp.where(allowed, scores, mask_fill)
        top = jnp.max(scores, 0, keepdims=True)
        expo = jnp.exp(scores - top)
        total = jnp.sum(expo, 0, keepdims=True)
        probs = (expo * (1.0 / total)).astype(bf16)
        mixed = dot_plain(vt_ref[:, :high], probs)
        out_ref[low:high, :] = jnp.transpose(mixed).astype(out_ref.dtype)
        norm_ref[0, :, low:high] = top + jnp.log(total)


def attend(queries, keys, values, starts):
    length, width = queries.shape
    heads = width // HEAD_DIM
    return pl.pallas_call(
        functools.partial(attend_kernel, block_rows_of(length)),
        grid=(heads,),
        in_specs=[
            pl.BlockSpec((length, HEAD_DIM), lambda h: (0, h)),
            pl.BlockSpec((length, HEAD_DIM), lambda h: (0, 0)),
            pl.BlockSpec((HEAD_DIM, length), lambda h: (0, 0)),
            pl.BlockSpec((1, length), lambda h: (0, 0)),
        ],
        out_specs=[
            pl.BlockSpec((length, HEAD_DIM), lambda h: (0, h)),
            pl.BlockSpec((1, 1, length), lambda h: (h, 0, 0)),
        ],
        out_shape=[
            jax.ShapeDtypeStruct((length, width), bf16),
            jax.ShapeDtypeStruct((heads, 1, length), f32),
        ],
        compiler_params=pltpu.CompilerParams(vmem_limit_bytes=48 << 20),
        cost_estimate=pl.CostEstimate(
            flops=3 * heads * length * length * HEAD_DIM,
            bytes_accessed=8 * length * width,
            transcendentals=heads * length * length,
        ),
        name="attend",
    )(queries, keys, jnp.transpose(values), starts)


def attend_back_kernel(
    rows_of, q_ref, k_ref, kt_ref, v_ref, starts_ref, norm_ref, out_ref, grad_ref, dq_ref, dk_ref, dv_ref
):
    length = q_ref.shape[0]

    @pl.when(pl.program_id(0) == 0)
    def _():
        dk_ref[...] = jnp.zeros_like(dk_ref)
        dv_ref[...] = jnp.zeros_like(dv_ref)

    for low in range(0, length, rows_of):
        high = low + rows_of
        starts = starts_ref[:, low:high]
        queries = q_ref[low:high, :]
        grads = grad_ref[low:high, :]
        scores, allowed = transposed_scores(k_ref[:high, :], queries, starts, low, high, high)
        probs = jnp.where(allowed, jnp.exp(scores - norm_ref[0, :, low:high]), 0.0)
        grad_prob = dot_right_t(v_ref[:high, :], grads)
        weighed = jnp.transpose(grads.astype(f32) * out_ref[low:high, :].astype(f32))
        delta = jnp.sum(weighed, 0, keepdims=True)
        grad_score = (probs * (grad_prob - delta)).astype(bf16)
        dv_ref[:high, :] += dot_plain(probs.astype(bf16), grads)
        dk_ref[:high, :] += dot_plain(grad_score, queries)
        dq_ref[low:high, :] = jnp.transpose(dot_plain(kt_ref[:, :high], grad_score))


def attend_back(queries, keys, values, starts, norm, out, grads):
    length, width = queries.shape
    heads = width // HEAD_DIM
    by_head = pl.BlockSpec((length, HEAD_DIM), lambda h: (0, h))
    shared = pl.BlockSpec((length, HEAD_DIM), lambda h: (0, 0))
    return pl.pallas_call(
        functools.partial(attend_back_kernel, block_rows_of(length)),
        grid=(heads,),
        in_specs=[
            by_head,
            shared,
            pl.BlockSpec((HEAD_DIM, length), lambda h: (0, 0)),
            shared,
            pl.BlockSpec((1, length), lambda h: (0, 0)),
            pl.BlockSpec((1, 1, length), lambda h: (h, 0, 0)),
            by_head,
            by_head,
        ],
        out_specs=[by_head, shared, shared],
        out_shape=[
            jax.ShapeDtypeStruct((length, width), f32),
            jax.ShapeDtypeStruct((length, HEAD_DIM), f32),
            jax.ShapeDtypeStruct((length, HEAD_DIM), f32),
        ],
        compiler_params=pltpu.CompilerParams(vmem_limit_bytes=56 << 20),
        cost_estimate=pl.CostEstimate(
            flops=7 * heads * length * length * HEAD_DIM,
            bytes_accessed=16 * length * width,
            transcendentals=heads * length * length,
        ),
        name="attend_back",
    )(queries, keys, jnp.transpose(keys), values, starts, norm, out, grads)


def per_device(
    layer_input,
    output_grad,
    layer_keep,
    group_ids,
    exit_scale,
    doc_lengths,
    attention_gain,
    query_weight,
    key_weight,
    value_weight,
    output_weight,
    feedforward_gain,
    gate_weight,
    up_weight,
    down_weight,
):
    tokens, width = layer_input.shape[1:]
    ring = lax.axis_size("fsdp")
    planes = lax.axis_size("dp")
    place = lax.axis_index("fsdp")
    length = tokens * ring
    own_rows = query_weight.shape[0]
    heads = HEADS // ring
    own_width = heads * HEAD_DIM
    ff_own = gate_weight.shape[1]
    rows = layer_input[0].astype(f32)
    keep = layer_keep[0].astype(f32)

    inv_first = rms_scale(rows)
    normed = lax.all_gather((rows * inv_first).astype(bf16), "fsdp", axis=0, tiled=True)

    gain_mine = attention_gain.astype(f32)[:, None]
    sharers = ring // KV_HEADS
    cols = own_width + 2 * HEAD_DIM

    def spread(weight):
        heads_of = (weight.astype(f32) * gain_mine).astype(bf16).reshape(own_rows, KV_HEADS, 1, HEAD_DIM)
        return jnp.broadcast_to(heads_of, (own_rows, KV_HEADS, sharers, HEAD_DIM)).reshape(
            own_rows, ring, HEAD_DIM
        )

    query_scaled = (query_weight.astype(f32) * gain_mine).astype(bf16).reshape(own_rows, ring, own_width)
    sent = jnp.concatenate([query_scaled, spread(key_weight), spread(value_weight)], -1)
    sent = jnp.transpose(sent, (1, 0, 2)).reshape(ring * own_rows, cols)
    plane_cols = lax.all_to_all(sent, "fsdp", split_axis=0, concat_axis=0, tiled=True)
    project = in_order(*plane_gather(plane_cols)).reshape(width, cols)

    picked = jnp.sum(
        jnp.where(jnp.arange(exit_scale.shape[0], dtype=jnp.int32) == group_ids[0], exit_scale, 0.0)
    )
    cotangent = output_grad[0].astype(f32) * picked
    direct = keep * cotangent
    direct_all = plane_gather(after(direct.astype(bf16), project))[0]
    direct_all = jnp.concatenate(direct_all, 0)

    gain_second = lax.all_gather(
        lax.all_gather(feedforward_gain, "fsdp", axis=0, tiled=False), "dp", axis=0, tiled=False
    ).reshape(width).astype(f32)

    output_full = lax.all_gather(output_weight, ("dp", "fsdp"), axis=0, tiled=True)
    gate_up = jnp.concatenate([gate_weight, up_weight], 1)
    gate_up = lax.all_gather(gate_up, "fsdp", axis=0, tiled=True)
    down_use = lax.all_gather(down_weight, "fsdp", axis=0, tiled=True)

    cosine, sine_part = rotary_tables(length)
    ends = jnp.sum(
        jnp.where(
            jnp.arange(doc_lengths.shape[1])[None, :] <= jnp.arange(doc_lengths.shape[1])[:, None],
            doc_lengths[0][None, :],
            0,
        ),
        1,
    )
    positions = jnp.arange(length, dtype=jnp.int32)
    starts = jnp.max(jnp.where(positions[None, :] >= ends[:, None], ends[:, None], 0), 0)[None, :]
    raw = dot_plain(normed, project)
    rotated = rotate(
        raw[:, : own_width + HEAD_DIM].reshape(length, heads + 1, HEAD_DIM), cosine, sine_part
    ).astype(bf16)
    queries = rotated[:, :heads].reshape(length, own_width)
    keys = rotated[:, heads]
    values = raw[:, own_width + HEAD_DIM :].astype(bf16)
    mixed, norm = attend(queries, keys, values, starts)
    attended_low = lax.all_to_all(mixed, "fsdp", split_axis=0, concat_axis=1, tiled=True)
    branch_attention = dot_plain(attended_low, output_full)
    middle = rows + branch_attention
    inv_second = rms_scale(middle)
    second_mine = (middle * inv_second * gain_second).astype(bf16)

    second_all = jnp.concatenate(plane_gather(second_mine)[0], 0)
    gate_use, up_use = gate_up[:, :ff_own], gate_up[:, ff_own:]
    gate_pre = dot_plain(second_all, gate_use)
    upward = dot_plain(second_all, up_use)
    sigmoid_gate = 1.0 / (1.0 + jnp.exp(-gate_pre))
    silu_gate = gate_pre * sigmoid_gate
    hidden_low = (silu_gate * upward).astype(bf16)
    grad_hidden = dot_right_t(direct_all, down_use)
    grad_gate_low = (
        grad_hidden * upward * sigmoid_gate * (1.0 + gate_pre * (1.0 - sigmoid_gate))
    ).astype(bf16)
    grad_up_low = (grad_hidden * silu_gate).astype(bf16)
    grad_both = jnp.concatenate([grad_gate_low, grad_up_low], 1)
    second_terms = dot_right_t(grad_both, gate_up).astype(bf16).reshape(planes, tokens, width)
    grad_second = plane_scatter([second_terms[i] for i in range(planes)])

    down_term = dot_left_t(hidden_low, direct_all).astype(bf16)
    gate_up_term = dot_left_t(second_all, grad_both).astype(bf16)
    down_grad = lax.psum_scatter(down_term, "fsdp", scatter_dimension=0, tiled=True).astype(f32)
    gate_up_grad = lax.psum_scatter(
        after(gate_up_term, down_term), "fsdp", scatter_dimension=0, tiled=True
    ).astype(f32)
    branch_terms = dot_plain(hidden_low, down_use).astype(bf16).reshape(planes, tokens, width)
    branch_terms = after(branch_terms, grad_second)
    branch_feed = plane_scatter([branch_terms[i] for i in range(planes)])
    output = (rows + keep * (branch_attention + branch_feed)).astype(bf16)

    second_gain_term = jnp.sum(grad_second * middle * inv_second, 0)
    weighted = grad_second * gain_second
    grad_middle = inv_second * weighted - middle * inv_second**3 * jnp.mean(
        weighted * middle, -1, keepdims=True
    )
    grad_branch_low = (direct + grad_middle).astype(bf16)
    grad_attended_low = dot_right_t(grad_branch_low, output_full).astype(bf16)
    grad_heads = lax.all_to_all(grad_attended_low, "fsdp", split_axis=1, concat_axis=0, tiled=True)
    dq, dk, dv = attend_back(queries, keys, values, starts, norm, mixed, grad_heads)
    turned = rotate(
        (jnp.concatenate([dq, dk], 1) * score_scale).reshape(length, heads + 1, HEAD_DIM),
        cosine,
        -sine_part,
    ).astype(bf16)
    grad_cols = jnp.concatenate([turned.reshape(length, own_width + HEAD_DIM), dv.astype(bf16)], 1)
    normed_terms = dot_right_t(grad_cols, project).astype(bf16)
    weighted_first = lax.psum_scatter(normed_terms, "fsdp", scatter_dimension=0, tiled=True).astype(f32)
    grad_rows = inv_first * weighted_first - rows * inv_first**3 * jnp.mean(
        weighted_first * rows, -1, keepdims=True
    )
    input_grad = cotangent + grad_middle + grad_rows

    project_term = dot_left_t(normed, grad_cols).astype(bf16).reshape(planes, ring * own_rows, cols)
    project_plane = plane_scatter(slots_of(project_term)).astype(bf16)
    back = lax.all_to_all(project_plane, "fsdp", split_axis=0, concat_axis=0, tiled=True)
    back = back.reshape(ring, own_rows, cols).astype(f32)

    def collect(low):
        parts = back[:, :, low : low + HEAD_DIM].reshape(KV_HEADS, sharers, own_rows, HEAD_DIM)
        return jnp.transpose(jnp.sum(parts, 1), (1, 0, 2)).reshape(own_rows, KV_HEADS * HEAD_DIM)

    query_plain = jnp.transpose(back[:, :, :own_width], (1, 0, 2)).reshape(own_rows, width)
    key_plain = collect(own_width)
    value_plain = collect(own_width + HEAD_DIM)
    first_gain_grad = (
        jnp.sum(query_plain * query_weight.astype(f32), 1)
        + jnp.sum(key_plain * key_weight.astype(f32), 1)
        + jnp.sum(value_plain * value_weight.astype(f32), 1)
    )
    attended_by_owner = jnp.transpose(
        attended_low.reshape(tokens, planes, ring, own_rows), (0, 2, 1, 3)
    ).reshape(tokens, width)
    output_term = dot_left_t(attended_by_owner, grad_branch_low).astype(bf16)
    output_plane = lax.psum_scatter(output_term, "fsdp", scatter_dimension=0, tiled=True)
    output_grad_weight = plane_scatter(
        slots_of(output_plane.reshape(planes, own_rows, width))
    )
    second_gain_all = lax.psum(lax.psum(second_gain_term, "fsdp"), "dp")
    mine = (lax.axis_index("dp") * ring + place) * own_rows
    second_gain_grad = lax.dynamic_slice_in_dim(second_gain_all, mine, own_rows)
    return (
        output[None],
        input_grad[None],
        first_gain_grad,
        query_plain * gain_mine,
        key_plain * gain_mine,
        value_plain * gain_mine,
        output_grad_weight,
        second_gain_grad,
        gate_up_grad[:, :ff_own],
        gate_up_grad[:, ff_own:],
        down_grad,
    )


PIECES = ((0, 0), (2, 0), (4, 0), (6, 0), (6, 1), (1, 0), (3, 0), (5, 0), (7, 0), (7, 1))
TO_CORE = (7, 3, 5, 1)
TO_CHIPS = (6, 2, 4, 0)
SLOT_HOPS = (
    (("down", 1), ("down", 1), ("up", 1), ("up", 1)),
    (("down", 2), ("up", 1), ("down", 1), ("up", 2)),
    (("down", 3), ("down", 2), ("up", 2), ("up", 3)),
)
VMEM = pl.BlockSpec(memory_space=pltpu.VMEM)
SMEM = pl.BlockSpec(memory_space=pltpu.SMEM)
log2_e = math.log2(math.e)


def start_of(place, piece, rows):
    bit, half = PIECES[piece]
    return pl.multiple_of((place ^ bit) * rows + half * (rows // 2), rows // 2)


def turn(block, cosine, sine, forward):
    rolled = pltpu.roll(block, HEAD_DIM // 2, 1)
    return block * cosine + rolled * sine if forward else block * cosine - rolled * sine


def masked_scores(keys, queries, starts, low):
    scores = dot_right_t(keys, queries) * (score_scale * log2_e)
    key_pos = lax.broadcasted_iota(jnp.int32, scores.shape, 0)
    query_pos = lax.broadcasted_iota(jnp.int32, scores.shape, 1) + low
    return scores, (key_pos <= query_pos) & (key_pos >= starts)


def front_kernel(tokens, at_ref, *refs):
    pieces, refs = refs[:10], refs[10:]
    hops, refs = refs[:7], refs[7:]
    cos_ref, sin_ref, starts_ref, refs = refs[0], refs[1], refs[2], refs[3:]
    q_ref, k_ref, v_ref, mixed_ref, norm_ref, project_ref, gain_ref, vt_ref = refs
    place, plane = at_ref[0], at_ref[1]
    length = 8 * tokens
    plane_rows = hops[0].shape[0] - 16

    def put(ref, owner):
        project_ref[pl.ds(pl.multiple_of(owner * plane_rows, plane_rows), plane_rows), :] = ref[:plane_rows, :]
        gain_ref[owner] = ref[plane_rows:, :]

    put(hops[0], plane)
    for hop in (1, 2, 3):

        @pl.when(plane >= hop)
        def _():
            put(hops[2 * hop - 1], plane - hop)

        @pl.when(plane + hop <= 3)
        def _():
            put(hops[2 * hop], plane + hop)

    q_width = q_ref.shape[1]
    for piece in range(10):
        here = pl.ds(start_of(place, piece, tokens), pieces[piece].shape[0])
        raw = dot_plain(pieces[piece][...], project_ref[...])
        cosine, sine = cos_ref[here, :], sin_ref[here, :]
        for low in range(0, q_width, HEAD_DIM):
            q_ref[here, low : low + HEAD_DIM] = turn(
                raw[:, low : low + HEAD_DIM], cosine, sine, True
            ).astype(bf16)
        k_ref[here, :] = turn(raw[:, q_width : q_width + HEAD_DIM], cosine, sine, True).astype(bf16)
        v_ref[here, :] = raw[:, q_width + HEAD_DIM :].astype(bf16)
    vt_ref[...] = jnp.transpose(v_ref[...].astype(f32)).astype(bf16)
    block = 256
    for head in range(q_width // HEAD_DIM):
        cols = slice(head * HEAD_DIM, (head + 1) * HEAD_DIM)
        for low in range(0, length, block):
            high = low + block
            scores, allowed = masked_scores(
                k_ref[:high, :], q_ref[low:high, cols], starts_ref[:, low:high], low
            )
            scores = jnp.where(allowed, scores, mask_fill)
            top = jnp.max(scores, 0, keepdims=True)
            expo = jnp.exp2(scores - top)
            total = jnp.sum(expo, 0, keepdims=True)
            probs = (expo * (1.0 / total)).astype(bf16)
            mixed_ref[low:high, cols] = jnp.transpose(dot_plain(vt_ref[:, :high], probs)).astype(bf16)
            norm_ref[head, :, low:high] = top + jnp.log2(total)


def front(at, pieces, hops, cosine, sine, starts):
    tokens = pieces[0].shape[0]
    length = 8 * tokens
    plane_rows, cols = hops[0].shape[0] - 16, hops[0].shape[1]
    q_width = cols - 2 * HEAD_DIM
    width = 4 * plane_rows
    shapes = [
        jax.ShapeDtypeStruct((length, q_width), bf16),
        jax.ShapeDtypeStruct((length, HEAD_DIM), bf16),
        jax.ShapeDtypeStruct((length, HEAD_DIM), bf16),
        jax.ShapeDtypeStruct((length, q_width), bf16),
        jax.ShapeDtypeStruct((q_width // HEAD_DIM, 1, length), f32),
        jax.ShapeDtypeStruct((width, cols), bf16),
        jax.ShapeDtypeStruct((4, 16, cols), bf16),
    ]
    return pl.pallas_call(
        functools.partial(front_kernel, tokens),
        in_specs=[SMEM] + [VMEM] * 20,
        out_specs=[VMEM] * 7,
        out_shape=shapes,
        scratch_shapes=[pltpu.VMEM((HEAD_DIM, length), bf16)],
        compiler_params=pltpu.CompilerParams(vmem_limit_bytes=52 << 20),
        cost_estimate=pl.CostEstimate(
            flops=2 * length * width * cols + 4 * length * length * q_width,
            bytes_accessed=2 * length * width + 4 * width * cols,
            transcendentals=length * length,
        ),
        name="front",
    )(at, *pieces, *hops, cosine, sine, starts)


def back_kernel(tokens, at_ref, q_ref, k_ref, v_ref, mixed_ref, norm_ref, grad_ref, project_ref,
                cos_ref, sin_ref, starts_ref, core_ref, chips_ref, cols_ref, kt_ref, dk_ref, dv_ref):
    place = at_ref[0]
    length, q_width = q_ref.shape
    block = 256
    kt_ref[...] = jnp.transpose(k_ref[...].astype(f32)).astype(bf16)
    dk_ref[...] = jnp.zeros_like(dk_ref)
    dv_ref[...] = jnp.zeros_like(dv_ref)
    for head in range(q_width // HEAD_DIM):
        cols = slice(head * HEAD_DIM, (head + 1) * HEAD_DIM)
        for low in range(0, length, block):
            high = low + block
            queries, grads = q_ref[low:high, cols], grad_ref[low:high, cols]
            scores, allowed = masked_scores(k_ref[:high, :], queries, starts_ref[:, low:high], low)
            probs = jnp.where(allowed, jnp.exp2(scores - norm_ref[head, :, low:high]), 0.0)
            grad_prob = dot_right_t(v_ref[:high, :], grads)
            weighed = jnp.transpose(grads.astype(f32) * mixed_ref[low:high, cols].astype(f32))
            grad_score = (probs * (grad_prob - jnp.sum(weighed, 0, keepdims=True))).astype(bf16)
            dv_ref[:high, :] += dot_plain(probs.astype(bf16), grads)
            dk_ref[:high, :] += dot_plain(grad_score, queries)
            dq = jnp.transpose(dot_plain(kt_ref[:, :high], grad_score)) * score_scale
            cols_ref[low:high, cols] = turn(
                dq, cos_ref[low:high, :], sin_ref[low:high, :], False
            ).astype(bf16)
    cols_ref[:, q_width : q_width + HEAD_DIM] = turn(
        dk_ref[...] * score_scale, cos_ref[...], sin_ref[...], False
    ).astype(bf16)
    cols_ref[:, q_width + HEAD_DIM :] = dv_ref[...].astype(bf16)
    for out_ref, bits in ((core_ref, TO_CORE), (chips_ref, TO_CHIPS)):
        for step, bit in enumerate(bits):
            here = pl.ds(pl.multiple_of((place ^ bit) * tokens, tokens), tokens)
            out_ref[step] = dot_right_t(cols_ref[here, :], project_ref[...]).astype(bf16)


def back(at, queries, keys, values, mixed, norm, grads, project, cosine, sine, starts):
    length, q_width = queries.shape
    width, cols = project.shape
    tokens = length // 8
    return pl.pallas_call(
        functools.partial(back_kernel, tokens),
        in_specs=[SMEM] + [VMEM] * 10,
        out_specs=[VMEM] * 3,
        out_shape=[
            jax.ShapeDtypeStruct((4, tokens, width), bf16),
            jax.ShapeDtypeStruct((4, tokens, width), bf16),
            jax.ShapeDtypeStruct((length, cols), bf16),
        ],
        scratch_shapes=[
            pltpu.VMEM((HEAD_DIM, length), bf16),
            pltpu.VMEM((length, HEAD_DIM), f32),
            pltpu.VMEM((length, HEAD_DIM), f32),
        ],
        compiler_params=pltpu.CompilerParams(vmem_limit_bytes=52 << 20),
        cost_estimate=pl.CostEstimate(
            flops=2 * length * width * cols + 7 * length * length * q_width,
            bytes_accessed=2 * length * width + 2 * width * cols,
            transcendentals=length * length,
        ),
        name="back",
    )(at, queries, keys, values, mixed, norm, grads, project, cosine, sine, starts)


def project_grad_kernel(tokens, at_ref, *refs):
    pieces, (cols_ref, out_ref) = refs[:10], refs[10:]
    place = at_ref[0]
    total = None
    for piece in range(10):
        here = pl.ds(start_of(place, piece, tokens), pieces[piece].shape[0])
        term = dot_left_t(cols_ref[here, :], pieces[piece][...])
        total = term if total is None else total + term
    turned = jnp.transpose(total).astype(bf16)
    out_ref[...] = turned.reshape(out_ref.shape)


def project_grad(at, pieces, grad_cols):
    tokens, width = pieces[0].shape
    cols = grad_cols.shape[1]
    return pl.pallas_call(
        functools.partial(project_grad_kernel, tokens),
        in_specs=[SMEM] + [VMEM] * 11,
        out_specs=VMEM,
        out_shape=jax.ShapeDtypeStruct((4, width // 4, cols), bf16),
        compiler_params=pltpu.CompilerParams(vmem_limit_bytes=52 << 20),
        cost_estimate=pl.CostEstimate(
            flops=16 * tokens * width * cols, bytes_accessed=16 * tokens * width, transcendentals=0
        ),
        name="project_grad",
    )(at, *pieces, grad_cols)


def output_grad_kernel(tokens, at_ref, *refs):
    pieces, (mixed_ref, out_ref, gain_ref) = refs[:10], refs[10:]
    place = at_ref[0]
    total = None
    gain = None
    for piece in range(10):
        bit, half = PIECES[piece]
        rows = tokens // 2 if bit >= 6 else tokens
        here = pl.ds(start_of(place, piece, tokens), rows)
        term = dot_left_t(mixed_ref[here, :], pieces[piece][:rows, :])
        total = term if total is None else total + term
        if pieces[piece].shape[0] > rows:
            extra = jnp.sum(pieces[piece][rows:, :].astype(f32), 0, keepdims=True)
            gain = extra if gain is None else gain + extra
    out_ref[...] = total.astype(bf16).reshape(out_ref.shape)
    gain_ref[...] = gain


def output_grad_term(at, pieces, mixed):
    length, own = mixed.shape
    tokens, width = length // 8, pieces[0].shape[1]
    return pl.pallas_call(
        functools.partial(output_grad_kernel, tokens),
        in_specs=[SMEM] + [VMEM] * 11,
        out_specs=[VMEM] * 2,
        out_shape=[
            jax.ShapeDtypeStruct((4, own // 4, width), bf16),
            jax.ShapeDtypeStruct((1, width), f32),
        ],
        compiler_params=pltpu.CompilerParams(vmem_limit_bytes=52 << 20),
        cost_estimate=pl.CostEstimate(
            flops=2 * length * own * width, bytes_accessed=2 * length * width, transcendentals=0
        ),
        name="output_grad_term",
    )(at, *pieces, mixed)


def feed_kernel(chosen, count, at_ref, *refs):
    n_ins = len(chosen[1])
    n_opts, d_opts, refs = refs[:n_ins], refs[n_ins : 2 * n_ins], refs[2 * n_ins :]
    both_ref, down_ref, refs = refs[0], refs[1], refs[2 + count :]
    second_ref, direct_ref, hidden_ref, grads_ref, term_ref, total_ref = refs
    step = pl.program_id(0)
    plane = at_ref[1]

    @pl.when(step == 0)
    def _():
        total_ref[...] = jnp.zeros_like(total_ref)
        if n_ins == 1:
            second_ref[...] = n_opts[0][...]
            direct_ref[...] = d_opts[0][...]
        else:
            for p in range(4):

                @pl.when(plane == p)
                def _():
                    second_ref[...] = n_opts[chosen[0][p]][...]
                    direct_ref[...] = d_opts[chosen[0][p]][...]

    second, direct = second_ref[...], direct_ref[...]
    both = both_ref[...]
    raw = dot_plain(second, both)
    half = raw.shape[1] // 2
    gate, upward = raw[:, :half], raw[:, half:]
    sig = 1.0 / (1.0 + jnp.exp(-gate))
    silu = gate * sig
    hidden_ref[...] = (silu * upward).astype(bf16)
    grad_hidden = dot_right_t(direct, down_ref[...])
    grads = jnp.concatenate(
        [
            (grad_hidden * upward * sig * (1.0 + gate * (1.0 - sig))).astype(bf16),
            (grad_hidden * silu).astype(bf16),
        ],
        1,
    )
    grads_ref[...] = grads
    total_ref[...] += dot_right_t(grads, both)

    @pl.when(step == pl.num_programs(0) - 1)
    def _():
        term_ref[...] = total_ref[...].astype(bf16)


def feed(at, slot, second_hops, direct_hops, both, down, so_far):
    if slot == 0:
        names, chosen = [("own", 0)], [0] * 4
    else:
        names = list(dict.fromkeys(SLOT_HOPS[slot - 1]))
        chosen = [names.index(name) for name in SLOT_HOPS[slot - 1]]
    tokens, width = second_hops["own", 0].shape
    ff = down.shape[0]
    unit = 128
    so_far = so_far or []
    whole = pl.BlockSpec((tokens, width), lambda i: (0, 0))
    shapes = [
        jax.ShapeDtypeStruct((4 * tokens, width), bf16),
        jax.ShapeDtypeStruct((4 * tokens, width), bf16),
        jax.ShapeDtypeStruct((4 * tokens, ff), bf16),
        jax.ShapeDtypeStruct((4 * tokens, 2 * ff), bf16),
        jax.ShapeDtypeStruct((tokens, width), bf16),
    ]
    first = 1 + 2 * len(names) + 2
    outs = pl.pallas_call(
        functools.partial(feed_kernel, (chosen, names), len(so_far)),
        grid=(ff // unit,),
        in_specs=[SMEM]
        + [whole] * (2 * len(names))
        + [
            pl.BlockSpec((width, 2 * unit), lambda i: (0, i)),
            pl.BlockSpec((unit, width), lambda i: (i, 0)),
        ]
        + [pl.BlockSpec(memory_space=pl.ANY)] * len(so_far),
        out_specs=[
            pl.BlockSpec((tokens, width), lambda i: (slot, 0)),
            pl.BlockSpec((tokens, width), lambda i: (slot, 0)),
            pl.BlockSpec((tokens, unit), lambda i: (slot, i)),
            pl.BlockSpec((tokens, 2 * unit), lambda i: (slot, i)),
            whole,
        ],
        out_shape=shapes,
        scratch_shapes=[pltpu.VMEM((tokens, width), f32)],
        input_output_aliases={first + i: i for i in range(len(so_far))},
        compiler_params=pltpu.CompilerParams(vmem_limit_bytes=52 << 20),
        cost_estimate=pl.CostEstimate(
            flops=10 * tokens * width * ff,
            bytes_accessed=6 * width * ff,
            transcendentals=tokens * ff,
        ),
        name="feed",
    )(
        at,
        *[second_hops[name] for name in names],
        *[direct_hops[name] for name in names],
        both,
        down,
        *so_far,
    )
    return outs[:4], outs[4]


def hop_on(hops, step, *earlier):
    before = (("own", 0), ("own", 0)) if step == 1 else (("up", step - 1), ("down", step - 1))
    for name, moves in ((0, UP), (1, DOWN)):
        block = hops[before[name]]
        if earlier:
            block = after(block, *earlier)
        hops[("up", "down")[name], step] = lax.ppermute(block, "dp", moves[step - 1 :])


def fast_device(
    layer_input,
    output_grad,
    layer_keep,
    group_ids,
    exit_scale,
    doc_lengths,
    attention_gain,
    query_weight,
    key_weight,
    value_weight,
    output_weight,
    feedforward_gain,
    gate_weight,
    up_weight,
    down_weight,
):
    tokens, width = layer_input.shape[1:]
    place, plane = lax.axis_index("fsdp"), lax.axis_index("dp")
    at = jnp.stack([place, plane]).astype(jnp.int32)
    length = tokens * 8
    own_rows = query_weight.shape[0]
    q_width = HEADS // 8 * HEAD_DIM
    cols = q_width + 2 * HEAD_DIM
    ff_own = gate_weight.shape[1]
    half = tokens // 2
    rows = layer_input[0].astype(f32)
    keep = layer_keep[0].astype(f32)

    output_full = lax.all_gather(output_weight, ("dp", "fsdp"), axis=0, tiled=True)
    both_mine = jnp.stack(
        [gate_weight.reshape(-1, ff_own // 128, 128), up_weight.reshape(-1, ff_own // 128, 128)], 2
    ).reshape(-1, 2 * ff_own)
    both = lax.all_gather(both_mine, "fsdp", axis=0, tiled=True)

    inv_first = rms_scale(rows)
    normed = (rows * inv_first).astype(bf16)
    along_x, along_y, on_core = flip(normed, 2), flip(normed, 4), flip(normed, 1)
    gain_mine = attention_gain.astype(f32)[:, None]

    def spread(weight):
        scaled = (weight.astype(f32) * gain_mine).astype(bf16).reshape(own_rows, KV_HEADS, 1, HEAD_DIM)
        return jnp.broadcast_to(scaled, (own_rows, KV_HEADS, 2, HEAD_DIM)).reshape(own_rows, 8, HEAD_DIM)

    query_scaled = (query_weight.astype(f32) * gain_mine).astype(bf16).reshape(own_rows, 8, q_width)
    sent = jnp.concatenate([query_scaled, spread(key_weight), spread(value_weight)], -1)
    gain_row = jnp.pad(feedforward_gain[None, None, :], ((0, 15), (0, 7), (0, cols - own_rows)))
    gain_row = jnp.broadcast_to(gain_row[:, :1], (16, 8, cols))
    sent = jnp.transpose(jnp.concatenate([sent, gain_row], 0), (1, 0, 2)).reshape(-1, cols)
    got = lax.all_to_all(sent, "fsdp", split_axis=0, concat_axis=0, tiled=True)
    got = got.reshape(8, own_rows + 16, cols)
    gains = jnp.pad(got[:, own_rows, :own_rows].reshape(1, 8 * own_rows), ((0, 15), (0, 0)))
    columns = {("own", 0): jnp.concatenate([got[:, :own_rows].reshape(-1, cols), gains], 0)}
    hop_on(columns, 1)
    low = flip(after(along_x[:half], columns["own", 0]), 4)
    high = flip(after(along_y[half:], columns["own", 0]), 2)
    down_use = lax.all_gather(
        after(down_weight, columns["own", 0]), "fsdp", axis=0, tiled=True
    )
    core_x, core_y = flip(along_x, 1), flip(along_y, 1)
    hop_on(columns, 2)
    core_low, core_high = flip(low, 1), flip(high, 1)
    hop_on(columns, 3)
    pieces = [normed, along_x, along_y, low, high, on_core, core_x, core_y, core_low, core_high]

    picked = jnp.sum(
        jnp.where(jnp.arange(exit_scale.shape[0], dtype=jnp.int32) == group_ids[0], exit_scale, 0.0)
    )
    cotangent = output_grad[0].astype(f32) * picked
    direct = keep * cotangent
    directs = {("own", 0): direct.astype(bf16)}
    hop_on(directs, 1, columns["up", 2], columns["down", 2])

    half_dim = HEAD_DIM // 2
    cosine, sine = rotary_tables(length)
    cosine, sine = cosine[:, 0], sine[:, 0]
    cosine = jnp.concatenate([cosine, cosine], 1)
    sine = jnp.concatenate([-sine, sine], 1)
    order = jnp.arange(doc_lengths.shape[1])
    ends = jnp.sum(jnp.where(order[None, :] <= order[:, None], doc_lengths[0][None, :], 0), 1)
    positions = jnp.arange(length, dtype=jnp.int32)
    starts = jnp.max(jnp.where(positions[None, :] >= ends[:, None], ends[:, None], 0), 0)[None, :]

    all_hops = [columns["own", 0]]
    for step in (1, 2, 3):
        all_hops += [columns["up", step], columns["down", step]]
    queries, keys, values, mixed, norm, project, gains = front(
        at, pieces, all_hops, cosine, sine, starts
    )
    gain_second = gains[:, 0, :].reshape(width).astype(f32)

    hop_on(directs, 2, mixed)
    attended_low = lax.all_to_all(mixed, "fsdp", split_axis=0, concat_axis=1, tiled=True)
    branch_attention = dot_plain(attended_low, output_full)
    middle = rows + branch_attention
    inv_second = rms_scale(middle)
    seconds = {("own", 0): (middle * inv_second * gain_second).astype(bf16)}

    hop_on(seconds, 1)
    hop_on(directs, 3, seconds["own", 0])
    stacked, term_own = feed(at, 0, seconds, directs, both, down_use, None)
    hop_on(seconds, 2)
    stacked, term_1 = feed(at, 1, seconds, directs, both, down_use, stacked)
    hop_on(seconds, 3)
    stacked, term_2 = feed(at, 2, seconds, directs, both, down_use, stacked)
    stacked, term_3 = feed(at, 3, seconds, directs, both, down_use, stacked)
    second_all, direct_all, hidden_all, grads_all = stacked
    grad_second = plane_scatter([term_own, term_1, term_2, term_3])

    down_term = dot_left_t(hidden_all, direct_all).astype(bf16)
    both_term = dot_left_t(second_all, grads_all).astype(bf16)
    down_grad = lax.psum_scatter(down_term, "fsdp", scatter_dimension=0, tiled=True).astype(f32)
    both_grad = lax.psum_scatter(both_term, "fsdp", scatter_dimension=0, tiled=True)
    branch_terms = dot_plain(hidden_all, down_use).astype(bf16).reshape(4, tokens, width)

    weighted = grad_second * gain_second
    grad_middle = inv_second * weighted - middle * inv_second**3 * jnp.mean(
        weighted * middle, -1, keepdims=True
    )
    grad_branch = (direct + grad_middle).astype(bf16)
    grad_attended = dot_right_t(grad_branch, output_full).astype(bf16)
    grad_heads = lax.all_to_all(grad_attended, "fsdp", split_axis=1, concat_axis=0, tiled=True)
    gain_term = jnp.sum(grad_second * middle * inv_second, 0, keepdims=True)
    gain_high = gain_term.astype(bf16)
    gain_low = (gain_term - gain_high.astype(f32)).astype(bf16)
    branch_block = jnp.concatenate(
        [grad_branch, gain_high, gain_low, jnp.zeros((14, width), bf16)], 0
    )
    branch_x, branch_y, branch_core = flip(branch_block, 2), flip(branch_block, 4), flip(branch_block, 1)

    core_terms, chip_terms, grad_cols = back(
        at, queries, keys, values, mixed, norm, grad_heads, project, cosine, sine, starts
    )
    other = flip(core_terms, 1)
    branch_low = flip(after(branch_x[:half], grad_cols), 4)
    branch_high = flip(after(branch_y[half:], grad_cols), 2)
    far = flip(add_low(chip_terms[0], other[0]), 6)
    near_x = flip(add_low(chip_terms[1], other[1]), 2)
    near_y = flip(add_low(chip_terms[2], other[2]), 4)
    project_term = project_grad(at, pieces, grad_cols)
    project_plane = plane_scatter(slots_of(project_term)).astype(bf16)
    branch_pieces = [branch_block, branch_x, branch_y, branch_low, branch_high, branch_core]
    branch_pieces += [flip(piece, 1) for piece in (branch_x, branch_y, branch_low, branch_high)]
    output_term, gain_sum = output_grad_term(at, branch_pieces, mixed)
    gain_own = lax.dynamic_slice_in_dim(gain_sum[0], place * 4 * own_rows, 4 * own_rows)
    gain_own = jnp.pad(gain_own.reshape(4, 1, own_rows), ((0, 0), (0, 15), (0, width - own_rows)))
    output_term = jnp.concatenate([output_term, gain_own.astype(bf16)], 1)
    output_sum = output_rows(output_term.reshape(-1, width))
    weighted_first = (
        chip_terms[3].astype(f32)
        + other[3].astype(f32)
        + far.astype(f32)
        + near_x.astype(f32)
        + near_y.astype(f32)
    )
    grad_rows = inv_first * weighted_first - rows * inv_first**3 * jnp.mean(
        weighted_first * rows, -1, keepdims=True
    )
    input_grad = cotangent + grad_middle + grad_rows

    branch_terms = after(branch_terms, grad_branch)
    branch_feed = plane_scatter([branch_terms[i] for i in range(4)])
    output = (rows + keep * (branch_attention + branch_feed)).astype(bf16)

    back_cols = lax.all_to_all(project_plane, "fsdp", split_axis=0, concat_axis=0, tiled=True)
    back_cols = back_cols.reshape(8, own_rows, cols).astype(f32)

    def collect(at_col):
        parts = back_cols[:, :, at_col : at_col + HEAD_DIM].reshape(KV_HEADS, 2, own_rows, HEAD_DIM)
        return jnp.transpose(jnp.sum(parts, 1), (1, 0, 2)).reshape(own_rows, KV_HEADS * HEAD_DIM)

    query_plain = jnp.transpose(back_cols[:, :, :q_width], (1, 0, 2)).reshape(own_rows, width)
    key_plain = collect(q_width)
    value_plain = collect(q_width + HEAD_DIM)
    first_gain_grad = (
        jnp.sum(query_plain * query_weight.astype(f32), 1)
        + jnp.sum(key_plain * key_weight.astype(f32), 1)
        + jnp.sum(value_plain * value_weight.astype(f32), 1)
    )
    both_parts = both_grad.reshape(-1, ff_own // 128, 2, 128)
    return (
        output[None],
        input_grad[None],
        first_gain_grad,
        query_plain * gain_mine,
        key_plain * gain_mine,
        value_plain * gain_mine,
        output_sum[:own_rows],
        output_sum[own_rows, :own_rows],
        both_parts[:, :, 0].reshape(-1, ff_own).astype(f32),
        both_parts[:, :, 1].reshape(-1, ff_own).astype(f32),
        down_grad,
    )


def solution(mesh):
    both = ("dp", "fsdp")
    fast = (mesh.shape["dp"], mesh.shape["fsdp"]) == (4, 8)
    return jax.shard_map(
        fast_device if fast else per_device,
        mesh=mesh,
        in_specs=(
            P("dp", "fsdp", None),
            P("dp", "fsdp", None),
            P("dp"),
            P("dp"),
            P(),
            P("dp", None),
            P(both),
            P(both, None),
            P(both, None),
            P(both, None),
            P(both, None),
            P(both),
            P("fsdp", "dp"),
            P("fsdp", "dp"),
            P(both, None),
        ),
        out_specs=(
            P("dp", "fsdp", None),
            P("dp", "fsdp", None),
            P(both),
            P(both, None),
            P(both, None),
            P(both, None),
            P(both, None),
            P(both),
            P("fsdp", "dp"),
            P("fsdp", "dp"),
            P(both, None),
        ),
        check_vma=False,
    )
```

```python
import functools
import math

import jax
import jax.numpy as jnp
from jax import lax
from jax.experimental import pallas as pl
from jax.experimental.pallas import tpu as pltpu
from jax.sharding import PartitionSpec as P

HEADS = 16
KV_HEADS = 4
HEAD_DIM = 128

norm_eps = 1e-05
rope_base = 10000.0
mask_fill = -1e30
score_scale = 1.0 / math.sqrt(HEAD_DIM)
f32 = jnp.float32
bf16 = jnp.bfloat16


def dot_plain(left, right):
    return jnp.dot(left, right, preferred_element_type=f32)


def dot_right_t(left, right):
    return lax.dot_general(left, right, (((1,), (1,)), ((), ())), preferred_element_type=f32)


def dot_left_t(left, right):
    return lax.dot_general(left, right, (((0,), (0,)), ((), ())), preferred_element_type=f32)


def rotary_tables(length):
    half_dim = HEAD_DIM // 2
    frequency = rope_base ** (-(2.0 * jnp.arange(half_dim, dtype=f32)) / HEAD_DIM)
    angles = jnp.arange(length, dtype=jnp.int32).astype(f32)[:, None] * frequency[None, :]
    return (jnp.cos(angles)[:, None, :], jnp.sin(angles)[:, None, :])


def rotate(vectors, cosine, sine_part):
    half_dim = vectors.shape[-1] // 2
    lower_half = vectors[..., :half_dim]
    upper_half = vectors[..., half_dim:]
    return jnp.concatenate(
        [
            lower_half * cosine - upper_half * sine_part,
            upper_half * cosine + lower_half * sine_part,
        ],
        -1,
    )


def rms_scale(rows):
    return lax.rsqrt(jnp.mean(rows * rows, -1, keepdims=True) + norm_eps)


def after(value, *earlier):
    return lax.optimization_barrier((value, *earlier))[0]


def plane_gather(block):
    whole = lax.all_gather(block, "dp", axis=0)
    return [whole[i] for i in range(whole.shape[0])]


def add_low(left, right):
    return (left.astype(f32) + right.astype(f32)).astype(left.dtype)


def plane_scatter(whole):
    return lax.psum_scatter(whole, "dp", scatter_dimension=0, tiled=False).astype(f32)


FLIP = {bit: [(i, i ^ bit) for i in range(8)] for bit in (1, 2, 4, 6)}


def flip(block, bit):
    return lax.ppermute(block, "fsdp", FLIP[bit])


def shift(block, step):
    return lax.ppermute(block, "dp", [(i, (i + step) % 4) for i in range(4)])


def gather_planes(block):
    copies = jnp.broadcast_to(block[None], (4, *block.shape))
    return lax.all_to_all(copies, "dp", split_axis=0, concat_axis=0)


def swap_planes(whole):
    return lax.all_to_all(whole, "dp", split_axis=0, concat_axis=0)


def output_rows(mine, others, *earlier):
    group, plane = lax.axis_index("fsdp") // 2, lax.axis_index("dp")
    whole = add_low(mine, flip(others, 1))

    def to(bit):
        return lax.dynamic_index_in_dim(whole, group ^ bit, 0, keepdims=False)

    parts = [to(0)] + [flip(to(bit), 2 * bit) for bit in (1, 2, 3)]
    by_group = jnp.zeros_like(whole)
    for bit, part in enumerate(parts):
        by_group = lax.dynamic_update_index_in_dim(by_group, part, group ^ bit, 0)
    by_group = after(by_group, *earlier)
    ahead = [lax.dynamic_index_in_dim(by_group, (plane + k) % 4, 0, keepdims=False) for k in range(4)]
    total = ahead[0].astype(f32)
    for k in (1, 2, 3):
        total = total + shift(ahead[k], k).astype(f32)
    return total


def block_rows_of(length):
    return math.gcd(length, 256)


def transposed_scores(keys, queries, starts, low, high, width):
    scores = dot_right_t(keys, queries) * score_scale
    key_pos = lax.broadcasted_iota(jnp.int32, (width, high - low), 0)
    query_pos = lax.broadcasted_iota(jnp.int32, (width, high - low), 1) + low
    allowed = (key_pos <= query_pos) & (key_pos >= starts)
    return scores, allowed


def attend_kernel(rows_of, q_ref, k_ref, vt_ref, starts_ref, out_ref, norm_ref):
    length = q_ref.shape[0]
    for low in range(0, length, rows_of):
        high = low + rows_of
        starts = starts_ref[:, low:high]
        scores, allowed = transposed_scores(
            k_ref[:high, :], q_ref[low:high, :], starts, low, high, high
        )
        scores = jnp.where(allowed, scores, mask_fill)
        top = jnp.max(scores, 0, keepdims=True)
        expo = jnp.exp(scores - top)
        total = jnp.sum(expo, 0, keepdims=True)
        probs = (expo * (1.0 / total)).astype(bf16)
        mixed = dot_plain(vt_ref[:, :high], probs)
        out_ref[low:high, :] = jnp.transpose(mixed).astype(out_ref.dtype)
        norm_ref[0, :, low:high] = top + jnp.log(total)


def attend(queries, keys, values, starts):
    length, width = queries.shape
    heads = width // HEAD_DIM
    return pl.pallas_call(
        functools.partial(attend_kernel, block_rows_of(length)),
        grid=(heads,),
        in_specs=[
            pl.BlockSpec((length, HEAD_DIM), lambda h: (0, h)),
            pl.BlockSpec((length, HEAD_DIM), lambda h: (0, 0)),
            pl.BlockSpec((HEAD_DIM, length), lambda h: (0, 0)),
            pl.BlockSpec((1, length), lambda h: (0, 0)),
        ],
        out_specs=[
            pl.BlockSpec((length, HEAD_DIM), lambda h: (0, h)),
            pl.BlockSpec((1, 1, length), lambda h: (h, 0, 0)),
        ],
        out_shape=[
            jax.ShapeDtypeStruct((length, width), bf16),
            jax.ShapeDtypeStruct((heads, 1, length), f32),
        ],
        compiler_params=pltpu.CompilerParams(vmem_limit_bytes=48 << 20),
        cost_estimate=pl.CostEstimate(
            flops=3 * heads * length * length * HEAD_DIM,
            bytes_accessed=8 * length * width,
            transcendentals=heads * length * length,
        ),
        name="attend",
    )(queries, keys, jnp.transpose(values), starts)


def attend_back_kernel(
    rows_of, q_ref, k_ref, kt_ref, v_ref, starts_ref, norm_ref, out_ref, grad_ref, dq_ref, dk_ref, dv_ref
):
    length = q_ref.shape[0]

    @pl.when(pl.program_id(0) == 0)
    def _():
        dk_ref[...] = jnp.zeros_like(dk_ref)
        dv_ref[...] = jnp.zeros_like(dv_ref)

    for low in range(0, length, rows_of):
        high = low + rows_of
        starts = starts_ref[:, low:high]
        queries = q_ref[low:high, :]
        grads = grad_ref[low:high, :]
        scores, allowed = transposed_scores(k_ref[:high, :], queries, starts, low, high, high)
        probs = jnp.where(allowed, jnp.exp(scores - norm_ref[0, :, low:high]), 0.0)
        grad_prob = dot_right_t(v_ref[:high, :], grads)
        weighed = jnp.transpose(grads.astype(f32) * out_ref[low:high, :].astype(f32))
        delta = jnp.sum(weighed, 0, keepdims=True)
        grad_score = (probs * (grad_prob - delta)).astype(bf16)
        dv_ref[:high, :] += dot_plain(probs.astype(bf16), grads)
        dk_ref[:high, :] += dot_plain(grad_score, queries)
        dq_ref[low:high, :] = jnp.transpose(dot_plain(kt_ref[:, :high], grad_score))


def attend_back(queries, keys, values, starts, norm, out, grads):
    length, width = queries.shape
    heads = width // HEAD_DIM
    by_head = pl.BlockSpec((length, HEAD_DIM), lambda h: (0, h))
    shared = pl.BlockSpec((length, HEAD_DIM), lambda h: (0, 0))
    return pl.pallas_call(
        functools.partial(attend_back_kernel, block_rows_of(length)),
        grid=(heads,),
        in_specs=[
            by_head,
            shared,
            pl.BlockSpec((HEAD_DIM, length), lambda h: (0, 0)),
            shared,
            pl.BlockSpec((1, length), lambda h: (0, 0)),
            pl.BlockSpec((1, 1, length), lambda h: (h, 0, 0)),
            by_head,
            by_head,
        ],
        out_specs=[by_head, shared, shared],
        out_shape=[
            jax.ShapeDtypeStruct((length, width), f32),
            jax.ShapeDtypeStruct((length, HEAD_DIM), f32),
            jax.ShapeDtypeStruct((length, HEAD_DIM), f32),
        ],
        compiler_params=pltpu.CompilerParams(vmem_limit_bytes=56 << 20),
        cost_estimate=pl.CostEstimate(
            flops=7 * heads * length * length * HEAD_DIM,
            bytes_accessed=16 * length * width,
            transcendentals=heads * length * length,
        ),
        name="attend_back",
    )(queries, keys, jnp.transpose(keys), values, starts, norm, out, grads)


def per_device(
    layer_input,
    output_grad,
    layer_keep,
    group_ids,
    exit_scale,
    doc_lengths,
    attention_gain,
    query_weight,
    key_weight,
    value_weight,
    output_weight,
    feedforward_gain,
    gate_weight,
    up_weight,
    down_weight,
):
    tokens, width = layer_input.shape[1:]
    ring = lax.axis_size("fsdp")
    planes = lax.axis_size("dp")
    place = lax.axis_index("fsdp")
    length = tokens * ring
    own_rows = query_weight.shape[0]
    heads = HEADS // ring
    own_width = heads * HEAD_DIM
    ff_own = gate_weight.shape[1]
    rows = layer_input[0].astype(f32)
    keep = layer_keep[0].astype(f32)

    inv_first = rms_scale(rows)
    normed = lax.all_gather((rows * inv_first).astype(bf16), "fsdp", axis=0, tiled=True)

    gain_mine = attention_gain.astype(f32)[:, None]
    sharers = ring // KV_HEADS
    cols = own_width + 2 * HEAD_DIM

    def spread(weight):
        heads_of = (weight.astype(f32) * gain_mine).astype(bf16).reshape(own_rows, KV_HEADS, 1, HEAD_DIM)
        return jnp.broadcast_to(heads_of, (own_rows, KV_HEADS, sharers, HEAD_DIM)).reshape(
            own_rows, ring, HEAD_DIM
        )

    query_scaled = (query_weight.astype(f32) * gain_mine).astype(bf16).reshape(own_rows, ring, own_width)
    sent = jnp.concatenate([query_scaled, spread(key_weight), spread(value_weight)], -1)
    sent = jnp.transpose(sent, (1, 0, 2)).reshape(ring * own_rows, cols)
    plane_cols = lax.all_to_all(sent, "fsdp", split_axis=0, concat_axis=0, tiled=True)
    project = jnp.concatenate(plane_gather(plane_cols), 0)

    picked = jnp.sum(
        jnp.where(jnp.arange(exit_scale.shape[0], dtype=jnp.int32) == group_ids[0], exit_scale, 0.0)
    )
    cotangent = output_grad[0].astype(f32) * picked
    direct = keep * cotangent
    direct_all = jnp.concatenate(plane_gather(direct.astype(bf16)), 0)

    gain_second = lax.all_gather(
        lax.all_gather(feedforward_gain, "fsdp", axis=0, tiled=False), "dp", axis=0, tiled=False
    ).reshape(width).astype(f32)

    output_full = lax.all_gather(output_weight, ("dp", "fsdp"), axis=0, tiled=True)
    gate_up = jnp.concatenate([gate_weight, up_weight], 1)
    gate_up = lax.all_gather(gate_up, "fsdp", axis=0, tiled=True)
    down_use = lax.all_gather(down_weight, "fsdp", axis=0, tiled=True)

    cosine, sine_part = rotary_tables(length)
    ends = jnp.sum(
        jnp.where(
            jnp.arange(doc_lengths.shape[1])[None, :] <= jnp.arange(doc_lengths.shape[1])[:, None],
            doc_lengths[0][None, :],
            0,
        ),
        1,
    )
    positions = jnp.arange(length, dtype=jnp.int32)
    starts = jnp.max(jnp.where(positions[None, :] >= ends[:, None], ends[:, None], 0), 0)[None, :]
    raw = dot_plain(normed, project)
    rotated = rotate(
        raw[:, : own_width + HEAD_DIM].reshape(length, heads + 1, HEAD_DIM), cosine, sine_part
    ).astype(bf16)
    queries = rotated[:, :heads].reshape(length, own_width)
    keys = rotated[:, heads]
    values = raw[:, own_width + HEAD_DIM :].astype(bf16)
    mixed, norm = attend(queries, keys, values, starts)
    attended_low = lax.all_to_all(mixed, "fsdp", split_axis=0, concat_axis=1, tiled=True)
    branch_attention = dot_plain(attended_low, output_full)
    middle = rows + branch_attention
    inv_second = rms_scale(middle)
    second_mine = (middle * inv_second * gain_second).astype(bf16)

    second_all = jnp.concatenate(plane_gather(second_mine), 0)
    gate_use, up_use = gate_up[:, :ff_own], gate_up[:, ff_own:]
    gate_pre = dot_plain(second_all, gate_use)
    upward = dot_plain(second_all, up_use)
    sigmoid_gate = 1.0 / (1.0 + jnp.exp(-gate_pre))
    silu_gate = gate_pre * sigmoid_gate
    hidden_low = (silu_gate * upward).astype(bf16)
    grad_hidden = dot_right_t(direct_all, down_use)
    grad_gate_low = (
        grad_hidden * upward * sigmoid_gate * (1.0 + gate_pre * (1.0 - sigmoid_gate))
    ).astype(bf16)
    grad_up_low = (grad_hidden * silu_gate).astype(bf16)
    grad_both = jnp.concatenate([grad_gate_low, grad_up_low], 1)
    second_terms = dot_right_t(grad_both, gate_up).astype(bf16).reshape(planes, tokens, width)
    grad_second = plane_scatter(second_terms)

    down_term = dot_left_t(hidden_low, direct_all).astype(bf16)
    gate_up_term = dot_left_t(second_all, grad_both).astype(bf16)
    down_grad = lax.psum_scatter(down_term, "fsdp", scatter_dimension=0, tiled=True).astype(f32)
    gate_up_grad = lax.psum_scatter(
        after(gate_up_term, down_term), "fsdp", scatter_dimension=0, tiled=True
    ).astype(f32)
    branch_terms = dot_plain(hidden_low, down_use).astype(bf16).reshape(planes, tokens, width)
    branch_terms = after(branch_terms, grad_second)
    branch_feed = plane_scatter(branch_terms)
    output = (rows + keep * (branch_attention + branch_feed)).astype(bf16)

    second_gain_term = jnp.sum(grad_second * middle * inv_second, 0)
    weighted = grad_second * gain_second
    grad_middle = inv_second * weighted - middle * inv_second**3 * jnp.mean(
        weighted * middle, -1, keepdims=True
    )
    grad_branch_low = (direct + grad_middle).astype(bf16)
    grad_attended_low = dot_right_t(grad_branch_low, output_full).astype(bf16)
    grad_heads = lax.all_to_all(grad_attended_low, "fsdp", split_axis=1, concat_axis=0, tiled=True)
    dq, dk, dv = attend_back(queries, keys, values, starts, norm, mixed, grad_heads)
    turned = rotate(
        (jnp.concatenate([dq, dk], 1) * score_scale).reshape(length, heads + 1, HEAD_DIM),
        cosine,
        -sine_part,
    ).astype(bf16)
    grad_cols = jnp.concatenate([turned.reshape(length, own_width + HEAD_DIM), dv.astype(bf16)], 1)
    normed_terms = dot_right_t(grad_cols, project).astype(bf16)
    weighted_first = lax.psum_scatter(normed_terms, "fsdp", scatter_dimension=0, tiled=True).astype(f32)
    grad_rows = inv_first * weighted_first - rows * inv_first**3 * jnp.mean(
        weighted_first * rows, -1, keepdims=True
    )
    input_grad = cotangent + grad_middle + grad_rows

    project_term = dot_left_t(normed, grad_cols).astype(bf16).reshape(planes, ring * own_rows, cols)
    project_plane = plane_scatter(project_term).astype(bf16)
    back = lax.all_to_all(project_plane, "fsdp", split_axis=0, concat_axis=0, tiled=True)
    back = back.reshape(ring, own_rows, cols).astype(f32)

    def collect(low):
        parts = back[:, :, low : low + HEAD_DIM].reshape(KV_HEADS, sharers, own_rows, HEAD_DIM)
        return jnp.transpose(jnp.sum(parts, 1), (1, 0, 2)).reshape(own_rows, KV_HEADS * HEAD_DIM)

    query_plain = jnp.transpose(back[:, :, :own_width], (1, 0, 2)).reshape(own_rows, width)
    key_plain = collect(own_width)
    value_plain = collect(own_width + HEAD_DIM)
    first_gain_grad = (
        jnp.sum(query_plain * query_weight.astype(f32), 1)
        + jnp.sum(key_plain * key_weight.astype(f32), 1)
        + jnp.sum(value_plain * value_weight.astype(f32), 1)
    )
    attended_by_owner = jnp.transpose(
        attended_low.reshape(tokens, planes, ring, own_rows), (0, 2, 1, 3)
    ).reshape(tokens, width)
    output_term = dot_left_t(attended_by_owner, grad_branch_low).astype(bf16)
    output_plane = lax.psum_scatter(output_term, "fsdp", scatter_dimension=0, tiled=True)
    output_grad_weight = plane_scatter(output_plane.reshape(planes, own_rows, width))
    second_gain_all = lax.psum(lax.psum(second_gain_term, "fsdp"), "dp")
    mine = (lax.axis_index("dp") * ring + place) * own_rows
    second_gain_grad = lax.dynamic_slice_in_dim(second_gain_all, mine, own_rows)
    return (
        output[None],
        input_grad[None],
        first_gain_grad,
        query_plain * gain_mine,
        key_plain * gain_mine,
        value_plain * gain_mine,
        output_grad_weight,
        second_gain_grad,
        gate_up_grad[:, :ff_own],
        gate_up_grad[:, ff_own:],
        down_grad,
    )


PIECES = ((0, 0), (2, 0), (4, 0), (6, 0), (6, 1), (1, 0), (3, 0), (5, 0), (7, 0), (7, 1))
TO_CORE = (7, 3, 5, 1)
TO_CHIPS = (6, 2, 4, 0)
VMEM = pl.BlockSpec(memory_space=pltpu.VMEM)
SMEM = pl.BlockSpec(memory_space=pltpu.SMEM)
log2_e = math.log2(math.e)


def start_of(place, piece, rows):
    bit, half = PIECES[piece]
    return pl.multiple_of((place ^ bit) * rows + half * (rows // 2), rows // 2)


def turn(block, cosine, sine, forward):
    rolled = pltpu.roll(block, HEAD_DIM // 2, 1)
    return block * cosine + rolled * sine if forward else block * cosine - rolled * sine


def masked_scores(keys, queries, starts, low):
    scores = dot_right_t(keys, queries) * (score_scale * log2_e)
    key_pos = lax.broadcasted_iota(jnp.int32, scores.shape, 0)
    query_pos = lax.broadcasted_iota(jnp.int32, scores.shape, 1) + low
    return scores, (key_pos <= query_pos) & (key_pos >= starts)


def front_kernel(at_ref, normed_ref, *refs):
    columns_refs, refs = refs[:2], refs[2:]
    cos_ref, sin_ref, starts_ref, refs = refs[0], refs[1], refs[2], refs[3:]
    q_ref, k_ref, v_ref, mixed_ref, norm_ref, project_ref, gain_ref, vt_ref = refs
    place = at_ref[0]
    length = normed_ref.shape[0]
    core = place & 1
    group = place >> 1
    rows = columns_refs[0].shape[2] - 16
    q_width = q_ref.shape[1]
    q_all = 2 * q_width
    for owner in range(4):
        for bit in range(4):
            for side in range(2):
                block = columns_refs[side]
                device = 2 * (group ^ bit) + (core ^ side)
                here = pl.ds(pl.multiple_of((owner * 8 + device) * rows, rows), rows)
                for which in range(2):

                    @pl.when(core == which)
                    def _():
                        project_ref[here, :q_width] = block[owner, bit, :rows, which * q_width : (which + 1) * q_width]

                project_ref[here, q_width:] = block[owner, bit, :rows, q_all:]
                gain_ref[owner * 8 + device] = block[owner, bit, rows:, :HEAD_DIM]

    for low_row in range(0, length, 256):
        here = slice(low_row, low_row + 256)
        raw = dot_plain(normed_ref[here, :], project_ref[...])
        cosine, sine = cos_ref[here, :], sin_ref[here, :]
        for low in range(0, q_width, HEAD_DIM):
            q_ref[here, low : low + HEAD_DIM] = turn(
                raw[:, low : low + HEAD_DIM], cosine, sine, True
            ).astype(bf16)
        k_ref[here, :] = turn(raw[:, q_width : q_width + HEAD_DIM], cosine, sine, True).astype(bf16)
        v_ref[here, :] = raw[:, q_width + HEAD_DIM :].astype(bf16)
    vt_ref[...] = jnp.transpose(v_ref[...].astype(f32)).astype(bf16)
    block = 256
    for head in range(q_width // HEAD_DIM):
        cols = slice(head * HEAD_DIM, (head + 1) * HEAD_DIM)
        for low in range(0, length, block):
            high = low + block
            scores, allowed = masked_scores(
                k_ref[:high, :], q_ref[low:high, cols], starts_ref[:, low:high], low
            )
            scores = jnp.where(allowed, scores, mask_fill)
            top = jnp.max(scores, 0, keepdims=True)
            expo = jnp.exp2(scores - top)
            total = jnp.sum(expo, 0, keepdims=True)
            probs = (expo * (1.0 / total)).astype(bf16)
            mixed_ref[low:high, cols] = jnp.transpose(dot_plain(vt_ref[:, :high], probs)).astype(bf16)
            norm_ref[head, :, low:high] = top + jnp.log2(total)


def front(at, normed, columns, columns_other, cosine, sine, starts):
    length = normed.shape[0]
    q_width = (columns.shape[3] - 2 * HEAD_DIM) // 2
    cols = q_width + 2 * HEAD_DIM
    width = 32 * (columns.shape[2] - 16)
    shapes = [
        jax.ShapeDtypeStruct((length, q_width), bf16),
        jax.ShapeDtypeStruct((length, HEAD_DIM), bf16),
        jax.ShapeDtypeStruct((length, HEAD_DIM), bf16),
        jax.ShapeDtypeStruct((length, q_width), bf16),
        jax.ShapeDtypeStruct((q_width // HEAD_DIM, 1, length), f32),
        jax.ShapeDtypeStruct((width, cols), bf16),
        jax.ShapeDtypeStruct((32, 16, HEAD_DIM), bf16),
    ]
    return pl.pallas_call(
        front_kernel,
        in_specs=[SMEM] + [VMEM] * 6,
        out_specs=[VMEM] * 7,
        out_shape=shapes,
        scratch_shapes=[pltpu.VMEM((HEAD_DIM, length), bf16)],
        compiler_params=pltpu.CompilerParams(vmem_limit_bytes=52 << 20),
        cost_estimate=pl.CostEstimate(
            flops=2 * length * width * cols + 4 * length * length * q_width,
            bytes_accessed=2 * length * width + 4 * width * cols,
            transcendentals=length * length,
        ),
        name="front",
    )(at, normed, columns, columns_other, cosine, sine, starts)


def back_kernel(tokens, at_ref, q_ref, k_ref, v_ref, mixed_ref, norm_ref, grad_ref, project_ref,
                cos_ref, sin_ref, starts_ref, core_ref, chips_ref, cols_ref, kt_ref, dk_ref, dv_ref):
    place = at_ref[0]
    length, q_width = q_ref.shape
    block = 256
    kt_ref[...] = jnp.transpose(k_ref[...].astype(f32)).astype(bf16)
    dk_ref[...] = jnp.zeros_like(dk_ref)
    dv_ref[...] = jnp.zeros_like(dv_ref)
    for head in range(q_width // HEAD_DIM):
        cols = slice(head * HEAD_DIM, (head + 1) * HEAD_DIM)
        for low in range(0, length, block):
            high = low + block
            queries, grads = q_ref[low:high, cols], grad_ref[low:high, cols]
            scores, allowed = masked_scores(k_ref[:high, :], queries, starts_ref[:, low:high], low)
            probs = jnp.where(allowed, jnp.exp2(scores - norm_ref[head, :, low:high]), 0.0)
            grad_prob = dot_right_t(v_ref[:high, :], grads)
            weighed = jnp.transpose(grads.astype(f32) * mixed_ref[low:high, cols].astype(f32))
            grad_score = (probs * (grad_prob - jnp.sum(weighed, 0, keepdims=True))).astype(bf16)
            dv_ref[:high, :] += dot_plain(probs.astype(bf16), grads)
            dk_ref[:high, :] += dot_plain(grad_score, queries)
            dq = jnp.transpose(dot_plain(kt_ref[:, :high], grad_score)) * score_scale
            cols_ref[low:high, cols] = turn(
                dq, cos_ref[low:high, :], sin_ref[low:high, :], False
            ).astype(bf16)
    cols_ref[:, q_width : q_width + HEAD_DIM] = turn(
        dk_ref[...] * score_scale, cos_ref[...], sin_ref[...], False
    ).astype(bf16)
    cols_ref[:, q_width + HEAD_DIM :] = dv_ref[...].astype(bf16)
    for out_ref, bits in ((core_ref, TO_CORE), (chips_ref, TO_CHIPS)):
        for step, bit in enumerate(bits):
            here = pl.ds(pl.multiple_of((place ^ bit) * tokens, tokens), tokens)
            out_ref[step] = dot_right_t(cols_ref[here, :], project_ref[...]).astype(bf16)


def back(at, queries, keys, values, mixed, norm, grads, project, cosine, sine, starts):
    length, q_width = queries.shape
    width, cols = project.shape
    tokens = length // 8
    return pl.pallas_call(
        functools.partial(back_kernel, tokens),
        in_specs=[SMEM] + [VMEM] * 10,
        out_specs=[VMEM] * 3,
        out_shape=[
            jax.ShapeDtypeStruct((4, tokens, width), bf16),
            jax.ShapeDtypeStruct((4, tokens, width), bf16),
            jax.ShapeDtypeStruct((length, cols), bf16),
        ],
        scratch_shapes=[
            pltpu.VMEM((HEAD_DIM, length), bf16),
            pltpu.VMEM((length, HEAD_DIM), f32),
            pltpu.VMEM((length, HEAD_DIM), f32),
        ],
        compiler_params=pltpu.CompilerParams(vmem_limit_bytes=52 << 20),
        cost_estimate=pl.CostEstimate(
            flops=140 * length * width * cols + 7 * length * length * q_width,
            bytes_accessed=2 * length * width + 2 * width * cols,
            transcendentals=length * length,
        ),
        name="back",
    )(at, queries, keys, values, mixed, norm, grads, project, cosine, sine, starts)


def project_grad_kernel(normed_ref, cols_ref, out_ref):
    out_ref[...] = jnp.transpose(dot_left_t(cols_ref[...], normed_ref[...])).astype(bf16)


def project_grad(normed, grad_cols):
    length, width = normed.shape
    cols = grad_cols.shape[1]
    part = 512
    return pl.pallas_call(
        project_grad_kernel,
        grid=(width // part,),
        in_specs=[
            pl.BlockSpec((length, part), lambda i: (0, i)),
            pl.BlockSpec((length, cols), lambda i: (0, 0)),
        ],
        out_specs=pl.BlockSpec((part, cols), lambda i: (i, 0)),
        out_shape=jax.ShapeDtypeStruct((width, cols), bf16),
        compiler_params=pltpu.CompilerParams(vmem_limit_bytes=52 << 20),
        cost_estimate=pl.CostEstimate(
            flops=10 * length * width * cols, bytes_accessed=2 * length * width, transcendentals=0
        ),
        name="project_grad",
    )(normed, grad_cols)


def output_grad_kernel(tokens, at_ref, *refs):
    pieces, (mixed_ref, other_ref, out_ref, rest_ref, gain_ref) = refs[:5], refs[5:]
    place = at_ref[0]
    core = place & 1
    totals = [None, None]
    gain = None
    for piece in range(5):
        bit, half = PIECES[piece]
        rows = tokens // 2 if bit >= 6 else tokens
        here = pl.ds(start_of(place, piece, tokens), rows)
        block = pieces[piece][:rows, :]
        for side, ref in enumerate((mixed_ref, other_ref)):
            term = dot_left_t(ref[here, :], block)
            totals[side] = term if totals[side] is None else totals[side] + term
        if pieces[piece].shape[0] > rows:
            extra = jnp.sum(pieces[piece][rows:, :].astype(f32), 0, keepdims=True)
            gain = extra if gain is None else gain + extra
    gain_ref[...] = gain
    rows = out_ref.shape[1]
    for side, total in enumerate(totals):
        blocks = total.astype(bf16).reshape(4, rows, total.shape[1])
        first = 2 * (core ^ side)
        for head in range(2):
            for which in range(2):

                @pl.when(core == which)
                def _():
                    out_ref[first + head] = blocks[2 * head + which]
                    rest_ref[first + head] = blocks[2 * head + 1 - which]


def output_grad_term(at, pieces, mixed, mixed_other):
    length, own = mixed.shape
    tokens, width = length // 8, pieces[0].shape[1]
    shape = jax.ShapeDtypeStruct((4, own // 4, width), bf16)
    return pl.pallas_call(
        functools.partial(output_grad_kernel, tokens),
        in_specs=[SMEM] + [VMEM] * 7,
        out_specs=[VMEM] * 3,
        out_shape=[shape, shape, jax.ShapeDtypeStruct((1, width), f32)],
        compiler_params=pltpu.CompilerParams(vmem_limit_bytes=52 << 20),
        cost_estimate=pl.CostEstimate(
            flops=2 * length * own * width, bytes_accessed=2 * length * width, transcendentals=0
        ),
        name="output_grad_term",
    )(at, *pieces, mixed, mixed_other)


def feed_kernel(units, count, at_ref, *refs):
    d_refs, n_ref, both_ref, down_ref, rows_ref, refs = refs[:4], *refs[4:8], refs[8 + count :]
    second_ref, direct_ref, hidden_ref, grads_ref, term_ref, held_ref = refs
    step = pl.program_id(0)

    @pl.when(step == 0)
    def _():
        second_ref[...] = n_ref[...].reshape(second_ref.shape)
        tokens = n_ref.shape[1]
        for slot in range(4):
            owner = (at_ref[1] - slot) & 3
            direct_ref[pl.ds(pl.multiple_of(owner * tokens, tokens), tokens), :] = d_refs[slot][...]

    @pl.when(step < units)
    def _():
        raw = dot_plain(second_ref[...], both_ref[...])
        half = raw.shape[1] // 2
        gate, upward = raw[:, :half], raw[:, half:]
        sig = 1.0 / (1.0 + jnp.exp(-gate))
        silu = gate * sig
        hidden_ref[...] = (silu * upward).astype(bf16)
        grad_hidden = dot_right_t(direct_ref[...], down_ref[...])
        grad_gate = (grad_hidden * upward * sig * (1.0 + gate * (1.0 - sig))).astype(bf16)
        grads = jnp.concatenate([grad_gate, (grad_hidden * silu).astype(bf16)], 1)
        grads_ref[...] = grads
        held_ref[step] = grads

    @pl.when(step >= units)
    def _():
        total = None
        for unit in range(units):
            cols = slice(unit * held_ref.shape[2], (unit + 1) * held_ref.shape[2])
            part = dot_right_t(held_ref[unit], rows_ref[:, cols])
            total = part if total is None else total + part
        term_ref[...] = total.astype(bf16).reshape(term_ref.shape)


def feed(at, part_at, parts_of, seconds, directs, both, down, so_far):
    tokens, width = seconds.shape[1:]
    some = 4 * tokens
    ff = down.shape[0]
    unit, part = 128, 256
    units, parts = ff // unit, width // part
    so_far = so_far or []
    total = parts_of * some
    outs = pl.pallas_call(
        functools.partial(feed_kernel, units, len(so_far)),
        grid=(units + parts,),
        in_specs=[
            SMEM,
            *[pl.BlockSpec((tokens, width), lambda i: (part_at, 0))] * 4,
            pl.BlockSpec((4, tokens, width), lambda i: (0, 0, 0)),
            pl.BlockSpec((width, 2 * unit), lambda i: (0, jnp.minimum(i, units - 1))),
            pl.BlockSpec((unit, width), lambda i: (jnp.minimum(i, units - 1), 0)),
            pl.BlockSpec((part, 2 * ff), lambda i: (jnp.maximum(i - units, 0), 0)),
        ]
        + [pl.BlockSpec(memory_space=pl.ANY)] * len(so_far),
        out_specs=[
            pl.BlockSpec((some, width), lambda i: (part_at, 0)),
            pl.BlockSpec((some, width), lambda i: (part_at, 0)),
            pl.BlockSpec((some, unit), lambda i: (part_at, jnp.minimum(i, units - 1))),
            pl.BlockSpec((some, 2 * unit), lambda i: (part_at, jnp.minimum(i, units - 1))),
            pl.BlockSpec((4, tokens, part), lambda i: (0, 0, jnp.maximum(i - units, 0))),
        ],
        out_shape=[
            jax.ShapeDtypeStruct((total, width), bf16),
            jax.ShapeDtypeStruct((total, width), bf16),
            jax.ShapeDtypeStruct((total, ff), bf16),
            jax.ShapeDtypeStruct((total, 2 * ff), bf16),
            jax.ShapeDtypeStruct((4, tokens, width), bf16),
        ],
        scratch_shapes=[pltpu.VMEM((units, some, 2 * unit), bf16)],
        input_output_aliases={9 + i: i for i in range(len(so_far))},
        compiler_params=pltpu.CompilerParams(vmem_limit_bytes=52 << 20),
        cost_estimate=pl.CostEstimate(
            flops=10 * some * width * ff,
            bytes_accessed=10 * width * ff,
            transcendentals=some * ff,
        ),
        name="feed",
    )(at, *directs, seconds, both, down, both, *so_far)
    return outs[:4], outs[4]


def split_kernel(both_ref, gate_ref, up_ref):
    half = gate_ref.shape[1]
    gate_ref[...] = both_ref[:, :half].astype(f32)
    up_ref[...] = both_ref[:, half:].astype(f32)


def split(both):
    rows, cols = both.shape
    out = jax.ShapeDtypeStruct((rows, cols // 2), f32)
    half = pl.BlockSpec((rows, 128), lambda i: (0, i))
    return pl.pallas_call(
        split_kernel,
        grid=(cols // 256,),
        in_specs=[pl.BlockSpec((rows, 256), lambda i: (0, i))],
        out_specs=[half, half],
        out_shape=[out, out],
        name="split",
    )(both)


def fast_device(
    layer_input,
    output_grad,
    layer_keep,
    group_ids,
    exit_scale,
    doc_lengths,
    attention_gain,
    query_weight,
    key_weight,
    value_weight,
    output_weight,
    feedforward_gain,
    gate_weight,
    up_weight,
    down_weight,
):
    tokens, width = layer_input.shape[1:]
    place, plane = lax.axis_index("fsdp"), lax.axis_index("dp")
    at = jnp.stack([place, plane]).astype(jnp.int32)
    length = tokens * 8
    own_rows = query_weight.shape[0]
    q_width = HEADS // 8 * HEAD_DIM
    cols = q_width + 2 * HEAD_DIM
    ff_own = gate_weight.shape[1]
    half = tokens // 2
    rows = layer_input[0].astype(f32)
    keep = layer_keep[0].astype(f32)

    both_mine = jnp.stack(
        [gate_weight.reshape(-1, ff_own // 128, 128), up_weight.reshape(-1, ff_own // 128, 128)], 2
    ).reshape(-1, 2 * ff_own)
    inv_first = rms_scale(rows)
    normed = (rows * inv_first).astype(bf16)
    first = lax.all_gather(jnp.concatenate([normed, down_weight], 0), "fsdp", axis=0, tiled=False)
    normed_all = first[:, :tokens].reshape(length, width)
    down_use = first[:, tokens:].reshape(ff_own, width)
    gain_mine = attention_gain.astype(f32)[:, None]

    def by_chip(weight):
        scaled = (weight.astype(f32) * gain_mine).astype(bf16)
        return scaled.reshape(own_rows, 4, weight.shape[1] // 4)

    sent = jnp.concatenate([by_chip(query_weight), by_chip(key_weight), by_chip(value_weight)], -1)
    sent = jnp.transpose(sent, (1, 0, 2))
    wide = sent.shape[2]
    gain_rows = jnp.pad(feedforward_gain[None, :], ((0, 15), (0, wide - own_rows)))
    group = place // 2

    def to_chip(bit):
        block = lax.dynamic_index_in_dim(sent, group ^ bit, 0, keepdims=False)
        return jnp.concatenate([block, gain_rows], 0)

    columns = jnp.stack([to_chip(0)] + [flip(to_chip(bit), 2 * bit) for bit in (1, 2, 3)])
    output_plane = gather_planes(after(output_weight, columns))
    columns = gather_planes(after(columns, output_plane))
    columns_other = flip(columns, 1)
    output_full = lax.all_gather(output_plane, "fsdp", axis=1, tiled=True).reshape(width, width)
    both = lax.all_gather(after(both_mine, columns), "fsdp", axis=0, tiled=True)
    picked = jnp.sum(
        jnp.where(jnp.arange(exit_scale.shape[0], dtype=jnp.int32) == group_ids[0], exit_scale, 0.0)
    )
    cotangent = output_grad[0].astype(f32) * picked
    direct = keep * cotangent

    half_dim = HEAD_DIM // 2
    cosine, sine = rotary_tables(length)
    cosine, sine = cosine[:, 0], sine[:, 0]
    cosine = jnp.concatenate([cosine, cosine], 1)
    sine = jnp.concatenate([-sine, sine], 1)
    order = jnp.arange(doc_lengths.shape[1])
    ends = jnp.sum(jnp.where(order[None, :] <= order[:, None], doc_lengths[0][None, :], 0), 1)
    positions = jnp.arange(length, dtype=jnp.int32)
    starts = jnp.max(jnp.where(positions[None, :] >= ends[:, None], ends[:, None], 0), 0)[None, :]

    direct_low = after(direct.astype(bf16), columns)
    direct_1 = shift(direct_low, 1)
    queries, keys, values, mixed, norm, project, gains = front(
        at, normed_all, columns, columns_other, cosine, sine, starts
    )
    mixed = after(mixed, direct_1)
    direct_2 = shift(direct_low, 2)
    mixed_other = flip(mixed, 1)
    gain_second = gains[:, 0, :own_rows].reshape(width).astype(f32)

    attended_low = lax.all_to_all(mixed, "fsdp", split_axis=0, concat_axis=1, tiled=True)
    direct_3 = shift(direct_low, 3)
    attended_low = after(attended_low, direct_2)
    branch_attention = dot_plain(attended_low, output_full)
    middle = rows + branch_attention
    inv_second = rms_scale(middle)
    directs = [direct_low, direct_1, direct_2, direct_3]
    second_mine = (middle * inv_second * gain_second).astype(bf16)
    seconds_low = gather_planes(after(second_mine[:half], direct_3, mixed_other))
    seconds_high = gather_planes(after(second_mine[half:], seconds_low))

    stacked, terms_low = feed(at, 0, 2, seconds_low, directs, both, down_use, None)
    stacked, terms_high = feed(at, 1, 2, seconds_high, directs, both, down_use, stacked)
    second_all, direct_all, hidden_all, grads_all = stacked
    got_low = swap_planes(terms_low)

    down_term = dot_left_t(hidden_all, direct_all).astype(bf16)
    got_high = swap_planes(after(terms_high, got_low))
    grad_second = jnp.concatenate(
        [jnp.sum(got_low.astype(f32), 0), jnp.sum(got_high.astype(f32), 0)], 0
    )
    both_term = dot_left_t(second_all, grads_all).astype(bf16)
    down_grad = lax.psum_scatter(down_term, "fsdp", scatter_dimension=0, tiled=True).astype(f32)
    both_grad = lax.psum_scatter(both_term, "fsdp", scatter_dimension=0, tiled=True)
    branch_terms = dot_plain(hidden_all, down_use).astype(bf16).reshape(2, 4, half, width)
    branch_terms = jnp.transpose(branch_terms, (1, 0, 2, 3)).reshape(4, tokens, width)

    weighted = grad_second * gain_second
    grad_middle = inv_second * weighted - middle * inv_second**3 * jnp.mean(
        weighted * middle, -1, keepdims=True
    )
    grad_branch = (direct + grad_middle).astype(bf16)
    grad_attended = dot_right_t(grad_branch, output_full).astype(bf16)
    grad_heads = lax.all_to_all(grad_attended, "fsdp", split_axis=1, concat_axis=0, tiled=True)
    gain_term = jnp.sum(grad_second * middle * inv_second, 0, keepdims=True)
    gain_high = gain_term.astype(bf16)
    gain_low = (gain_term - gain_high.astype(f32)).astype(bf16)
    branch_block = jnp.concatenate(
        [grad_branch, gain_high, gain_low, jnp.zeros((14, width), bf16)], 0
    )
    ahead = [
        lax.dynamic_index_in_dim(branch_terms, (plane + k) % 4, 0, keepdims=False) for k in range(4)
    ]
    branch_1, branch_3 = shift(after(ahead[1], grad_branch), 1), shift(after(ahead[3], grad_branch), 3)
    branch_x, branch_y = flip(branch_block, 2), flip(branch_block, 4)
    grad_heads = after(grad_heads, branch_x, branch_y, branch_1, branch_3)
    branch_2 = shift(after(ahead[2], grad_branch), 2)
    branch_low, branch_high = flip(branch_x[:half], 4), flip(branch_y[half:], 2)
    core_terms, chip_terms, grad_cols = back(
        at, queries, keys, values, mixed, norm, grad_heads, project, cosine, sine, starts
    )
    core_terms = after(core_terms, branch_2, branch_low, branch_high)
    other = flip(core_terms, 1)
    branch_pieces = [branch_block, branch_x, branch_y, branch_low, branch_high]
    mine, others, gain_sum = output_grad_term(at, branch_pieces, after(mixed, core_terms), mixed_other)
    other = after(other, mine)
    sums = [add_low(chip_terms[i], other[i]) for i in range(3)]
    far, near_x, near_y = flip(sums[0], 6), flip(sums[1], 2), flip(sums[2], 4)
    project_term = project_grad(normed_all, after(grad_cols, *sums)).reshape(4, width // 4, cols)
    project_got = swap_planes(project_term)
    branch_feed = (
        ahead[0].astype(f32) + branch_1.astype(f32) + branch_2.astype(f32) + branch_3.astype(f32)
    )
    group, core = place // 2, place % 2
    gain_own = lax.dynamic_slice_in_dim(gain_sum[0], group * 8 * own_rows, 8 * own_rows)
    gain_own = gain_own.reshape(4, 2, own_rows).astype(bf16)
    gain_own = jnp.pad(gain_own[:, :, None, :], ((0, 0), (0, 0), (0, 15), (0, width - own_rows)))
    mine = jnp.concatenate([mine, lax.dynamic_index_in_dim(gain_own, core, 1, keepdims=False)], 1)
    others = jnp.concatenate([others, lax.dynamic_index_in_dim(gain_own, 1 - core, 1, keepdims=False)], 1)
    output_sum = output_rows(after(mine, far, near_x, near_y), others, project_got)
    project_plane = jnp.sum(project_got.astype(f32), 0).astype(bf16)
    weighted_first = (
        chip_terms[3].astype(f32)
        + other[3].astype(f32)
        + far.astype(f32)
        + near_x.astype(f32)
        + near_y.astype(f32)
    )
    grad_rows = inv_first * weighted_first - rows * inv_first**3 * jnp.mean(
        weighted_first * rows, -1, keepdims=True
    )
    input_grad = cotangent + grad_middle + grad_rows

    output = (rows + keep * (branch_attention + branch_feed)).astype(bf16)

    back_cols = lax.all_to_all(project_plane, "fsdp", split_axis=0, concat_axis=0, tiled=True)
    back_cols = back_cols.reshape(8, own_rows, cols).astype(f32)

    def collect(at_col):
        parts = back_cols[:, :, at_col : at_col + HEAD_DIM].reshape(KV_HEADS, 2, own_rows, HEAD_DIM)
        return jnp.transpose(jnp.sum(parts, 1), (1, 0, 2)).reshape(own_rows, KV_HEADS * HEAD_DIM)

    query_plain = jnp.transpose(back_cols[:, :, :q_width], (1, 0, 2)).reshape(own_rows, width)
    key_plain = collect(q_width)
    value_plain = collect(q_width + HEAD_DIM)
    first_gain_grad = (
        jnp.sum(query_plain * query_weight.astype(f32), 1)
        + jnp.sum(key_plain * key_weight.astype(f32), 1)
        + jnp.sum(value_plain * value_weight.astype(f32), 1)
    )
    gate_grad, up_grad = split(both_grad)
    return (
        output[None],
        input_grad[None],
        first_gain_grad,
        query_plain * gain_mine,
        key_plain * gain_mine,
        value_plain * gain_mine,
        output_sum[:own_rows],
        output_sum[own_rows, :own_rows],
        gate_grad,
        up_grad,
        down_grad,
    )


def solution(mesh):
    both = ("dp", "fsdp")
    fast = (mesh.shape["dp"], mesh.shape["fsdp"]) == (4, 8)
    return jax.shard_map(
        fast_device if fast else per_device,
        mesh=mesh,
        in_specs=(
            P("dp", "fsdp", None),
            P("dp", "fsdp", None),
            P("dp"),
            P("dp"),
            P(),
            P("dp", None),
            P(both),
            P(both, None),
            P(both, None),
            P(both, None),
            P(both, None),
            P(both),
            P("fsdp", "dp"),
            P("fsdp", "dp"),
            P(both, None),
        ),
        out_specs=(
            P("dp", "fsdp", None),
            P("dp", "fsdp", None),
            P(both),
            P(both, None),
            P(both, None),
            P(both, None),
            P(both, None),
            P(both),
            P("fsdp", "dp"),
            P("fsdp", "dp"),
            P(both, None),
        ),
        check_vma=False,
    )
```

```python
import functools
import math

import jax
import jax.numpy as jnp
from jax import lax
from jax.experimental import pallas as pl
from jax.experimental.pallas import tpu as pltpu
from jax.sharding import PartitionSpec as P

HEADS = 16
KV_HEADS = 4
HEAD_DIM = 128

norm_eps = 1e-05
rope_base = 10000.0
mask_fill = -1e30
score_scale = 1.0 / math.sqrt(HEAD_DIM)
f32 = jnp.float32
bf16 = jnp.bfloat16


def dot_plain(left, right):
    return jnp.dot(left, right, preferred_element_type=f32)


def dot_right_t(left, right):
    return lax.dot_general(left, right, (((1,), (1,)), ((), ())), preferred_element_type=f32)


def dot_left_t(left, right):
    return lax.dot_general(left, right, (((0,), (0,)), ((), ())), preferred_element_type=f32)


def rotary_tables(length):
    half_dim = HEAD_DIM // 2
    frequency = rope_base ** (-(2.0 * jnp.arange(half_dim, dtype=f32)) / HEAD_DIM)
    angles = jnp.arange(length, dtype=jnp.int32).astype(f32)[:, None] * frequency[None, :]
    return (jnp.cos(angles)[:, None, :], jnp.sin(angles)[:, None, :])


def rotate(vectors, cosine, sine_part):
    half_dim = vectors.shape[-1] // 2
    lower_half = vectors[..., :half_dim]
    upper_half = vectors[..., half_dim:]
    return jnp.concatenate(
        [
            lower_half * cosine - upper_half * sine_part,
            upper_half * cosine + lower_half * sine_part,
        ],
        -1,
    )


def rms_scale(rows):
    return lax.rsqrt(jnp.mean(rows * rows, -1, keepdims=True) + norm_eps)


def after_all(values, *earlier):
    return lax.optimization_barrier((*values, *earlier))[: len(values)]


def after(value, *earlier):
    return lax.optimization_barrier((value, *earlier))[0]


def plane_gather(block):
    whole = lax.all_gather(block, "dp", axis=0)
    return [whole[i] for i in range(whole.shape[0])]


def add_low(left, right):
    return (left.astype(f32) + right.astype(f32)).astype(left.dtype)


def plane_scatter(whole):
    return lax.psum_scatter(whole, "dp", scatter_dimension=0, tiled=False).astype(f32)


FLIP = {bit: [(i, i ^ bit) for i in range(8)] for bit in (1, 2, 4, 6)}


def flip(block, bit):
    return lax.ppermute(block, "fsdp", FLIP[bit])


def shift(block, step):
    return lax.ppermute(block, "dp", [(i, (i + step) % 4) for i in range(4)])


UP = [(0, 1), (1, 2), (2, 3)]
DOWN = [(1, 0), (2, 1), (3, 2)]
LINE = (0, -1, 1, -2, 2, 3)


def line_first(block):
    return lax.ppermute(block, "dp", UP), lax.ppermute(block, "dp", DOWN)


def line_second(up, down):
    plane = lax.axis_index("dp")
    far = jnp.where(plane == 2, down, up)
    return (
        lax.ppermute(up, "dp", UP[1:]),
        lax.ppermute(down, "dp", DOWN[:2]),
        lax.ppermute(far, "dp", [(2, 0), (1, 3)]),
    )


def gather_planes(block):
    copies = jnp.broadcast_to(block[None], (4, *block.shape))
    return lax.all_to_all(copies, "dp", split_axis=0, concat_axis=0)


def swap_planes(whole):
    return lax.all_to_all(whole, "dp", split_axis=0, concat_axis=0)


def block_rows_of(length):
    return math.gcd(length, 256)


def transposed_scores(keys, queries, starts, low, high, width):
    scores = dot_right_t(keys, queries) * score_scale
    key_pos = lax.broadcasted_iota(jnp.int32, (width, high - low), 0)
    query_pos = lax.broadcasted_iota(jnp.int32, (width, high - low), 1) + low
    allowed = (key_pos <= query_pos) & (key_pos >= starts)
    return scores, allowed


def attend_kernel(rows_of, q_ref, k_ref, vt_ref, starts_ref, out_ref, norm_ref):
    length = q_ref.shape[0]
    for low in range(0, length, rows_of):
        high = low + rows_of
        starts = starts_ref[:, low:high]
        scores, allowed = transposed_scores(
            k_ref[:high, :], q_ref[low:high, :], starts, low, high, high
        )
        scores = jnp.where(allowed, scores, mask_fill)
        top = jnp.max(scores, 0, keepdims=True)
        expo = jnp.exp(scores - top)
        total = jnp.sum(expo, 0, keepdims=True)
        probs = (expo * (1.0 / total)).astype(bf16)
        mixed = dot_plain(vt_ref[:, :high], probs)
        out_ref[low:high, :] = jnp.transpose(mixed).astype(out_ref.dtype)
        norm_ref[0, :, low:high] = top + jnp.log(total)


def attend(queries, keys, values, starts):
    length, width = queries.shape
    heads = width // HEAD_DIM
    return pl.pallas_call(
        functools.partial(attend_kernel, block_rows_of(length)),
        grid=(heads,),
        in_specs=[
            pl.BlockSpec((length, HEAD_DIM), lambda h: (0, h)),
            pl.BlockSpec((length, HEAD_DIM), lambda h: (0, 0)),
            pl.BlockSpec((HEAD_DIM, length), lambda h: (0, 0)),
            pl.BlockSpec((1, length), lambda h: (0, 0)),
        ],
        out_specs=[
            pl.BlockSpec((length, HEAD_DIM), lambda h: (0, h)),
            pl.BlockSpec((1, 1, length), lambda h: (h, 0, 0)),
        ],
        out_shape=[
            jax.ShapeDtypeStruct((length, width), bf16),
            jax.ShapeDtypeStruct((heads, 1, length), f32),
        ],
        compiler_params=pltpu.CompilerParams(vmem_limit_bytes=48 << 20),
        cost_estimate=pl.CostEstimate(
            flops=3 * heads * length * length * HEAD_DIM,
            bytes_accessed=8 * length * width,
            transcendentals=heads * length * length,
        ),
        name="attend",
    )(queries, keys, jnp.transpose(values), starts)


def attend_back_kernel(
    rows_of, q_ref, k_ref, kt_ref, v_ref, starts_ref, norm_ref, out_ref, grad_ref, dq_ref, dk_ref, dv_ref
):
    length = q_ref.shape[0]

    @pl.when(pl.program_id(0) == 0)
    def _():
        dk_ref[...] = jnp.zeros_like(dk_ref)
        dv_ref[...] = jnp.zeros_like(dv_ref)

    for low in range(0, length, rows_of):
        high = low + rows_of
        starts = starts_ref[:, low:high]
        queries = q_ref[low:high, :]
        grads = grad_ref[low:high, :]
        scores, allowed = transposed_scores(k_ref[:high, :], queries, starts, low, high, high)
        probs = jnp.where(allowed, jnp.exp(scores - norm_ref[0, :, low:high]), 0.0)
        grad_prob = dot_right_t(v_ref[:high, :], grads)
        weighed = jnp.transpose(grads.astype(f32) * out_ref[low:high, :].astype(f32))
        delta = jnp.sum(weighed, 0, keepdims=True)
        grad_score = (probs * (grad_prob - delta)).astype(bf16)
        dv_ref[:high, :] += dot_plain(probs.astype(bf16), grads)
        dk_ref[:high, :] += dot_plain(grad_score, queries)
        dq_ref[low:high, :] = jnp.transpose(dot_plain(kt_ref[:, :high], grad_score))


def attend_back(queries, keys, values, starts, norm, out, grads):
    length, width = queries.shape
    heads = width // HEAD_DIM
    by_head = pl.BlockSpec((length, HEAD_DIM), lambda h: (0, h))
    shared = pl.BlockSpec((length, HEAD_DIM), lambda h: (0, 0))
    return pl.pallas_call(
        functools.partial(attend_back_kernel, block_rows_of(length)),
        grid=(heads,),
        in_specs=[
            by_head,
            shared,
            pl.BlockSpec((HEAD_DIM, length), lambda h: (0, 0)),
            shared,
            pl.BlockSpec((1, length), lambda h: (0, 0)),
            pl.BlockSpec((1, 1, length), lambda h: (h, 0, 0)),
            by_head,
            by_head,
        ],
        out_specs=[by_head, shared, shared],
        out_shape=[
            jax.ShapeDtypeStruct((length, width), f32),
            jax.ShapeDtypeStruct((length, HEAD_DIM), f32),
            jax.ShapeDtypeStruct((length, HEAD_DIM), f32),
        ],
        compiler_params=pltpu.CompilerParams(vmem_limit_bytes=56 << 20),
        cost_estimate=pl.CostEstimate(
            flops=7 * heads * length * length * HEAD_DIM,
            bytes_accessed=16 * length * width,
            transcendentals=heads * length * length,
        ),
        name="attend_back",
    )(queries, keys, jnp.transpose(keys), values, starts, norm, out, grads)


def per_device(
    layer_input,
    output_grad,
    layer_keep,
    group_ids,
    exit_scale,
    doc_lengths,
    attention_gain,
    query_weight,
    key_weight,
    value_weight,
    output_weight,
    feedforward_gain,
    gate_weight,
    up_weight,
    down_weight,
):
    tokens, width = layer_input.shape[1:]
    ring = lax.axis_size("fsdp")
    planes = lax.axis_size("dp")
    place = lax.axis_index("fsdp")
    length = tokens * ring
    own_rows = query_weight.shape[0]
    heads = HEADS // ring
    own_width = heads * HEAD_DIM
    ff_own = gate_weight.shape[1]
    rows = layer_input[0].astype(f32)
    keep = layer_keep[0].astype(f32)

    inv_first = rms_scale(rows)
    normed = lax.all_gather((rows * inv_first).astype(bf16), "fsdp", axis=0, tiled=True)

    gain_mine = attention_gain.astype(f32)[:, None]
    sharers = ring // KV_HEADS
    cols = own_width + 2 * HEAD_DIM

    def spread(weight):
        heads_of = (weight.astype(f32) * gain_mine).astype(bf16).reshape(own_rows, KV_HEADS, 1, HEAD_DIM)
        return jnp.broadcast_to(heads_of, (own_rows, KV_HEADS, sharers, HEAD_DIM)).reshape(
            own_rows, ring, HEAD_DIM
        )

    query_scaled = (query_weight.astype(f32) * gain_mine).astype(bf16).reshape(own_rows, ring, own_width)
    sent = jnp.concatenate([query_scaled, spread(key_weight), spread(value_weight)], -1)
    sent = jnp.transpose(sent, (1, 0, 2)).reshape(ring * own_rows, cols)
    plane_cols = lax.all_to_all(sent, "fsdp", split_axis=0, concat_axis=0, tiled=True)
    project = jnp.concatenate(plane_gather(plane_cols), 0)

    picked = jnp.sum(
        jnp.where(jnp.arange(exit_scale.shape[0], dtype=jnp.int32) == group_ids[0], exit_scale, 0.0)
    )
    cotangent = output_grad[0].astype(f32) * picked
    direct = keep * cotangent
    direct_all = jnp.concatenate(plane_gather(direct.astype(bf16)), 0)

    gain_second = lax.all_gather(
        lax.all_gather(feedforward_gain, "fsdp", axis=0, tiled=False), "dp", axis=0, tiled=False
    ).reshape(width).astype(f32)

    output_full = lax.all_gather(output_weight, ("dp", "fsdp"), axis=0, tiled=True)
    gate_up = jnp.concatenate([gate_weight, up_weight], 1)
    gate_up = lax.all_gather(gate_up, "fsdp", axis=0, tiled=True)
    down_use = lax.all_gather(down_weight, "fsdp", axis=0, tiled=True)

    cosine, sine_part = rotary_tables(length)
    ends = jnp.sum(
        jnp.where(
            jnp.arange(doc_lengths.shape[1])[None, :] <= jnp.arange(doc_lengths.shape[1])[:, None],
            doc_lengths[0][None, :],
            0,
        ),
        1,
    )
    positions = jnp.arange(length, dtype=jnp.int32)
    starts = jnp.max(jnp.where(positions[None, :] >= ends[:, None], ends[:, None], 0), 0)[None, :]
    raw = dot_plain(normed, project)
    rotated = rotate(
        raw[:, : own_width + HEAD_DIM].reshape(length, heads + 1, HEAD_DIM), cosine, sine_part
    ).astype(bf16)
    queries = rotated[:, :heads].reshape(length, own_width)
    keys = rotated[:, heads]
    values = raw[:, own_width + HEAD_DIM :].astype(bf16)
    mixed, norm = attend(queries, keys, values, starts)
    attended_low = lax.all_to_all(mixed, "fsdp", split_axis=0, concat_axis=1, tiled=True)
    branch_attention = dot_plain(attended_low, output_full)
    middle = rows + branch_attention
    inv_second = rms_scale(middle)
    second_mine = (middle * inv_second * gain_second).astype(bf16)

    second_all = jnp.concatenate(plane_gather(second_mine), 0)
    gate_use, up_use = gate_up[:, :ff_own], gate_up[:, ff_own:]
    gate_pre = dot_plain(second_all, gate_use)
    upward = dot_plain(second_all, up_use)
    sigmoid_gate = 1.0 / (1.0 + jnp.exp(-gate_pre))
    silu_gate = gate_pre * sigmoid_gate
    hidden_low = (silu_gate * upward).astype(bf16)
    grad_hidden = dot_right_t(direct_all, down_use)
    grad_gate_low = (
        grad_hidden * upward * sigmoid_gate * (1.0 + gate_pre * (1.0 - sigmoid_gate))
    ).astype(bf16)
    grad_up_low = (grad_hidden * silu_gate).astype(bf16)
    grad_both = jnp.concatenate([grad_gate_low, grad_up_low], 1)
    second_terms = dot_right_t(grad_both, gate_up).astype(bf16).reshape(planes, tokens, width)
    grad_second = plane_scatter(second_terms)

    down_term = dot_left_t(hidden_low, direct_all).astype(bf16)
    gate_up_term = dot_left_t(second_all, grad_both).astype(bf16)
    down_grad = lax.psum_scatter(down_term, "fsdp", scatter_dimension=0, tiled=True).astype(f32)
    gate_up_grad = lax.psum_scatter(
        after(gate_up_term, down_term), "fsdp", scatter_dimension=0, tiled=True
    ).astype(f32)
    branch_terms = dot_plain(hidden_low, down_use).astype(bf16).reshape(planes, tokens, width)
    branch_terms = after(branch_terms, grad_second)
    branch_feed = plane_scatter(branch_terms)
    output = (rows + keep * (branch_attention + branch_feed)).astype(bf16)

    second_gain_term = jnp.sum(grad_second * middle * inv_second, 0)
    weighted = grad_second * gain_second
    grad_middle = inv_second * weighted - middle * inv_second**3 * jnp.mean(
        weighted * middle, -1, keepdims=True
    )
    grad_branch_low = (direct + grad_middle).astype(bf16)
    grad_attended_low = dot_right_t(grad_branch_low, output_full).astype(bf16)
    grad_heads = lax.all_to_all(grad_attended_low, "fsdp", split_axis=1, concat_axis=0, tiled=True)
    dq, dk, dv = attend_back(queries, keys, values, starts, norm, mixed, grad_heads)
    turned = rotate(
        (jnp.concatenate([dq, dk], 1) * score_scale).reshape(length, heads + 1, HEAD_DIM),
        cosine,
        -sine_part,
    ).astype(bf16)
    grad_cols = jnp.concatenate([turned.reshape(length, own_width + HEAD_DIM), dv.astype(bf16)], 1)
    normed_terms = dot_right_t(grad_cols, project).astype(bf16)
    weighted_first = lax.psum_scatter(normed_terms, "fsdp", scatter_dimension=0, tiled=True).astype(f32)
    grad_rows = inv_first * weighted_first - rows * inv_first**3 * jnp.mean(
        weighted_first * rows, -1, keepdims=True
    )
    input_grad = cotangent + grad_middle + grad_rows

    project_term = dot_left_t(normed, grad_cols).astype(bf16).reshape(planes, ring * own_rows, cols)
    project_plane = plane_scatter(project_term).astype(bf16)
    back = lax.all_to_all(project_plane, "fsdp", split_axis=0, concat_axis=0, tiled=True)
    back = back.reshape(ring, own_rows, cols).astype(f32)

    def collect(low):
        parts = back[:, :, low : low + HEAD_DIM].reshape(KV_HEADS, sharers, own_rows, HEAD_DIM)
        return jnp.transpose(jnp.sum(parts, 1), (1, 0, 2)).reshape(own_rows, KV_HEADS * HEAD_DIM)

    query_plain = jnp.transpose(back[:, :, :own_width], (1, 0, 2)).reshape(own_rows, width)
    key_plain = collect(own_width)
    value_plain = collect(own_width + HEAD_DIM)
    first_gain_grad = (
        jnp.sum(query_plain * query_weight.astype(f32), 1)
        + jnp.sum(key_plain * key_weight.astype(f32), 1)
        + jnp.sum(value_plain * value_weight.astype(f32), 1)
    )
    attended_by_owner = jnp.transpose(
        attended_low.reshape(tokens, planes, ring, own_rows), (0, 2, 1, 3)
    ).reshape(tokens, width)
    output_term = dot_left_t(attended_by_owner, grad_branch_low).astype(bf16)
    output_plane = lax.psum_scatter(output_term, "fsdp", scatter_dimension=0, tiled=True)
    output_grad_weight = plane_scatter(output_plane.reshape(planes, own_rows, width))
    second_gain_all = lax.psum(lax.psum(second_gain_term, "fsdp"), "dp")
    mine = (lax.axis_index("dp") * ring + place) * own_rows
    second_gain_grad = lax.dynamic_slice_in_dim(second_gain_all, mine, own_rows)
    return (
        output[None],
        input_grad[None],
        first_gain_grad,
        query_plain * gain_mine,
        key_plain * gain_mine,
        value_plain * gain_mine,
        output_grad_weight,
        second_gain_grad,
        gate_up_grad[:, :ff_own],
        gate_up_grad[:, ff_own:],
        down_grad,
    )


TO_CORE = (7, 3, 5, 1)
TO_CHIPS = (6, 2, 4, 0)
VMEM = pl.BlockSpec(memory_space=pltpu.VMEM)
SMEM = pl.BlockSpec(memory_space=pltpu.SMEM)
log2_e = math.log2(math.e)


def turn(block, cosine, sine, forward):
    rolled = pltpu.roll(block, HEAD_DIM // 2, 1)
    return block * cosine + rolled * sine if forward else block * cosine - rolled * sine


def masked_scores(keys, queries, starts, low):
    scores = dot_right_t(keys, queries) * (score_scale * log2_e)
    key_pos = lax.broadcasted_iota(jnp.int32, scores.shape, 0)
    query_pos = lax.broadcasted_iota(jnp.int32, scores.shape, 1) + low
    return scores, (key_pos <= query_pos) & (key_pos >= starts)


anywhere = pl.BlockSpec(memory_space=pl.ANY)


def whole_of(array):
    return pl.BlockSpec(array.shape, lambda i: (0,) * len(array.shape))


def front_kernel(at_ref, normed_ref, *refs):
    first_ref, refs = refs[0], refs[1:]
    down_ref, held_ref, sem, refs = refs[-4], refs[-2], refs[-1], (*refs[:-4], refs[-3])
    devices, tokens = normed_ref.shape[:2]
    chunk = first_ref.shape[1] - tokens
    copies = [
        pltpu.make_async_copy(
            first_ref.at[device, pl.ds(tokens, chunk)],
            held_ref.at[pl.ds(device * chunk, chunk)],
            sem.at[device],
        )
        for device in range(devices)
    ]
    for copy in copies:
        copy.start()
    out = pltpu.make_async_copy(held_ref, down_ref, sem.at[devices])

    def midway():
        for copy in copies:
            copy.wait()
        out.start()

    front_body(midway, at_ref, normed_ref, *refs)
    out.wait()


def front_body(midway, at_ref, normed_ref, *refs):
    columns_refs, refs = refs[:2], refs[2:]
    cos_ref, sin_ref, starts_ref, refs = refs[0], refs[1], refs[2], refs[3:]
    q_ref, k_ref, v_ref, mixed_ref, norm_ref, project_ref, gain_ref, vt_ref = refs
    place = at_ref[0]
    devices, tokens = normed_ref.shape[:2]
    length = devices * tokens
    core = place & 1
    group = place >> 1
    rows = columns_refs[0].shape[2] - 16
    q_width = q_ref.shape[1]
    q_all = 2 * q_width
    for owner in range(4):
        for bit in range(4):
            for side in range(2):
                block = columns_refs[side]
                device = 2 * (group ^ bit) + (core ^ side)
                here = pl.ds(pl.multiple_of((owner * 8 + device) * rows, rows), rows)
                for which in range(2):

                    @pl.when(core == which)
                    def _():
                        project_ref[here, :q_width] = block[owner, bit, :rows, which * q_width : (which + 1) * q_width]

                project_ref[here, q_width:] = block[owner, bit, :rows, q_all:]
                gain_ref[owner * 8 + device] = block[owner, bit, rows:, :HEAD_DIM]

    for device in range(devices):
        here = slice(device * tokens, (device + 1) * tokens)
        raw = dot_plain(normed_ref[device], project_ref[...])
        cosine, sine = cos_ref[here, :], sin_ref[here, :]
        for low in range(0, q_width, HEAD_DIM):
            q_ref[here, low : low + HEAD_DIM] = turn(
                raw[:, low : low + HEAD_DIM], cosine, sine, True
            ).astype(bf16)
        k_ref[here, :] = turn(raw[:, q_width : q_width + HEAD_DIM], cosine, sine, True).astype(bf16)
        v_ref[here, :] = raw[:, q_width + HEAD_DIM :].astype(bf16)
    midway()
    vt_ref[...] = jnp.transpose(v_ref[...].astype(f32)).astype(bf16)
    block = 256
    for head in range(q_width // HEAD_DIM):
        cols = slice(head * HEAD_DIM, (head + 1) * HEAD_DIM)
        for low in range(0, length, block):
            high = low + block
            scores, allowed = masked_scores(
                k_ref[:high, :], q_ref[low:high, cols], starts_ref[:, low:high], low
            )
            scores = jnp.where(allowed, scores, mask_fill)
            top = jnp.max(scores, 0, keepdims=True)
            expo = jnp.exp2(scores - top)
            total = jnp.sum(expo, 0, keepdims=True)
            probs = (expo * (1.0 / total)).astype(bf16)
            mixed_ref[low:high, cols] = jnp.transpose(dot_plain(vt_ref[:, :high], probs)).astype(bf16)
            norm_ref[head, :, low:high] = top + jnp.log2(total)


def front(at, first, tokens, columns, columns_other, cosine, sine, starts):
    length = 8 * tokens
    q_width = (columns.shape[3] - 2 * HEAD_DIM) // 2
    cols = q_width + 2 * HEAD_DIM
    width = 32 * (columns.shape[2] - 16)
    shapes = [
        jax.ShapeDtypeStruct((length, q_width), bf16),
        jax.ShapeDtypeStruct((length, HEAD_DIM), bf16),
        jax.ShapeDtypeStruct((length, HEAD_DIM), bf16),
        jax.ShapeDtypeStruct((length, q_width), bf16),
        jax.ShapeDtypeStruct((q_width // HEAD_DIM, 1, length), f32),
        jax.ShapeDtypeStruct((width, cols), bf16),
        jax.ShapeDtypeStruct((32, 16, HEAD_DIM), bf16),
    ]
    return pl.pallas_call(
        front_kernel,
        grid=(1,),
        in_specs=[SMEM, pl.BlockSpec((8, tokens, width), lambda i: (0, 0, 0)), anywhere]
        + [whole_of(x) for x in (columns, columns_other, cosine, sine, starts)],
        out_specs=[whole_of(x) for x in shapes] + [anywhere],
        out_shape=shapes + [jax.ShapeDtypeStruct((8 * (first.shape[1] - tokens), width), bf16)],
        scratch_shapes=[
            pltpu.VMEM((HEAD_DIM, length), bf16),
            pltpu.VMEM((8 * (first.shape[1] - tokens), width), bf16),
            pltpu.SemaphoreType.DMA((9,)),
        ],
        compiler_params=pltpu.CompilerParams(vmem_limit_bytes=52 << 20),
        cost_estimate=pl.CostEstimate(
            flops=2 * length * width * cols + 4 * length * length * q_width,
            bytes_accessed=2 * length * width + 4 * width * cols,
            transcendentals=length * length,
        ),
        name="front",
    )(at, first, first, columns, columns_other, cosine, sine, starts)


def back_kernel(tokens, at_ref, q_ref, k_ref, v_ref, mixed_ref, norm_ref, packed_ref, project_ref,
                cos_ref, sin_ref, starts_ref, core_ref, chips_ref, cols_ref, kt_ref, dk_ref, dv_ref,
                grad_ref):
    place = at_ref[0]
    length, q_width = q_ref.shape
    for device in range(8):
        grad_ref[device * tokens : (device + 1) * tokens, :] = packed_ref[device, :tokens, :q_width]
    block = 256
    kt_ref[...] = jnp.transpose(k_ref[...].astype(f32)).astype(bf16)
    dk_ref[...] = jnp.zeros_like(dk_ref)
    dv_ref[...] = jnp.zeros_like(dv_ref)
    for head in range(q_width // HEAD_DIM):
        cols = slice(head * HEAD_DIM, (head + 1) * HEAD_DIM)
        for low in range(0, length, block):
            high = low + block
            queries, grads = q_ref[low:high, cols], grad_ref[low:high, cols]
            scores, allowed = masked_scores(k_ref[:high, :], queries, starts_ref[:, low:high], low)
            probs = jnp.where(allowed, jnp.exp2(scores - norm_ref[head, :, low:high]), 0.0)
            grad_prob = dot_right_t(v_ref[:high, :], grads)
            weighed = jnp.transpose(grads.astype(f32) * mixed_ref[low:high, cols].astype(f32))
            grad_score = (probs * (grad_prob - jnp.sum(weighed, 0, keepdims=True))).astype(bf16)
            dv_ref[:high, :] += dot_plain(probs.astype(bf16), grads)
            dk_ref[:high, :] += dot_plain(grad_score, queries)
            dq = jnp.transpose(dot_plain(kt_ref[:, :high], grad_score)) * score_scale
            cols_ref[low:high, cols] = turn(
                dq, cos_ref[low:high, :], sin_ref[low:high, :], False
            ).astype(bf16)
    cols_ref[:, q_width : q_width + HEAD_DIM] = turn(
        dk_ref[...] * score_scale, cos_ref[...], sin_ref[...], False
    ).astype(bf16)
    cols_ref[:, q_width + HEAD_DIM :] = dv_ref[...].astype(bf16)
    for out_ref, bits in ((core_ref, TO_CORE), (chips_ref, TO_CHIPS)):
        for step, bit in enumerate(bits):
            here = pl.ds(pl.multiple_of((place ^ bit) * tokens, tokens), tokens)
            out_ref[step] = dot_right_t(cols_ref[here, :], project_ref[...]).astype(bf16)


def back(at, queries, keys, values, mixed, norm, grads, project, cosine, sine, starts):
    length, q_width = queries.shape
    width, cols = project.shape
    tokens = length // 8
    return pl.pallas_call(
        functools.partial(back_kernel, tokens),
        in_specs=[SMEM] + [VMEM] * 10,
        out_specs=[VMEM] * 3,
        out_shape=[
            jax.ShapeDtypeStruct((4, tokens, width), bf16),
            jax.ShapeDtypeStruct((4, tokens, width), bf16),
            jax.ShapeDtypeStruct((length, cols), bf16),
        ],
        scratch_shapes=[
            pltpu.VMEM((HEAD_DIM, length), bf16),
            pltpu.VMEM((length, HEAD_DIM), f32),
            pltpu.VMEM((length, HEAD_DIM), f32),
            pltpu.VMEM((length, q_width), bf16),
        ],
        compiler_params=pltpu.CompilerParams(vmem_limit_bytes=52 << 20),
        cost_estimate=pl.CostEstimate(
            flops=600 * length * width * cols + 7 * length * length * q_width,
            bytes_accessed=2 * length * width + 2 * width * cols,
            transcendentals=length * length,
        ),
        name="back",
    )(at, queries, keys, values, mixed, norm, grads, project, cosine, sine, starts)


def project_grad_kernel(first_ref, cols_ref, out_ref):
    normed = first_ref[...].reshape(cols_ref.shape[0], first_ref.shape[2])
    out_ref[...] = jnp.transpose(dot_left_t(cols_ref[...], normed)).astype(bf16)


def project_grad(first, grad_cols):
    length, cols = grad_cols.shape
    width = first.shape[2]
    part = 512
    return pl.pallas_call(
        project_grad_kernel,
        grid=(width // part,),
        in_specs=[
            pl.BlockSpec((8, length // 8, part), lambda i: (0, 0, i)),
            pl.BlockSpec((length, cols), lambda i: (0, 0)),
        ],
        out_specs=pl.BlockSpec((part, cols), lambda i: (i, 0)),
        out_shape=jax.ShapeDtypeStruct((width, cols), bf16),
        compiler_params=pltpu.CompilerParams(vmem_limit_bytes=52 << 20),
        cost_estimate=pl.CostEstimate(
            flops=20 * length * width * cols, bytes_accessed=2 * length * width, transcendentals=0
        ),
        name="project_grad",
    )(first, grad_cols)


def output_grad_kernel(at_ref, packed_ref, attended_ref, out_ref):
    own = packed_ref.shape[2] // 2
    rows = out_ref.shape[1] - 16
    tokens = packed_ref.shape[1] - 16
    total = None
    gain = None
    for device in range(8):
        term = dot_left_t(
            packed_ref[device, :tokens, own:], attended_ref[device * tokens : (device + 1) * tokens, :]
        )
        extra = jnp.sum(packed_ref[device, tokens:, own:].astype(f32), 0, keepdims=True)
        total = term if total is None else total + term
        gain = extra if gain is None else gain + extra
    turned = jnp.transpose(total).astype(bf16)
    first = lax.broadcasted_iota(jnp.int32, (16, own), 0) == 0
    gain_rows = jnp.where(first, jnp.broadcast_to(gain, (16, own)), 0.0)
    for owner in range(4):
        out_ref[owner, :rows, :] = turned[owner * rows : (owner + 1) * rows, :]
        here = jnp.where(at_ref[0] // 2 == owner, 1.0, 0.0)
        out_ref[owner, rows:, :] = (gain_rows * here).astype(bf16)


def output_grad_term(at, packed, attended):
    length, width = attended.shape
    own = packed.shape[2] // 2
    return pl.pallas_call(
        output_grad_kernel,
        in_specs=[SMEM] + [VMEM] * 2,
        out_specs=VMEM,
        out_shape=jax.ShapeDtypeStruct((4, width // 4 + 16, own), bf16),
        compiler_params=pltpu.CompilerParams(vmem_limit_bytes=52 << 20),
        cost_estimate=pl.CostEstimate(
            flops=60 * length * own * width, bytes_accessed=2 * length * width, transcendentals=0
        ),
        name="output_grad_term",
    )(at, packed, attended)


def place_blocks(plane, blocks, out_ref):
    tokens = blocks[0].shape[0]
    for block, move in zip(blocks, LINE):
        owner = plane + move if move != 3 else 3 - plane
        valid = (owner >= 0) & (owner <= 3) if move != 3 else (plane == 0) | (plane == 3)

        @pl.when(valid)
        def _():
            out_ref[pl.ds(pl.multiple_of(owner * tokens, tokens), tokens), :] = block[...]


def feed_kernel(units, count, n_count, at_ref, *refs):
    d_refs, n_refs, refs = refs[:6], refs[6 : 6 + n_count], refs[6 + n_count :]
    both_ref, down_ref, rows_ref, refs = *refs[:3], refs[3 + count :]
    second_ref, direct_ref, hidden_ref, grads_ref, term_ref, held_ref = refs
    step = pl.program_id(0)

    @pl.when(step == 0)
    def _():
        place_blocks(at_ref[1], d_refs, direct_ref)
        if n_count == 6:
            place_blocks(at_ref[1], n_refs, second_ref)
        else:
            second_ref[...] = n_refs[0][...].reshape(second_ref.shape)

    @pl.when(step < units)
    def _():
        raw = dot_plain(second_ref[...], both_ref[...])
        half = raw.shape[1] // 2
        gate, upward = raw[:, :half], raw[:, half:]
        sig = 1.0 / (1.0 + jnp.exp(-gate))
        silu = gate * sig
        hidden_ref[...] = (silu * upward).astype(bf16)
        grad_hidden = dot_right_t(direct_ref[...], down_ref[...])
        grad_gate = (grad_hidden * upward * sig * (1.0 + gate * (1.0 - sig))).astype(bf16)
        grads = jnp.concatenate([grad_gate, (grad_hidden * silu).astype(bf16)], 1)
        grads_ref[...] = grads
        held_ref[step] = grads

    @pl.when(step >= units)
    def _():
        total = None
        for unit in range(units):
            cols = slice(unit * held_ref.shape[2], (unit + 1) * held_ref.shape[2])
            part = dot_right_t(held_ref[unit], rows_ref[:, cols])
            total = part if total is None else total + part
        term_ref[...] = total.astype(bf16).reshape(term_ref.shape)


def feed(at, part_at, parts_of, seconds, directs, both, down, so_far):
    tokens, width = seconds[0].shape[-2:]
    some = 4 * tokens
    ff = down.shape[0]
    n_count = len(seconds)
    gathered = pl.BlockSpec((4, tokens, width), lambda i: (0, 0, 0))
    single = pl.BlockSpec((tokens, width), lambda i: (0, 0))
    unit, part = 128, 256
    units, parts = ff // unit, width // part
    so_far = so_far or []
    total = parts_of * some
    outs = pl.pallas_call(
        functools.partial(feed_kernel, units, len(so_far), n_count),
        grid=(units + parts,),
        in_specs=[
            SMEM,
            *[pl.BlockSpec((tokens, width), lambda i: (part_at, 0))] * 6,
            *[single if n_count == 6 else gathered] * n_count,
            pl.BlockSpec((width, 2 * unit), lambda i: (0, jnp.minimum(i, units - 1))),
            pl.BlockSpec((unit, width), lambda i: (jnp.minimum(i, units - 1), 0)),
            pl.BlockSpec((part, 2 * ff), lambda i: (jnp.maximum(i - units, 0), 0)),
        ]
        + [pl.BlockSpec(memory_space=pl.ANY)] * len(so_far),
        out_specs=[
            pl.BlockSpec((some, width), lambda i: (part_at, 0)),
            pl.BlockSpec((some, width), lambda i: (part_at, 0)),
            pl.BlockSpec((some, unit), lambda i: (part_at, jnp.minimum(i, units - 1))),
            pl.BlockSpec((some, 2 * unit), lambda i: (part_at, jnp.minimum(i, units - 1))),
            pl.BlockSpec((4, tokens, part), lambda i: (0, 0, jnp.maximum(i - units, 0))),
        ],
        out_shape=[
            jax.ShapeDtypeStruct((total, width), bf16),
            jax.ShapeDtypeStruct((total, width), bf16),
            jax.ShapeDtypeStruct((total, ff), bf16),
            jax.ShapeDtypeStruct((total, 2 * ff), bf16),
            jax.ShapeDtypeStruct((4, tokens, width), bf16),
        ],
        scratch_shapes=[pltpu.VMEM((units, some, 2 * unit), bf16)],
        input_output_aliases={10 + n_count + i: i for i in range(len(so_far))},
        compiler_params=pltpu.CompilerParams(vmem_limit_bytes=52 << 20),
        cost_estimate=pl.CostEstimate(
            flops=10 * some * width * ff,
            bytes_accessed=10 * width * ff,
            transcendentals=some * ff,
        ),
        name="feed",
    )(at, *directs, *seconds, both, down, both, *so_far)
    return outs[:4], outs[4]


def branch_kernel(hidden_ref, down_ref, out_ref):
    out_ref[...] = dot_plain(hidden_ref[...], down_ref[...]).astype(bf16).reshape(out_ref.shape)


def branch(hidden, down, parts):
    rows, ff = hidden.shape
    width = down.shape[1]
    tokens = rows // (4 * parts)
    return pl.pallas_call(
        branch_kernel,
        grid=(parts, 4),
        in_specs=[
            pl.BlockSpec((4 * tokens, ff), lambda h, i: (h, 0)),
            pl.BlockSpec((ff, width // 4), lambda h, i: (0, i)),
        ],
        out_specs=pl.BlockSpec((4, tokens, width // 4), lambda h, i: (0, h, i)),
        out_shape=jax.ShapeDtypeStruct((4, parts * tokens, width), bf16),
        compiler_params=pltpu.CompilerParams(vmem_limit_bytes=52 << 20),
        cost_estimate=pl.CostEstimate(flops=1 << 20, bytes_accessed=1 << 16, transcendentals=0),
        name="branch",
    )(hidden, down)


def split_kernel(both_ref, gate_ref, up_ref):
    for low in range(0, gate_ref.shape[1], 128):
        gate_ref[:, low : low + 128] = both_ref[:, 2 * low : 2 * low + 128].astype(f32)
        up_ref[:, low : low + 128] = both_ref[:, 2 * low + 128 : 2 * low + 256].astype(f32)


def split(both):
    rows, cols = both.shape
    out = jax.ShapeDtypeStruct((rows, cols // 2), f32)
    part = pl.BlockSpec((64, cols // 2), lambda i: (i, 0))
    return pl.pallas_call(
        split_kernel,
        grid=(rows // 64,),
        in_specs=[pl.BlockSpec((64, cols), lambda i: (i, 0))],
        out_specs=[part, part],
        out_shape=[out, out],
        name="split",
    )(both)


def fast_device(
    layer_input,
    output_grad,
    layer_keep,
    group_ids,
    exit_scale,
    doc_lengths,
    attention_gain,
    query_weight,
    key_weight,
    value_weight,
    output_weight,
    feedforward_gain,
    gate_weight,
    up_weight,
    down_weight,
):
    tokens, width = layer_input.shape[1:]
    place, plane = lax.axis_index("fsdp"), lax.axis_index("dp")
    at = jnp.stack([place, plane]).astype(jnp.int32)
    length = tokens * 8
    own_rows = query_weight.shape[0]
    q_width = HEADS // 8 * HEAD_DIM
    cols = q_width + 2 * HEAD_DIM
    ff_own = gate_weight.shape[1]
    half = tokens // 2
    rows = layer_input[0].astype(f32)
    keep = layer_keep[0].astype(f32)

    both_mine = jnp.stack(
        [gate_weight.reshape(-1, ff_own // 128, 128), up_weight.reshape(-1, ff_own // 128, 128)], 2
    ).reshape(-1, 2 * ff_own)
    inv_first = rms_scale(rows)
    normed = (rows * inv_first).astype(bf16)
    first = lax.all_gather(jnp.concatenate([normed, down_weight], 0), "fsdp", axis=0, tiled=False)
    gain_mine = attention_gain.astype(f32)[:, None]

    def by_chip(weight):
        scaled = (weight.astype(f32) * gain_mine).astype(bf16)
        return scaled.reshape(own_rows, 4, weight.shape[1] // 4)

    sent = jnp.concatenate([by_chip(query_weight), by_chip(key_weight), by_chip(value_weight)], -1)
    sent = jnp.transpose(sent, (1, 0, 2))
    wide = sent.shape[2]
    gain_rows = jnp.pad(feedforward_gain[None, :], ((0, 15), (0, wide - own_rows)))
    group = place // 2

    def to_chip(bit):
        block = lax.dynamic_index_in_dim(sent, group ^ bit, 0, keepdims=False)
        return jnp.concatenate([block, gain_rows], 0)

    picked = jnp.sum(
        jnp.where(jnp.arange(exit_scale.shape[0], dtype=jnp.int32) == group_ids[0], exit_scale, 0.0)
    )
    cotangent = output_grad[0].astype(f32) * picked
    direct = keep * cotangent
    direct_low = direct.astype(bf16)
    direct_near = line_first(direct_low)
    columns = jnp.stack([to_chip(0)] + [flip(to_chip(bit), 2 * bit) for bit in (1, 2, 3)])
    output_plane = gather_planes(after(output_weight, columns, *direct_near))
    columns = gather_planes(after(columns, output_plane))
    columns_other = flip(columns, 1)
    output_full = lax.all_gather(output_plane, "fsdp", axis=1, tiled=True).reshape(width, width)
    both = lax.all_gather(after(both_mine, columns), "fsdp", axis=0, tiled=True)
    half_dim = HEAD_DIM // 2
    cosine, sine = rotary_tables(length)
    cosine, sine = cosine[:, 0], sine[:, 0]
    cosine = jnp.concatenate([cosine, cosine], 1)
    sine = jnp.concatenate([-sine, sine], 1)
    order = jnp.arange(doc_lengths.shape[1])
    ends = jnp.sum(jnp.where(order[None, :] <= order[:, None], doc_lengths[0][None, :], 0), 1)
    positions = jnp.arange(length, dtype=jnp.int32)
    starts = jnp.max(jnp.where(positions[None, :] >= ends[:, None], ends[:, None], 0), 0)[None, :]

    direct_second = line_second(*after_all(direct_near, columns))
    queries, keys, values, mixed, norm, project, gains, down_use = front(
        at, first, tokens, columns, columns_other, cosine, sine, starts
    )
    gain_second = gains[:, 0, :own_rows].reshape(width).astype(f32)

    attended_low = lax.all_to_all(mixed, "fsdp", split_axis=0, concat_axis=1, tiled=True)
    attended_low = after(attended_low, *direct_second)
    branch_attention = dot_plain(attended_low, output_full)
    middle = rows + branch_attention
    inv_second = rms_scale(middle)
    directs = [direct_low, *direct_near, *direct_second]
    second_mine = (middle * inv_second * gain_second).astype(bf16)
    second_half = second_mine[:half]
    second_near = line_first(second_half)
    seconds_low = [second_half, *second_near, *line_second(*second_near)]
    attended_all = lax.all_gather(after(attended_low, *seconds_low), "fsdp", axis=0, tiled=True)
    seconds_high = gather_planes(after(second_mine[half:], *seconds_low))

    stacked, terms_low = feed(at, 0, 2, seconds_low, directs, both, down_use, None)
    stacked, terms_high = feed(at, 1, 2, [seconds_high], directs, both, down_use, stacked)
    second_all, direct_all, hidden_all, grads_all = stacked
    got_low = swap_planes(terms_low)

    branch_terms = branch(hidden_all, down_use, 2)
    down_term = dot_left_t(hidden_all, direct_all).astype(bf16)
    got_high = swap_planes(after(terms_high, got_low))
    grad_second = jnp.concatenate(
        [jnp.sum(after(got_low, got_high).astype(f32), 0), jnp.sum(got_high.astype(f32), 0)], 0
    )
    both_term = dot_left_t(second_all, grads_all).astype(bf16)
    down_grad = lax.psum_scatter(down_term, "fsdp", scatter_dimension=0, tiled=True).astype(f32)
    both_grad = lax.psum_scatter(both_term, "fsdp", scatter_dimension=0, tiled=True)

    weighted = grad_second * gain_second
    grad_middle = inv_second * weighted - middle * inv_second**3 * jnp.mean(
        weighted * middle, -1, keepdims=True
    )
    grad_branch = (direct + grad_middle).astype(bf16)
    grad_attended = dot_right_t(grad_branch, output_full).astype(bf16)
    gain_term = jnp.sum(grad_second * middle * inv_second, 0, keepdims=True)
    gain_high = gain_term.astype(bf16)
    gain_low = (gain_term - gain_high.astype(f32)).astype(bf16)
    gain_rows = jnp.concatenate([gain_high, gain_low, jnp.zeros((14, width), bf16)], 0)
    packed = jnp.concatenate(
        [
            jnp.concatenate([grad_attended, jnp.zeros((16, width), bf16)], 0).reshape(-1, 8, q_width),
            jnp.concatenate([grad_branch, gain_rows], 0).reshape(-1, 8, q_width),
        ],
        2,
    )
    packed = lax.all_to_all(jnp.transpose(packed, (1, 0, 2)), "fsdp", split_axis=0, concat_axis=0)
    def ahead(step):
        return lax.dynamic_index_in_dim(branch_terms, jnp.clip(step, 0, 3), 0, keepdims=False)

    branch_up2 = lax.ppermute(after(ahead(plane + 2), grad_branch), "dp", UP[:2])
    branch_down2 = lax.ppermute(after(ahead(plane - 2), grad_branch), "dp", DOWN[1:])
    branch_far = lax.ppermute(after(ahead(3 - plane), grad_branch), "dp", [(3, 1), (0, 2)])
    zero = jnp.zeros((), bf16)
    sent_up = (
        ahead(plane + 1).astype(f32)
        + branch_up2.astype(f32)
        + jnp.where(plane == 2, branch_far, zero).astype(f32)
    ).astype(bf16)
    sent_down = (
        ahead(plane - 1).astype(f32)
        + branch_down2.astype(f32)
        + jnp.where(plane == 1, branch_far, zero).astype(f32)
    ).astype(bf16)
    packed = after(packed, sent_up, sent_down)
    branch_up1 = lax.ppermute(sent_up, "dp", UP)
    branch_down1 = lax.ppermute(sent_down, "dp", DOWN)
    output_term = output_grad_term(at, packed, attended_all)
    output_got = swap_planes(output_term)
    packed = after(packed, output_term)
    core_terms, chip_terms, grad_cols = back(
        at, queries, keys, values, mixed, norm, packed, project, cosine, sine, starts
    )
    other = flip(core_terms, 1)
    project_term = project_grad(first, after(grad_cols, branch_up1, branch_down1))
    other = after(other, project_term)
    sums = [add_low(chip_terms[i], other[i]) for i in range(3)]
    far, near_x, near_y = flip(sums[0], 6), flip(sums[1], 2), flip(sums[2], 4)
    core = place % 2
    keys_term, values_term = project_term[:, q_width : q_width + HEAD_DIM], project_term[:, q_width + HEAD_DIM :]
    kept = jnp.where(core == 0, keys_term, values_term)
    kept = add_low(kept, flip(jnp.where(core == 0, values_term, keys_term), 1))
    project_term = jnp.concatenate([project_term[:, :q_width], kept], 1)
    kept_cols = q_width + HEAD_DIM
    project_got = swap_planes(after(project_term.reshape(4, width // 4, kept_cols), output_got))
    branch_feed = ahead(plane).astype(f32) + branch_up1.astype(f32) + branch_down1.astype(f32)
    project_plane = jnp.sum(project_got.astype(f32), 0).astype(bf16)
    output_plane_sum = jnp.sum(output_got.astype(f32), 0).astype(bf16)
    both_plane = jnp.concatenate([project_plane, output_plane_sum[: 8 * own_rows]], 1)
    gain_four = output_plane_sum[8 * own_rows].reshape(4, own_rows)
    low_half = place % 2 == 0
    gain_eight = jnp.concatenate(
        [jnp.where(low_half, gain_four, 0), jnp.where(low_half, 0, gain_four)], 0
    )
    gain_eight = jnp.pad(gain_eight[:, None, :], ((0, 0), (0, 15), (0, kept_cols + q_width - own_rows)))
    final = jnp.concatenate([both_plane.reshape(8, own_rows, kept_cols + q_width), gain_eight], 1)
    weighted_first = (
        chip_terms[3].astype(f32)
        + other[3].astype(f32)
        + far.astype(f32)
        + near_x.astype(f32)
        + near_y.astype(f32)
    )
    grad_rows = inv_first * weighted_first - rows * inv_first**3 * jnp.mean(
        weighted_first * rows, -1, keepdims=True
    )
    input_grad = cotangent + grad_middle + grad_rows

    output = (rows + keep * (branch_attention + branch_feed)).astype(bf16)

    gate_grad, up_grad = split(both_grad)
    final = lax.all_to_all(after(final, input_grad), "fsdp", split_axis=0, concat_axis=0)
    final = after(final, gate_grad)
    back_cols = final[:, :own_rows].astype(f32)
    output_sum = jnp.transpose(back_cols[:, :, kept_cols:], (1, 0, 2)).reshape(own_rows, width)
    second_gain_grad = jnp.sum(final[:, own_rows, :own_rows].astype(f32), 0)

    def collect(side):
        parts = back_cols[side::2, :, q_width:kept_cols]
        return jnp.transpose(parts, (1, 0, 2)).reshape(own_rows, KV_HEADS * HEAD_DIM)

    query_plain = jnp.transpose(back_cols[:, :, :q_width], (1, 0, 2)).reshape(own_rows, width)
    key_plain = collect(0)
    value_plain = collect(1)
    first_gain_grad = (
        jnp.sum(query_plain * query_weight.astype(f32), 1)
        + jnp.sum(key_plain * key_weight.astype(f32), 1)
        + jnp.sum(value_plain * value_weight.astype(f32), 1)
    )
    return (
        output[None],
        input_grad[None],
        first_gain_grad,
        query_plain * gain_mine,
        key_plain * gain_mine,
        value_plain * gain_mine,
        output_sum,
        second_gain_grad,
        gate_grad,
        up_grad,
        down_grad,
    )


def solution(mesh):
    both = ("dp", "fsdp")
    fast = (mesh.shape["dp"], mesh.shape["fsdp"]) == (4, 8)
    return jax.shard_map(
        fast_device if fast else per_device,
        mesh=mesh,
        in_specs=(
            P("dp", "fsdp", None),
            P("dp", "fsdp", None),
            P("dp"),
            P("dp"),
            P(),
            P("dp", None),
            P(both),
            P(both, None),
            P(both, None),
            P(both, None),
            P(both, None),
            P(both),
            P("fsdp", "dp"),
            P("fsdp", "dp"),
            P(both, None),
        ),
        out_specs=(
            P("dp", "fsdp", None),
            P("dp", "fsdp", None),
            P(both),
            P(both, None),
            P(both, None),
            P(both, None),
            P(both, None),
            P(both),
            P("fsdp", "dp"),
            P("fsdp", "dp"),
            P(both, None),
        ),
        check_vma=False,
    )
```

```python
import functools
import math

import jax
import jax.numpy as jnp
import numpy as np
from jax import lax
from jax.experimental import pallas as pl
from jax.experimental.pallas import tpu as pltpu
from jax.sharding import PartitionSpec as P

HEADS = 16
KV_HEADS = 4
HEAD_DIM = 128

norm_eps = 1e-05
rope_base = 10000.0
mask_fill = -1e30
score_scale = 1.0 / math.sqrt(HEAD_DIM)
f32 = jnp.float32
bf16 = jnp.bfloat16


def dot_plain(left, right):
    return jnp.dot(left, right, preferred_element_type=f32)


def dot_right_t(left, right):
    return lax.dot_general(left, right, (((1,), (1,)), ((), ())), preferred_element_type=f32)


def dot_left_t(left, right):
    return lax.dot_general(left, right, (((0,), (0,)), ((), ())), preferred_element_type=f32)


def rotary_tables(length):
    half_dim = HEAD_DIM // 2
    frequency = rope_base ** (-(2.0 * jnp.arange(half_dim, dtype=f32)) / HEAD_DIM)
    angles = jnp.arange(length, dtype=jnp.int32).astype(f32)[:, None] * frequency[None, :]
    return (jnp.cos(angles)[:, None, :], jnp.sin(angles)[:, None, :])


def rotate(vectors, cosine, sine_part):
    half_dim = vectors.shape[-1] // 2
    lower_half = vectors[..., :half_dim]
    upper_half = vectors[..., half_dim:]
    return jnp.concatenate(
        [
            lower_half * cosine - upper_half * sine_part,
            upper_half * cosine + lower_half * sine_part,
        ],
        -1,
    )


def rms_scale(rows):
    return lax.rsqrt(jnp.mean(rows * rows, -1, keepdims=True) + norm_eps)


def after_all(values, *earlier):
    return lax.optimization_barrier((*values, *earlier))[: len(values)]


def after(value, *earlier):
    return lax.optimization_barrier((value, *earlier))[0]


def plane_gather(block):
    whole = lax.all_gather(block, "dp", axis=0)
    return [whole[i] for i in range(whole.shape[0])]


def add_low(left, right):
    return (left.astype(f32) + right.astype(f32)).astype(left.dtype)


def plane_scatter(whole):
    return lax.psum_scatter(whole, "dp", scatter_dimension=0, tiled=False).astype(f32)


FLIP = {bit: [(i, i ^ bit) for i in range(8)] for bit in (1, 2, 4, 6)}


def flip(block, bit):
    return lax.ppermute(block, "fsdp", FLIP[bit])


def shift(block, step):
    return lax.ppermute(block, "dp", [(i, (i + step) % 4) for i in range(4)])


UP = [(0, 1), (1, 2), (2, 3)]
DOWN = [(1, 0), (2, 1), (3, 2)]
LINE = (0, -1, 1, -2, 2, 3)


def line_first(block):
    return lax.ppermute(block, "dp", UP), lax.ppermute(block, "dp", DOWN)


def line_second(up, down):
    plane = lax.axis_index("dp")
    far = jnp.where(plane == 2, down, up)
    return (
        lax.ppermute(up, "dp", UP[1:]),
        lax.ppermute(down, "dp", DOWN[:2]),
        lax.ppermute(far, "dp", [(2, 0), (1, 3)]),
    )


def gather_planes(block):
    copies = jnp.broadcast_to(block[None], (4, *block.shape))
    return lax.all_to_all(copies, "dp", split_axis=0, concat_axis=0)


def swap_planes(whole):
    return lax.all_to_all(whole, "dp", split_axis=0, concat_axis=0)


def block_rows_of(length):
    return math.gcd(length, 256)


def transposed_scores(keys, queries, starts, low, high, width):
    scores = dot_right_t(keys, queries) * score_scale
    key_pos = lax.broadcasted_iota(jnp.int32, (width, high - low), 0)
    query_pos = lax.broadcasted_iota(jnp.int32, (width, high - low), 1) + low
    allowed = (key_pos <= query_pos) & (key_pos >= starts)
    return scores, allowed


def attend_kernel(rows_of, q_ref, k_ref, vt_ref, starts_ref, out_ref, norm_ref):
    length = q_ref.shape[0]
    for low in range(0, length, rows_of):
        high = low + rows_of
        starts = starts_ref[:, low:high]
        scores, allowed = transposed_scores(
            k_ref[:high, :], q_ref[low:high, :], starts, low, high, high
        )
        scores = jnp.where(allowed, scores, mask_fill)
        top = jnp.max(scores, 0, keepdims=True)
        expo = jnp.exp(scores - top)
        total = jnp.sum(expo, 0, keepdims=True)
        probs = (expo * (1.0 / total)).astype(bf16)
        mixed = dot_plain(vt_ref[:, :high], probs)
        out_ref[low:high, :] = jnp.transpose(mixed).astype(out_ref.dtype)
        norm_ref[0, :, low:high] = top + jnp.log(total)


def attend(queries, keys, values, starts):
    length, width = queries.shape
    heads = width // HEAD_DIM
    return pl.pallas_call(
        functools.partial(attend_kernel, block_rows_of(length)),
        grid=(heads,),
        in_specs=[
            pl.BlockSpec((length, HEAD_DIM), lambda h: (0, h)),
            pl.BlockSpec((length, HEAD_DIM), lambda h: (0, 0)),
            pl.BlockSpec((HEAD_DIM, length), lambda h: (0, 0)),
            pl.BlockSpec((1, length), lambda h: (0, 0)),
        ],
        out_specs=[
            pl.BlockSpec((length, HEAD_DIM), lambda h: (0, h)),
            pl.BlockSpec((1, 1, length), lambda h: (h, 0, 0)),
        ],
        out_shape=[
            jax.ShapeDtypeStruct((length, width), bf16),
            jax.ShapeDtypeStruct((heads, 1, length), f32),
        ],
        compiler_params=pltpu.CompilerParams(vmem_limit_bytes=48 << 20),
        cost_estimate=pl.CostEstimate(
            flops=3 * heads * length * length * HEAD_DIM,
            bytes_accessed=8 * length * width,
            transcendentals=heads * length * length,
        ),
        name="attend",
    )(queries, keys, jnp.transpose(values), starts)


def attend_back_kernel(
    rows_of, q_ref, k_ref, kt_ref, v_ref, starts_ref, norm_ref, out_ref, grad_ref, dq_ref, dk_ref, dv_ref
):
    length = q_ref.shape[0]

    @pl.when(pl.program_id(0) == 0)
    def _():
        dk_ref[...] = jnp.zeros_like(dk_ref)
        dv_ref[...] = jnp.zeros_like(dv_ref)

    for low in range(0, length, rows_of):
        high = low + rows_of
        starts = starts_ref[:, low:high]
        queries = q_ref[low:high, :]
        grads = grad_ref[low:high, :]
        scores, allowed = transposed_scores(k_ref[:high, :], queries, starts, low, high, high)
        probs = jnp.where(allowed, jnp.exp(scores - norm_ref[0, :, low:high]), 0.0)
        grad_prob = dot_right_t(v_ref[:high, :], grads)
        weighed = jnp.transpose(grads.astype(f32) * out_ref[low:high, :].astype(f32))
        delta = jnp.sum(weighed, 0, keepdims=True)
        grad_score = (probs * (grad_prob - delta)).astype(bf16)
        dv_ref[:high, :] += dot_plain(probs.astype(bf16), grads)
        dk_ref[:high, :] += dot_plain(grad_score, queries)
        dq_ref[low:high, :] = jnp.transpose(dot_plain(kt_ref[:, :high], grad_score))


def attend_back(queries, keys, values, starts, norm, out, grads):
    length, width = queries.shape
    heads = width // HEAD_DIM
    by_head = pl.BlockSpec((length, HEAD_DIM), lambda h: (0, h))
    shared = pl.BlockSpec((length, HEAD_DIM), lambda h: (0, 0))
    return pl.pallas_call(
        functools.partial(attend_back_kernel, block_rows_of(length)),
        grid=(heads,),
        in_specs=[
            by_head,
            shared,
            pl.BlockSpec((HEAD_DIM, length), lambda h: (0, 0)),
            shared,
            pl.BlockSpec((1, length), lambda h: (0, 0)),
            pl.BlockSpec((1, 1, length), lambda h: (h, 0, 0)),
            by_head,
            by_head,
        ],
        out_specs=[by_head, shared, shared],
        out_shape=[
            jax.ShapeDtypeStruct((length, width), f32),
            jax.ShapeDtypeStruct((length, HEAD_DIM), f32),
            jax.ShapeDtypeStruct((length, HEAD_DIM), f32),
        ],
        compiler_params=pltpu.CompilerParams(vmem_limit_bytes=56 << 20),
        cost_estimate=pl.CostEstimate(
            flops=7 * heads * length * length * HEAD_DIM,
            bytes_accessed=16 * length * width,
            transcendentals=heads * length * length,
        ),
        name="attend_back",
    )(queries, keys, jnp.transpose(keys), values, starts, norm, out, grads)


def per_device(
    layer_input,
    output_grad,
    layer_keep,
    group_ids,
    exit_scale,
    doc_lengths,
    attention_gain,
    query_weight,
    key_weight,
    value_weight,
    output_weight,
    feedforward_gain,
    gate_weight,
    up_weight,
    down_weight,
):
    tokens, width = layer_input.shape[1:]
    ring = lax.axis_size("fsdp")
    planes = lax.axis_size("dp")
    place = lax.axis_index("fsdp")
    length = tokens * ring
    own_rows = query_weight.shape[0]
    heads = HEADS // ring
    own_width = heads * HEAD_DIM
    ff_own = gate_weight.shape[1]
    rows = layer_input[0].astype(f32)
    keep = layer_keep[0].astype(f32)

    inv_first = rms_scale(rows)
    normed = lax.all_gather((rows * inv_first).astype(bf16), "fsdp", axis=0, tiled=True)

    gain_mine = attention_gain.astype(f32)[:, None]
    sharers = ring // KV_HEADS
    cols = own_width + 2 * HEAD_DIM

    def spread(weight):
        heads_of = (weight.astype(f32) * gain_mine).astype(bf16).reshape(own_rows, KV_HEADS, 1, HEAD_DIM)
        return jnp.broadcast_to(heads_of, (own_rows, KV_HEADS, sharers, HEAD_DIM)).reshape(
            own_rows, ring, HEAD_DIM
        )

    query_scaled = (query_weight.astype(f32) * gain_mine).astype(bf16).reshape(own_rows, ring, own_width)
    sent = jnp.concatenate([query_scaled, spread(key_weight), spread(value_weight)], -1)
    sent = jnp.transpose(sent, (1, 0, 2)).reshape(ring * own_rows, cols)
    plane_cols = lax.all_to_all(sent, "fsdp", split_axis=0, concat_axis=0, tiled=True)
    project = jnp.concatenate(plane_gather(plane_cols), 0)

    picked = jnp.sum(
        jnp.where(jnp.arange(exit_scale.shape[0], dtype=jnp.int32) == group_ids[0], exit_scale, 0.0)
    )
    cotangent = output_grad[0].astype(f32) * picked
    direct = keep * cotangent
    direct_all = jnp.concatenate(plane_gather(direct.astype(bf16)), 0)

    gain_second = lax.all_gather(
        lax.all_gather(feedforward_gain, "fsdp", axis=0, tiled=False), "dp", axis=0, tiled=False
    ).reshape(width).astype(f32)

    output_full = lax.all_gather(output_weight, ("dp", "fsdp"), axis=0, tiled=True)
    gate_up = jnp.concatenate([gate_weight, up_weight], 1)
    gate_up = lax.all_gather(gate_up, "fsdp", axis=0, tiled=True)
    down_use = lax.all_gather(down_weight, "fsdp", axis=0, tiled=True)

    cosine, sine_part = rotary_tables(length)
    ends = jnp.sum(
        jnp.where(
            jnp.arange(doc_lengths.shape[1])[None, :] <= jnp.arange(doc_lengths.shape[1])[:, None],
            doc_lengths[0][None, :],
            0,
        ),
        1,
    )
    positions = jnp.arange(length, dtype=jnp.int32)
    starts = jnp.max(jnp.where(positions[None, :] >= ends[:, None], ends[:, None], 0), 0)[None, :]
    raw = dot_plain(normed, project)
    rotated = rotate(
        raw[:, : own_width + HEAD_DIM].reshape(length, heads + 1, HEAD_DIM), cosine, sine_part
    ).astype(bf16)
    queries = rotated[:, :heads].reshape(length, own_width)
    keys = rotated[:, heads]
    values = raw[:, own_width + HEAD_DIM :].astype(bf16)
    mixed, norm = attend(queries, keys, values, starts)
    attended_low = lax.all_to_all(mixed, "fsdp", split_axis=0, concat_axis=1, tiled=True)
    branch_attention = dot_plain(attended_low, output_full)
    middle = rows + branch_attention
    inv_second = rms_scale(middle)
    second_mine = (middle * inv_second * gain_second).astype(bf16)

    second_all = jnp.concatenate(plane_gather(second_mine), 0)
    gate_use, up_use = gate_up[:, :ff_own], gate_up[:, ff_own:]
    gate_pre = dot_plain(second_all, gate_use)
    upward = dot_plain(second_all, up_use)
    sigmoid_gate = 1.0 / (1.0 + jnp.exp(-gate_pre))
    silu_gate = gate_pre * sigmoid_gate
    hidden_low = (silu_gate * upward).astype(bf16)
    grad_hidden = dot_right_t(direct_all, down_use)
    grad_gate_low = (
        grad_hidden * upward * sigmoid_gate * (1.0 + gate_pre * (1.0 - sigmoid_gate))
    ).astype(bf16)
    grad_up_low = (grad_hidden * silu_gate).astype(bf16)
    grad_both = jnp.concatenate([grad_gate_low, grad_up_low], 1)
    second_terms = dot_right_t(grad_both, gate_up).astype(bf16).reshape(planes, tokens, width)
    grad_second = plane_scatter(second_terms)

    down_term = dot_left_t(hidden_low, direct_all).astype(bf16)
    gate_up_term = dot_left_t(second_all, grad_both).astype(bf16)
    down_grad = lax.psum_scatter(down_term, "fsdp", scatter_dimension=0, tiled=True).astype(f32)
    gate_up_grad = lax.psum_scatter(
        after(gate_up_term, down_term), "fsdp", scatter_dimension=0, tiled=True
    ).astype(f32)
    branch_terms = dot_plain(hidden_low, down_use).astype(bf16).reshape(planes, tokens, width)
    branch_terms = after(branch_terms, grad_second)
    branch_feed = plane_scatter(branch_terms)
    output = (rows + keep * (branch_attention + branch_feed)).astype(bf16)

    second_gain_term = jnp.sum(grad_second * middle * inv_second, 0)
    weighted = grad_second * gain_second
    grad_middle = inv_second * weighted - middle * inv_second**3 * jnp.mean(
        weighted * middle, -1, keepdims=True
    )
    grad_branch_low = (direct + grad_middle).astype(bf16)
    grad_attended_low = dot_right_t(grad_branch_low, output_full).astype(bf16)
    grad_heads = lax.all_to_all(grad_attended_low, "fsdp", split_axis=1, concat_axis=0, tiled=True)
    dq, dk, dv = attend_back(queries, keys, values, starts, norm, mixed, grad_heads)
    turned = rotate(
        (jnp.concatenate([dq, dk], 1) * score_scale).reshape(length, heads + 1, HEAD_DIM),
        cosine,
        -sine_part,
    ).astype(bf16)
    grad_cols = jnp.concatenate([turned.reshape(length, own_width + HEAD_DIM), dv.astype(bf16)], 1)
    normed_terms = dot_right_t(grad_cols, project).astype(bf16)
    weighted_first = lax.psum_scatter(normed_terms, "fsdp", scatter_dimension=0, tiled=True).astype(f32)
    grad_rows = inv_first * weighted_first - rows * inv_first**3 * jnp.mean(
        weighted_first * rows, -1, keepdims=True
    )
    input_grad = cotangent + grad_middle + grad_rows

    project_term = dot_left_t(normed, grad_cols).astype(bf16).reshape(planes, ring * own_rows, cols)
    project_plane = plane_scatter(project_term).astype(bf16)
    back = lax.all_to_all(project_plane, "fsdp", split_axis=0, concat_axis=0, tiled=True)
    back = back.reshape(ring, own_rows, cols).astype(f32)

    def collect(low):
        parts = back[:, :, low : low + HEAD_DIM].reshape(KV_HEADS, sharers, own_rows, HEAD_DIM)
        return jnp.transpose(jnp.sum(parts, 1), (1, 0, 2)).reshape(own_rows, KV_HEADS * HEAD_DIM)

    query_plain = jnp.transpose(back[:, :, :own_width], (1, 0, 2)).reshape(own_rows, width)
    key_plain = collect(own_width)
    value_plain = collect(own_width + HEAD_DIM)
    first_gain_grad = (
        jnp.sum(query_plain * query_weight.astype(f32), 1)
        + jnp.sum(key_plain * key_weight.astype(f32), 1)
        + jnp.sum(value_plain * value_weight.astype(f32), 1)
    )
    attended_by_owner = jnp.transpose(
        attended_low.reshape(tokens, planes, ring, own_rows), (0, 2, 1, 3)
    ).reshape(tokens, width)
    output_term = dot_left_t(attended_by_owner, grad_branch_low).astype(bf16)
    output_plane = lax.psum_scatter(output_term, "fsdp", scatter_dimension=0, tiled=True)
    output_grad_weight = plane_scatter(output_plane.reshape(planes, own_rows, width))
    second_gain_all = lax.psum(lax.psum(second_gain_term, "fsdp"), "dp")
    mine = (lax.axis_index("dp") * ring + place) * own_rows
    second_gain_grad = lax.dynamic_slice_in_dim(second_gain_all, mine, own_rows)
    return (
        output[None],
        input_grad[None],
        first_gain_grad,
        query_plain * gain_mine,
        key_plain * gain_mine,
        value_plain * gain_mine,
        output_grad_weight,
        second_gain_grad,
        gate_up_grad[:, :ff_own],
        gate_up_grad[:, ff_own:],
        down_grad,
    )


TO_CORE = (7, 3, 5, 1)
TO_CHIPS = (6, 2, 4, 0)
VMEM = pl.BlockSpec(memory_space=pltpu.VMEM)
SMEM = pl.BlockSpec(memory_space=pltpu.SMEM)
log2_e = math.log2(math.e)


def turn(block, cosine, sine, forward):
    rolled = pltpu.roll(block, HEAD_DIM // 2, 1)
    return block * cosine + rolled * sine if forward else block * cosine - rolled * sine


def masked_scores(keys, queries, starts, low):
    scores = dot_right_t(keys, queries) * (score_scale * log2_e)
    key_pos = lax.broadcasted_iota(jnp.int32, scores.shape, 0)
    query_pos = lax.broadcasted_iota(jnp.int32, scores.shape, 1) + low
    return scores, (key_pos <= query_pos) & (key_pos >= starts)


anywhere = pl.BlockSpec(memory_space=pl.ANY)


def whole_of(array):
    return pl.BlockSpec(array.shape, lambda i: (0,) * len(array.shape))


def front_kernel(at_ref, normed_ref, *refs):
    first_ref, refs = refs[0], refs[1:]
    down_ref, held_ref, sem, refs = refs[-4], refs[-2], refs[-1], (*refs[:-4], refs[-3])
    devices, tokens = normed_ref.shape[:2]
    chunk = first_ref.shape[1] - tokens
    copies = [
        pltpu.make_async_copy(
            first_ref.at[device, pl.ds(tokens, chunk)],
            held_ref.at[pl.ds(device * chunk, chunk)],
            sem.at[device],
        )
        for device in range(devices)
    ]
    for copy in copies:
        copy.start()
    out = pltpu.make_async_copy(held_ref, down_ref, sem.at[devices])

    def midway():
        for copy in copies:
            copy.wait()
        out.start()

    front_body(midway, at_ref, normed_ref, *refs)
    out.wait()


def front_body(midway, at_ref, normed_ref, *refs):
    columns_refs, refs = refs[:2], refs[2:]
    cos_ref, sin_ref, starts_ref, refs = refs[0], refs[1], refs[2], refs[3:]
    q_ref, k_ref, v_ref, mixed_ref, norm_ref, project_ref, gain_ref, vt_ref = refs
    place = at_ref[0]
    devices, tokens = normed_ref.shape[:2]
    length = devices * tokens
    core = place & 1
    group = place >> 1
    rows = columns_refs[0].shape[2] - 16
    q_width = q_ref.shape[1]
    q_all = 2 * q_width
    for owner in range(4):
        for bit in range(4):
            for side in range(2):
                block = columns_refs[side]
                device = 2 * (group ^ bit) + (core ^ side)
                here = pl.ds(pl.multiple_of((owner * 8 + device) * rows, rows), rows)
                for which in range(2):

                    @pl.when(core == which)
                    def _():
                        project_ref[here, :q_width] = block[owner, bit, :rows, which * q_width : (which + 1) * q_width]

                project_ref[here, q_width:] = block[owner, bit, :rows, q_all:]
                gain_ref[owner * 8 + device] = block[owner, bit, rows:, :HEAD_DIM]

    for device in range(devices):
        here = slice(device * tokens, (device + 1) * tokens)
        raw = dot_plain(normed_ref[device], project_ref[...])
        cosine, sine = cos_ref[here, :], sin_ref[here, :]
        for low in range(0, q_width, HEAD_DIM):
            q_ref[here, low : low + HEAD_DIM] = turn(
                raw[:, low : low + HEAD_DIM], cosine, sine, True
            ).astype(bf16)
        k_ref[here, :] = turn(raw[:, q_width : q_width + HEAD_DIM], cosine, sine, True).astype(bf16)
        v_ref[here, :] = raw[:, q_width + HEAD_DIM :].astype(bf16)
    midway()
    vt_ref[...] = jnp.transpose(v_ref[...].astype(f32)).astype(bf16)
    block = 256
    for head in range(q_width // HEAD_DIM):
        cols = slice(head * HEAD_DIM, (head + 1) * HEAD_DIM)
        for low in range(0, length, block):
            high = low + block
            scores, allowed = masked_scores(
                k_ref[:high, :], q_ref[low:high, cols], starts_ref[:, low:high], low
            )
            scores = jnp.where(allowed, scores, mask_fill)
            top = jnp.max(scores, 0, keepdims=True)
            expo = jnp.exp2(scores - top)
            total = jnp.sum(expo, 0, keepdims=True)
            probs = (expo * (1.0 / total)).astype(bf16)
            mixed_ref[low:high, cols] = jnp.transpose(dot_plain(vt_ref[:, :high], probs)).astype(bf16)
            norm_ref[head, :, low:high] = top + jnp.log2(total)


def front(at, first, tokens, columns, columns_other, cosine, sine, starts):
    length = 8 * tokens
    q_width = (columns.shape[3] - 2 * HEAD_DIM) // 2
    cols = q_width + 2 * HEAD_DIM
    width = 32 * (columns.shape[2] - 16)
    shapes = [
        jax.ShapeDtypeStruct((length, q_width), bf16),
        jax.ShapeDtypeStruct((length, HEAD_DIM), bf16),
        jax.ShapeDtypeStruct((length, HEAD_DIM), bf16),
        jax.ShapeDtypeStruct((length, q_width), bf16),
        jax.ShapeDtypeStruct((q_width // HEAD_DIM, 1, length), f32),
        jax.ShapeDtypeStruct((width, cols), bf16),
        jax.ShapeDtypeStruct((32, 16, HEAD_DIM), bf16),
    ]
    return pl.pallas_call(
        front_kernel,
        grid=(1,),
        in_specs=[SMEM, pl.BlockSpec((8, tokens, width), lambda i: (0, 0, 0)), anywhere]
        + [whole_of(x) for x in (columns, columns_other, cosine, sine, starts)],
        out_specs=[whole_of(x) for x in shapes] + [anywhere],
        out_shape=shapes + [jax.ShapeDtypeStruct((8 * (first.shape[1] - tokens), width), bf16)],
        scratch_shapes=[
            pltpu.VMEM((HEAD_DIM, length), bf16),
            pltpu.VMEM((8 * (first.shape[1] - tokens), width), bf16),
            pltpu.SemaphoreType.DMA((9,)),
        ],
        compiler_params=pltpu.CompilerParams(vmem_limit_bytes=52 << 20),
        cost_estimate=pl.CostEstimate(
            flops=2 * length * width * cols + 4 * length * length * q_width,
            bytes_accessed=2 * length * width + 4 * width * cols,
            transcendentals=length * length,
        ),
        name="front",
    )(at, first, first, columns, columns_other, cosine, sine, starts)


def back_kernel(tokens, at_ref, q_ref, k_ref, v_ref, mixed_ref, norm_ref, packed_ref, project_ref,
                cos_ref, sin_ref, starts_ref, core_ref, chips_ref, cols_ref, kt_ref, dk_ref, dv_ref,
                grad_ref):
    place = at_ref[0]
    length, q_width = q_ref.shape
    for device in range(8):
        grad_ref[device * tokens : (device + 1) * tokens, :] = packed_ref[device, :tokens, :q_width]
    block = 256
    kt_ref[...] = jnp.transpose(k_ref[...].astype(f32)).astype(bf16)
    dk_ref[...] = jnp.zeros_like(dk_ref)
    dv_ref[...] = jnp.zeros_like(dv_ref)
    for head in range(q_width // HEAD_DIM):
        cols = slice(head * HEAD_DIM, (head + 1) * HEAD_DIM)
        for low in range(0, length, block):
            high = low + block
            queries, grads = q_ref[low:high, cols], grad_ref[low:high, cols]
            scores, allowed = masked_scores(k_ref[:high, :], queries, starts_ref[:, low:high], low)
            probs = jnp.where(allowed, jnp.exp2(scores - norm_ref[head, :, low:high]), 0.0)
            grad_prob = dot_right_t(v_ref[:high, :], grads)
            weighed = jnp.transpose(grads.astype(f32) * mixed_ref[low:high, cols].astype(f32))
            grad_score = (probs * (grad_prob - jnp.sum(weighed, 0, keepdims=True))).astype(bf16)
            dv_ref[:high, :] += dot_plain(probs.astype(bf16), grads)
            dk_ref[:high, :] += dot_plain(grad_score, queries)
            dq = jnp.transpose(dot_plain(kt_ref[:, :high], grad_score)) * score_scale
            cols_ref[low:high, cols] = turn(
                dq, cos_ref[low:high, :], sin_ref[low:high, :], False
            ).astype(bf16)
    cols_ref[:, q_width : q_width + HEAD_DIM] = turn(
        dk_ref[...] * score_scale, cos_ref[...], sin_ref[...], False
    ).astype(bf16)
    cols_ref[:, q_width + HEAD_DIM :] = dv_ref[...].astype(bf16)
    for out_ref, bits in ((core_ref, TO_CORE), (chips_ref, TO_CHIPS)):
        for step, bit in enumerate(bits):
            here = pl.ds(pl.multiple_of((place ^ bit) * tokens, tokens), tokens)
            out_ref[step] = dot_right_t(cols_ref[here, :], project_ref[...]).astype(bf16)


def back(at, queries, keys, values, mixed, norm, grads, project, cosine, sine, starts):
    length, q_width = queries.shape
    width, cols = project.shape
    tokens = length // 8
    return pl.pallas_call(
        functools.partial(back_kernel, tokens),
        in_specs=[SMEM] + [VMEM] * 10,
        out_specs=[VMEM] * 3,
        out_shape=[
            jax.ShapeDtypeStruct((4, tokens, width), bf16),
            jax.ShapeDtypeStruct((4, tokens, width), bf16),
            jax.ShapeDtypeStruct((length, cols), bf16),
        ],
        scratch_shapes=[
            pltpu.VMEM((HEAD_DIM, length), bf16),
            pltpu.VMEM((length, HEAD_DIM), f32),
            pltpu.VMEM((length, HEAD_DIM), f32),
            pltpu.VMEM((length, q_width), bf16),
        ],
        compiler_params=pltpu.CompilerParams(vmem_limit_bytes=52 << 20),
        cost_estimate=pl.CostEstimate(
            flops=600 * length * width * cols + 7 * length * length * q_width,
            bytes_accessed=2 * length * width + 2 * width * cols,
            transcendentals=length * length,
        ),
        name="back",
    )(at, queries, keys, values, mixed, norm, grads, project, cosine, sine, starts)


def project_grad_kernel(first_ref, cols_ref, out_ref):
    normed = first_ref[...].reshape(cols_ref.shape[0], first_ref.shape[2])
    out_ref[...] = jnp.transpose(dot_left_t(cols_ref[...], normed)).astype(bf16)


def project_grad(first, grad_cols):
    length, cols = grad_cols.shape
    width = first.shape[2]
    part = 512
    return pl.pallas_call(
        project_grad_kernel,
        grid=(width // part,),
        in_specs=[
            pl.BlockSpec((8, length // 8, part), lambda i: (0, 0, i)),
            pl.BlockSpec((length, cols), lambda i: (0, 0)),
        ],
        out_specs=pl.BlockSpec((part, cols), lambda i: (i, 0)),
        out_shape=jax.ShapeDtypeStruct((width, cols), bf16),
        compiler_params=pltpu.CompilerParams(vmem_limit_bytes=52 << 20),
        cost_estimate=pl.CostEstimate(
            flops=20 * length * width * cols, bytes_accessed=2 * length * width, transcendentals=0
        ),
        name="project_grad",
    )(first, grad_cols)


def output_grad_kernel(at_ref, packed_ref, attended_ref, out_ref):
    own = packed_ref.shape[2] // 2
    rows = out_ref.shape[1] - 16
    tokens = packed_ref.shape[1] - 16
    total = None
    gain = None
    for device in range(8):
        term = dot_left_t(
            packed_ref[device, :tokens, own:], attended_ref[device * tokens : (device + 1) * tokens, :]
        )
        extra = jnp.sum(packed_ref[device, tokens:, own:].astype(f32), 0, keepdims=True)
        total = term if total is None else total + term
        gain = extra if gain is None else gain + extra
    turned = jnp.transpose(total).astype(bf16)
    first = lax.broadcasted_iota(jnp.int32, (16, own), 0) == 0
    gain_rows = jnp.where(first, jnp.broadcast_to(gain, (16, own)), 0.0)
    for owner in range(4):
        out_ref[owner, :rows, :] = turned[owner * rows : (owner + 1) * rows, :]
        here = jnp.where(at_ref[0] // 2 == owner, 1.0, 0.0)
        out_ref[owner, rows:, :] = (gain_rows * here).astype(bf16)


def output_grad_term(at, packed, attended):
    length, width = attended.shape
    own = packed.shape[2] // 2
    return pl.pallas_call(
        output_grad_kernel,
        in_specs=[SMEM] + [VMEM] * 2,
        out_specs=VMEM,
        out_shape=jax.ShapeDtypeStruct((4, width // 4 + 16, own), bf16),
        compiler_params=pltpu.CompilerParams(vmem_limit_bytes=52 << 20),
        cost_estimate=pl.CostEstimate(
            flops=60 * length * own * width, bytes_accessed=2 * length * width, transcendentals=0
        ),
        name="output_grad_term",
    )(at, packed, attended)


def place_blocks(plane, blocks, out_ref):
    tokens = blocks[0].shape[0]
    for block, move in zip(blocks, LINE):
        owner = plane + move if move != 3 else 3 - plane
        valid = (owner >= 0) & (owner <= 3) if move != 3 else (plane == 0) | (plane == 3)

        @pl.when(valid)
        def _():
            out_ref[pl.ds(pl.multiple_of(owner * tokens, tokens), tokens), :] = block[...]


def feed_kernel(units, count, n_count, at_ref, *refs):
    d_refs, n_refs, refs = refs[:4], refs[4 : 4 + n_count], refs[4 + n_count :]
    both_ref, down_ref, rows_ref, refs = *refs[:3], refs[3 + count :]
    second_ref, direct_ref, hidden_ref, grads_ref, term_ref, held_ref = refs
    step = pl.program_id(0)

    @pl.when(step == 0)
    def _():
        tokens = d_refs[0].shape[0]
        for slot in range(4):
            owner = (at_ref[1] - slot) & 3
            direct_ref[pl.ds(pl.multiple_of(owner * tokens, tokens), tokens), :] = d_refs[slot][...]
        if n_count == 6:
            place_blocks(at_ref[1], n_refs, second_ref)
        else:
            second_ref[...] = n_refs[0][...].reshape(second_ref.shape)

    @pl.when(step < units)
    def _():
        raw = dot_plain(second_ref[...], both_ref[...])
        half = raw.shape[1] // 2
        gate, upward = raw[:, :half], raw[:, half:]
        sig = 1.0 / (1.0 + jnp.exp(-gate))
        silu = gate * sig
        hidden_ref[...] = (silu * upward).astype(bf16)
        grad_hidden = dot_right_t(direct_ref[...], down_ref[...])
        grad_gate = (grad_hidden * upward * sig * (1.0 + gate * (1.0 - sig))).astype(bf16)
        grads = jnp.concatenate([grad_gate, (grad_hidden * silu).astype(bf16)], 1)
        grads_ref[...] = grads
        held_ref[step] = grads

    @pl.when(step >= units)
    def _():
        total = None
        for unit in range(units):
            cols = slice(unit * held_ref.shape[2], (unit + 1) * held_ref.shape[2])
            part = dot_right_t(held_ref[unit], rows_ref[:, cols])
            total = part if total is None else total + part
        term_ref[...] = total.astype(bf16).reshape(term_ref.shape)


def feed(at, part_at, parts_of, seconds, directs, both, down, so_far):
    tokens, width = seconds[0].shape[-2:]
    some = 4 * tokens
    ff = down.shape[0]
    n_count = len(seconds)
    gathered = pl.BlockSpec((4, tokens, width), lambda i: (0, 0, 0))
    single = pl.BlockSpec((tokens, width), lambda i: (0, 0))
    unit, part = 128, 256
    units, parts = ff // unit, width // part
    so_far = so_far or []
    total = parts_of * some
    outs = pl.pallas_call(
        functools.partial(feed_kernel, units, len(so_far), n_count),
        grid=(units + parts,),
        in_specs=[
            SMEM,
            *[pl.BlockSpec((tokens, width), lambda i: (part_at, 0))] * 4,
            *[single if n_count == 6 else gathered] * n_count,
            pl.BlockSpec((width, 2 * unit), lambda i: (0, jnp.minimum(i, units - 1))),
            pl.BlockSpec((unit, width), lambda i: (jnp.minimum(i, units - 1), 0)),
            pl.BlockSpec((part, 2 * ff), lambda i: (jnp.maximum(i - units, 0), 0)),
        ]
        + [pl.BlockSpec(memory_space=pl.ANY)] * len(so_far),
        out_specs=[
            pl.BlockSpec((some, width), lambda i: (part_at, 0)),
            pl.BlockSpec((some, width), lambda i: (part_at, 0)),
            pl.BlockSpec((some, unit), lambda i: (part_at, jnp.minimum(i, units - 1))),
            pl.BlockSpec((some, 2 * unit), lambda i: (part_at, jnp.minimum(i, units - 1))),
            pl.BlockSpec((4, tokens, part), lambda i: (0, 0, jnp.maximum(i - units, 0))),
        ],
        out_shape=[
            jax.ShapeDtypeStruct((total, width), bf16),
            jax.ShapeDtypeStruct((total, width), bf16),
            jax.ShapeDtypeStruct((total, ff), bf16),
            jax.ShapeDtypeStruct((total, 2 * ff), bf16),
            jax.ShapeDtypeStruct((4, tokens, width), bf16),
        ],
        scratch_shapes=[pltpu.VMEM((units, some, 2 * unit), bf16)],
        input_output_aliases={8 + n_count + i: i for i in range(len(so_far))},
        compiler_params=pltpu.CompilerParams(vmem_limit_bytes=52 << 20),
        cost_estimate=pl.CostEstimate(
            flops=10 * some * width * ff,
            bytes_accessed=10 * width * ff,
            transcendentals=some * ff,
        ),
        name="feed",
    )(at, *directs, *seconds, both, down, both, *so_far)
    return outs[:4], outs[4]


def branch_kernel(hidden_ref, down_ref, out_ref):
    out_ref[...] = dot_plain(hidden_ref[...], down_ref[...]).astype(bf16).reshape(out_ref.shape)


def branch(hidden, down, parts):
    rows, ff = hidden.shape
    width = down.shape[1]
    tokens = rows // (4 * parts)
    return pl.pallas_call(
        branch_kernel,
        grid=(parts, 4),
        in_specs=[
            pl.BlockSpec((4 * tokens, ff), lambda h, i: (h, 0)),
            pl.BlockSpec((ff, width // 4), lambda h, i: (0, i)),
        ],
        out_specs=pl.BlockSpec((4, tokens, width // 4), lambda h, i: (0, h, i)),
        out_shape=jax.ShapeDtypeStruct((4, parts * tokens, width), bf16),
        compiler_params=pltpu.CompilerParams(vmem_limit_bytes=52 << 20),
        cost_estimate=pl.CostEstimate(flops=1 << 20, bytes_accessed=1 << 16, transcendentals=0),
        name="branch",
    )(hidden, down)


def split_kernel(both_ref, gate_ref, up_ref):
    for low in range(0, gate_ref.shape[1], 128):
        gate_ref[:, low : low + 128] = both_ref[:, 2 * low : 2 * low + 128].astype(f32)
        up_ref[:, low : low + 128] = both_ref[:, 2 * low + 128 : 2 * low + 256].astype(f32)


def split(both):
    rows, cols = both.shape
    out = jax.ShapeDtypeStruct((rows, cols // 2), f32)
    part = pl.BlockSpec((64, cols // 2), lambda i: (i, 0))
    return pl.pallas_call(
        split_kernel,
        grid=(rows // 64,),
        in_specs=[pl.BlockSpec((64, cols), lambda i: (i, 0))],
        out_specs=[part, part],
        out_shape=[out, out],
        name="split",
    )(both)


def finish_kernel(final_ref, gain_ref, qw_ref, kw_ref, vw_ref, q_ref, k_ref, v_ref, o_ref, first_ref, second_ref):
    rows = q_ref.shape[0]
    own = q_ref.shape[1] // 8
    gain = gain_ref[...]
    first = None
    second = None
    for device in range(8):
        block = final_ref[device, :rows, :].astype(f32)
        cols = slice(device * own, (device + 1) * own)
        head = slice(device // 2 * HEAD_DIM, (device // 2 + 1) * HEAD_DIM)
        out_ref, weight_ref = ((k_ref, kw_ref), (v_ref, vw_ref))[device % 2]
        query, shared = block[:, :own], block[:, own : own + HEAD_DIM]
        q_ref[:, cols] = query * gain
        out_ref[:, head] = shared * gain
        o_ref[:, cols] = block[:, own + HEAD_DIM :]
        term = jnp.sum(query * qw_ref[:, cols].astype(f32), 1, keepdims=True) + jnp.sum(
            shared * weight_ref[:, head].astype(f32), 1, keepdims=True
        )
        extra = jnp.sum(final_ref[device, rows:, :HEAD_DIM].astype(f32), 0, keepdims=True)
        first = term if first is None else first + term
        second = extra if second is None else second + extra
    first_ref[...] = first
    second_ref[...] = second


def finish(final, gain, query_weight, key_weight, value_weight):
    def like(weight):
        return jax.ShapeDtypeStruct(weight.shape, f32)

    rows = query_weight.shape[0]
    return pl.pallas_call(
        finish_kernel,
        in_specs=[VMEM] * 5,
        out_specs=[VMEM] * 6,
        out_shape=[
            like(query_weight),
            like(key_weight),
            like(value_weight),
            like(query_weight),
            jax.ShapeDtypeStruct((rows, 1), f32),
            jax.ShapeDtypeStruct((1, HEAD_DIM), f32),
        ],
        compiler_params=pltpu.CompilerParams(vmem_limit_bytes=32 << 20),
        name="finish",
    )(final, gain, query_weight, key_weight, value_weight)


def middle_back_kernel(low_ref, high_ref, middle_ref, inv_ref, gain_ref, direct_ref, weight_ref,
                       packed_ref, grad_ref, branch_ref):
    tokens, width = grad_ref.shape
    half = tokens // 2
    own = weight_ref.shape[0]
    step = pl.program_id(0)

    @pl.when(step == 0)
    def _():
        for first, ref in ((0, low_ref), (half, high_ref)):
            here = slice(first, first + half)
            total = ref[0].astype(f32)
            for plane in (1, 2, 3):
                total = total + ref[plane].astype(f32)
            middle, inv = middle_ref[here, :], inv_ref[here, :]
            weighted = total * gain_ref[...]
            grad = inv * weighted - middle * inv**3 * jnp.mean(weighted * middle, -1, keepdims=True)
            grad_ref[here, :] = grad
            branch_ref[here, :] = (direct_ref[here, :] + grad).astype(bf16)
            term = jnp.sum(total * middle * inv, 0, keepdims=True)
            gain_term = term if first == 0 else gain_term + term
        gain_high = gain_term.astype(bf16).astype(f32)
        row = lax.broadcasted_iota(jnp.int32, (16, width), 0)
        branch_ref[tokens:, :] = jnp.where(
            row == 0, gain_high, jnp.where(row == 1, gain_term - gain_high, 0.0)
        ).astype(bf16)

    packed_ref[0, :tokens, :own] = dot_right_t(branch_ref[:tokens, :], weight_ref[...]).astype(bf16)
    packed_ref[0, tokens:, :own] = jnp.zeros((16, own), bf16)
    packed_ref[0, :, own:] = branch_ref[:, pl.ds(pl.multiple_of(step * own, own), own)]


def middle_back(low, high, middle, inv, gain, direct, weight):
    tokens, width = middle.shape
    own = width // 8
    whole = pl.BlockSpec((4, tokens // 2, width), lambda i: (0, 0, 0))
    rows = pl.BlockSpec((tokens, width), lambda i: (0, 0))
    return pl.pallas_call(
        middle_back_kernel,
        grid=(8,),
        in_specs=[
            whole,
            whole,
            rows,
            pl.BlockSpec((tokens, 1), lambda i: (0, 0)),
            pl.BlockSpec((1, width), lambda i: (0, 0)),
            rows,
            pl.BlockSpec((own, width), lambda i: (i, 0)),
        ],
        out_specs=[pl.BlockSpec((1, tokens + 16, 2 * own), lambda i: (i, 0, 0)), rows],
        out_shape=[
            jax.ShapeDtypeStruct((8, tokens + 16, 2 * own), bf16),
            jax.ShapeDtypeStruct((tokens, width), f32),
        ],
        scratch_shapes=[pltpu.VMEM((tokens + 16, width), bf16)],
        compiler_params=pltpu.CompilerParams(vmem_limit_bytes=48 << 20),
        cost_estimate=pl.CostEstimate(
            flops=2 * tokens * width * width, bytes_accessed=3 * width * width, transcendentals=0
        ),
        name="middle_back",
    )(low, high, middle, inv, gain, direct, weight)


def middle_kernel(parts_ref, weight_ref, rows_ref, gain_ref, attended_ref, branch_ref, middle_ref, inv_ref,
                  low_ref, high_ref, total_ref):
    step = pl.program_id(0)
    term = dot_plain(parts_ref[0], weight_ref[...])
    attended_ref[...] = parts_ref[0]

    @pl.when(step == 0)
    def _():
        total_ref[...] = term

    @pl.when(step > 0)
    def _():
        total_ref[...] += term

    @pl.when(step == pl.num_programs(0) - 1)
    def _():
        half = low_ref.shape[0]
        branch = total_ref[...]
        middle = rows_ref[...].astype(f32) + branch
        inv = rms_scale(middle)
        branch_ref[...] = branch
        middle_ref[...] = middle
        inv_ref[...] = inv
        second = (middle * inv * gain_ref[...]).astype(bf16)
        low_ref[...] = second[:half]
        high_ref[...] = second[half:]


def middle_forward(parts, weight, rows, gain):
    devices, tokens, own = parts.shape
    width = weight.shape[1]
    half = pl.BlockSpec((tokens // 2, width), lambda i: (0, 0))
    whole = pl.BlockSpec((tokens, width), lambda i: (0, 0))
    return pl.pallas_call(
        middle_kernel,
        grid=(devices,),
        in_specs=[
            pl.BlockSpec((1, tokens, own), lambda i: (i, 0, 0)),
            pl.BlockSpec((own, width), lambda i: (i, 0)),
            whole,
            pl.BlockSpec((1, width), lambda i: (0, 0)),
        ],
        out_specs=[
            pl.BlockSpec((tokens, own), lambda i: (0, i)),
            whole,
            whole,
            pl.BlockSpec((tokens, 1), lambda i: (0, 0)),
            half,
            half,
        ],
        out_shape=[
            jax.ShapeDtypeStruct((tokens, devices * own), bf16),
            jax.ShapeDtypeStruct((tokens, width), f32),
            jax.ShapeDtypeStruct((tokens, width), f32),
            jax.ShapeDtypeStruct((tokens, 1), f32),
            jax.ShapeDtypeStruct((tokens // 2, width), bf16),
            jax.ShapeDtypeStruct((tokens // 2, width), bf16),
        ],
        scratch_shapes=[pltpu.VMEM((tokens, width), f32)],
        compiler_params=pltpu.CompilerParams(vmem_limit_bytes=48 << 20),
        cost_estimate=pl.CostEstimate(
            flops=2 * tokens * width * width, bytes_accessed=3 * width * width, transcendentals=0
        ),
        name="middle_forward",
    )(parts, weight, rows, gain)


def fast_device(
    layer_input,
    output_grad,
    layer_keep,
    group_ids,
    exit_scale,
    doc_lengths,
    attention_gain,
    query_weight,
    key_weight,
    value_weight,
    output_weight,
    feedforward_gain,
    gate_weight,
    up_weight,
    down_weight,
):
    tokens, width = layer_input.shape[1:]
    place, plane = lax.axis_index("fsdp"), lax.axis_index("dp")
    at = jnp.stack([place, plane]).astype(jnp.int32)
    length = tokens * 8
    own_rows = query_weight.shape[0]
    q_width = HEADS // 8 * HEAD_DIM
    cols = q_width + 2 * HEAD_DIM
    ff_own = gate_weight.shape[1]
    half = tokens // 2
    rows = layer_input[0].astype(f32)
    keep = layer_keep[0].astype(f32)

    both_mine = jnp.stack(
        [gate_weight.reshape(-1, ff_own // 128, 128), up_weight.reshape(-1, ff_own // 128, 128)], 2
    ).reshape(-1, 2 * ff_own)
    inv_first = rms_scale(rows)
    normed = (rows * inv_first).astype(bf16)
    first = lax.all_gather(jnp.concatenate([normed, down_weight], 0), "fsdp", axis=0, tiled=False)
    gain_mine = attention_gain.astype(f32)[:, None]

    def by_chip(weight):
        scaled = (weight.astype(f32) * gain_mine).astype(bf16)
        return scaled.reshape(own_rows, 4, weight.shape[1] // 4)

    sent = jnp.concatenate([by_chip(query_weight), by_chip(key_weight), by_chip(value_weight)], -1)
    sent = jnp.transpose(sent, (1, 0, 2))
    wide = sent.shape[2]
    gain_rows = jnp.pad(feedforward_gain[None, :], ((0, 15), (0, wide - own_rows)))
    group = place // 2

    def to_chip(bit):
        block = lax.dynamic_index_in_dim(sent, group ^ bit, 0, keepdims=False)
        return jnp.concatenate([block, gain_rows], 0)

    picked = jnp.sum(
        jnp.where(jnp.arange(exit_scale.shape[0], dtype=jnp.int32) == group_ids[0], exit_scale, 0.0)
    )
    cotangent = output_grad[0].astype(f32) * picked
    direct = keep * cotangent
    direct_low = direct.astype(bf16)
    direct_1 = shift(direct_low, 1)
    columns = jnp.stack([to_chip(0)] + [flip(to_chip(bit), 2 * bit) for bit in (1, 2, 3)])
    output_plane = gather_planes(after(output_weight, columns, direct_1))
    columns = gather_planes(after(columns, output_plane))
    columns_other = flip(columns, 1)
    output_full = lax.all_gather(output_plane, "fsdp", axis=1, tiled=True).reshape(width, width)
    both = lax.all_gather(after(both_mine, columns), "fsdp", axis=0, tiled=True)
    half_dim = HEAD_DIM // 2
    frequency = rope_base ** (-(2.0 * np.arange(HEAD_DIM // 2, dtype=np.float32)) / HEAD_DIM)
    angles = np.arange(length, dtype=np.float32)[:, None] * frequency.astype(np.float32)[None, :]
    cosine = jnp.asarray(np.concatenate([np.cos(angles), np.cos(angles)], 1).astype(np.float32))
    sine = jnp.asarray(np.concatenate([-np.sin(angles), np.sin(angles)], 1).astype(np.float32))
    order = jnp.arange(doc_lengths.shape[1])
    ends = jnp.sum(jnp.where(order[None, :] <= order[:, None], doc_lengths[0][None, :], 0), 1)
    positions = jnp.arange(length, dtype=jnp.int32)
    starts = jnp.max(jnp.where(positions[None, :] >= ends[:, None], ends[:, None], 0), 0)[None, :]

    direct_2 = shift(after(direct_low, columns), 2)
    queries, keys, values, mixed, norm, project, gains, down_use = front(
        at, first, tokens, columns, columns_other, cosine, sine, starts
    )
    gain_second = gains[:, 0, :own_rows].reshape(width).astype(f32)

    parts = lax.all_to_all(mixed.reshape(8, tokens, q_width), "fsdp", split_axis=0, concat_axis=0)
    direct_3 = shift(after(direct_low, columns), 3)
    parts = after(parts, direct_2)
    attended_low, branch_attention, middle, inv_second, second_low, second_high = middle_forward(
        parts, output_full, layer_input[0], gain_second[None, :]
    )
    directs = [direct_low, direct_1, direct_2, direct_3]
    second_half = after(second_low, direct_3)
    second_near = line_first(second_half)
    seconds_low = [second_half, *second_near, *line_second(*second_near)]
    attended_all = lax.all_gather(after(attended_low, *seconds_low), "fsdp", axis=0, tiled=True)
    seconds_high = gather_planes(after(second_high, *seconds_low))

    stacked, terms_low = feed(at, 0, 2, seconds_low, directs, both, down_use, None)
    stacked, terms_high = feed(at, 1, 2, [seconds_high], directs, both, down_use, stacked)
    second_all, direct_all, hidden_all, grads_all = stacked
    got_low = swap_planes(terms_low)

    branch_terms = branch(hidden_all, down_use, 2)
    down_term = dot_left_t(after(hidden_all, got_low), direct_all).astype(bf16)
    both_term = dot_left_t(second_all, grads_all).astype(bf16)
    got_high = after(swap_planes(after(terms_high, got_low)), branch_terms, both_term)
    down_grad = lax.psum_scatter(down_term, "fsdp", scatter_dimension=0, tiled=True).astype(f32)
    both_grad = lax.psum_scatter(both_term, "fsdp", scatter_dimension=0, tiled=True)

    to_send, grad_middle = middle_back(
        got_low, got_high, middle, inv_second, gain_second[None, :], direct, output_full
    )
    packed = lax.all_to_all(to_send, "fsdp", split_axis=0, concat_axis=0)

    def ahead(step):
        return lax.dynamic_index_in_dim(branch_terms, jnp.clip(step, 0, 3), 0, keepdims=False)

    branch_up2 = lax.ppermute(after(ahead(plane + 2), to_send), "dp", UP[:2])
    branch_down2 = lax.ppermute(after(ahead(plane - 2), to_send), "dp", DOWN[1:])
    branch_far = lax.ppermute(after(ahead(3 - plane), to_send), "dp", [(3, 1), (0, 2)])
    output_term = output_grad_term(at, packed, attended_all)
    output_got = swap_planes(output_term)
    packed = after(packed, output_term)
    core_terms, chip_terms, grad_cols = back(
        at, queries, keys, values, mixed, norm, packed, project, cosine, sine, starts
    )
    core_terms, branch_up2, branch_down2, branch_far = after_all(
        (core_terms, branch_up2, branch_down2, branch_far)
    )
    other = flip(core_terms, 1)
    project_term = project_grad(first, grad_cols)
    other = after(other, project_term)
    sums = [add_low(chip_terms[i], other[i]) for i in range(3)]
    far, near_x, near_y = flip(sums[0], 6), flip(sums[1], 2), flip(sums[2], 4)
    core = place % 2
    keys_term, values_term = project_term[:, q_width : q_width + HEAD_DIM], project_term[:, q_width + HEAD_DIM :]
    kept = jnp.where(core == 0, keys_term, values_term)
    kept = add_low(kept, flip(jnp.where(core == 0, values_term, keys_term), 1))
    project_term = jnp.concatenate([project_term[:, :q_width], kept], 1)
    kept_cols = q_width + HEAD_DIM
    project_got = swap_planes(after(project_term.reshape(4, width // 4, kept_cols), output_got))
    zero = jnp.zeros((), bf16)
    branch_up2, branch_down2, branch_far = after_all((branch_up2, branch_down2, branch_far), *sums)
    sent_up = (
        ahead(plane + 1).astype(f32)
        + branch_up2.astype(f32)
        + jnp.where(plane == 2, branch_far, zero).astype(f32)
    ).astype(bf16)
    sent_down = (
        ahead(plane - 1).astype(f32)
        + branch_down2.astype(f32)
        + jnp.where(plane == 1, branch_far, zero).astype(f32)
    ).astype(bf16)
    branch_up1 = lax.ppermute(sent_up, "dp", UP)
    branch_down1 = lax.ppermute(sent_down, "dp", DOWN)
    branch_feed = ahead(plane).astype(f32) + branch_up1.astype(f32) + branch_down1.astype(f32)
    project_plane = jnp.sum(project_got.astype(f32), 0).astype(bf16)
    output_plane_sum = jnp.sum(output_got.astype(f32), 0).astype(bf16)
    both_plane = jnp.concatenate([project_plane, output_plane_sum[: 8 * own_rows]], 1)
    gain_four = output_plane_sum[8 * own_rows].reshape(4, own_rows)
    low_half = place % 2 == 0
    gain_eight = jnp.concatenate(
        [jnp.where(low_half, gain_four, 0), jnp.where(low_half, 0, gain_four)], 0
    )
    gain_eight = jnp.pad(gain_eight[:, None, :], ((0, 0), (0, 15), (0, kept_cols + q_width - own_rows)))
    final = jnp.concatenate([both_plane.reshape(8, own_rows, kept_cols + q_width), gain_eight], 1)
    gate_grad, up_grad = split(both_grad)
    final = lax.all_to_all(after(final, far, near_x, near_y, sent_up, sent_down, gate_grad), "fsdp", split_axis=0, concat_axis=0)
    weighted_first = (
        chip_terms[3].astype(f32)
        + other[3].astype(f32)
        + far.astype(f32)
        + near_x.astype(f32)
        + near_y.astype(f32)
    )
    grad_rows = inv_first * weighted_first - rows * inv_first**3 * jnp.mean(
        weighted_first * rows, -1, keepdims=True
    )
    input_grad = cotangent + grad_middle + grad_rows

    output = (rows + keep * (branch_attention + branch_feed)).astype(bf16)

    final = after(final, branch_up1, branch_down1)
    query_grad, key_grad, value_grad, output_sum, first_gain, second_gain = finish(
        final, gain_mine, query_weight, key_weight, value_weight
    )
    return (
        output[None],
        input_grad[None],
        first_gain[:, 0],
        query_grad,
        key_grad,
        value_grad,
        output_sum,
        second_gain[0, :own_rows],
        gate_grad,
        up_grad,
        down_grad,
    )


def solution(mesh):
    both = ("dp", "fsdp")
    fast = (mesh.shape["dp"], mesh.shape["fsdp"]) == (4, 8)
    return jax.shard_map(
        fast_device if fast else per_device,
        mesh=mesh,
        in_specs=(
            P("dp", "fsdp", None),
            P("dp", "fsdp", None),
            P("dp"),
            P("dp"),
            P(),
            P("dp", None),
            P(both),
            P(both, None),
            P(both, None),
            P(both, None),
            P(both, None),
            P(both),
            P("fsdp", "dp"),
            P("fsdp", "dp"),
            P(both, None),
        ),
        out_specs=(
            P("dp", "fsdp", None),
            P("dp", "fsdp", None),
            P(both),
            P(both, None),
            P(both, None),
            P(both, None),
            P(both, None),
            P(both),
            P("fsdp", "dp"),
            P("fsdp", "dp"),
            P(both, None),
        ),
        check_vma=False,
    )
```

```python
import functools
import math

import jax
import jax.numpy as jnp
import numpy as np
from jax import lax
from jax.experimental import pallas as pl
from jax.experimental.pallas import tpu as pltpu
from jax.sharding import PartitionSpec as P

HEADS = 16
KV_HEADS = 4
HEAD_DIM = 128

norm_eps = 1e-05
rope_base = 10000.0
mask_fill = -1e30
score_scale = 1.0 / math.sqrt(HEAD_DIM)
f32 = jnp.float32
bf16 = jnp.bfloat16


def dot_plain(left, right):
    return jnp.dot(left, right, preferred_element_type=f32)


def dot_right_t(left, right):
    return lax.dot_general(left, right, (((1,), (1,)), ((), ())), preferred_element_type=f32)


def dot_left_t(left, right):
    return lax.dot_general(left, right, (((0,), (0,)), ((), ())), preferred_element_type=f32)


def rotary_tables(length):
    half_dim = HEAD_DIM // 2
    frequency = rope_base ** (-(2.0 * jnp.arange(half_dim, dtype=f32)) / HEAD_DIM)
    angles = jnp.arange(length, dtype=jnp.int32).astype(f32)[:, None] * frequency[None, :]
    return (jnp.cos(angles)[:, None, :], jnp.sin(angles)[:, None, :])


def rotate(vectors, cosine, sine_part):
    half_dim = vectors.shape[-1] // 2
    lower_half = vectors[..., :half_dim]
    upper_half = vectors[..., half_dim:]
    return jnp.concatenate(
        [
            lower_half * cosine - upper_half * sine_part,
            upper_half * cosine + lower_half * sine_part,
        ],
        -1,
    )


def rms_scale(rows):
    return lax.rsqrt(jnp.mean(rows * rows, -1, keepdims=True) + norm_eps)


def after_all(values, *earlier):
    return lax.optimization_barrier((*values, *earlier))[: len(values)]


def after(value, *earlier):
    return lax.optimization_barrier((value, *earlier))[0]


def plane_gather(block):
    whole = lax.all_gather(block, "dp", axis=0)
    return [whole[i] for i in range(whole.shape[0])]


def add_low(left, right):
    return (left.astype(f32) + right.astype(f32)).astype(left.dtype)


def plane_scatter(whole):
    return lax.psum_scatter(whole, "dp", scatter_dimension=0, tiled=False).astype(f32)


FLIP = {bit: [(i, i ^ bit) for i in range(8)] for bit in (1, 2, 4, 6)}


def flip(block, bit):
    return lax.ppermute(block, "fsdp", FLIP[bit])


def shift(block, step):
    return lax.ppermute(block, "dp", [(i, (i + step) % 4) for i in range(4)])


UP = [(0, 1), (1, 2), (2, 3)]
DOWN = [(1, 0), (2, 1), (3, 2)]
LINE = (0, -1, 1, -2, 2, 3)


def line_first(block):
    return lax.ppermute(block, "dp", UP), lax.ppermute(block, "dp", DOWN)


def line_second(up, down):
    plane = lax.axis_index("dp")
    far = jnp.where(plane == 2, down, up)
    return (
        lax.ppermute(up, "dp", UP[1:]),
        lax.ppermute(down, "dp", DOWN[:2]),
        lax.ppermute(far, "dp", [(2, 0), (1, 3)]),
    )


def gather_planes(block):
    copies = jnp.broadcast_to(block[None], (4, *block.shape))
    return lax.all_to_all(copies, "dp", split_axis=0, concat_axis=0)


def swap_planes(whole):
    return lax.all_to_all(whole, "dp", split_axis=0, concat_axis=0)


def block_rows_of(length):
    return math.gcd(length, 256)


def transposed_scores(keys, queries, starts, low, high, width):
    scores = dot_right_t(keys, queries) * score_scale
    key_pos = lax.broadcasted_iota(jnp.int32, (width, high - low), 0)
    query_pos = lax.broadcasted_iota(jnp.int32, (width, high - low), 1) + low
    allowed = (key_pos <= query_pos) & (key_pos >= starts)
    return scores, allowed


def attend_kernel(rows_of, q_ref, k_ref, vt_ref, starts_ref, out_ref, norm_ref):
    length = q_ref.shape[0]
    for low in range(0, length, rows_of):
        high = low + rows_of
        starts = starts_ref[:, low:high]
        scores, allowed = transposed_scores(
            k_ref[:high, :], q_ref[low:high, :], starts, low, high, high
        )
        scores = jnp.where(allowed, scores, mask_fill)
        top = jnp.max(scores, 0, keepdims=True)
        expo = jnp.exp(scores - top)
        total = jnp.sum(expo, 0, keepdims=True)
        probs = (expo * (1.0 / total)).astype(bf16)
        mixed = dot_plain(vt_ref[:, :high], probs)
        out_ref[low:high, :] = jnp.transpose(mixed).astype(out_ref.dtype)
        norm_ref[0, :, low:high] = top + jnp.log(total)


def attend(queries, keys, values, starts):
    length, width = queries.shape
    heads = width // HEAD_DIM
    return pl.pallas_call(
        functools.partial(attend_kernel, block_rows_of(length)),
        grid=(heads,),
        in_specs=[
            pl.BlockSpec((length, HEAD_DIM), lambda h: (0, h)),
            pl.BlockSpec((length, HEAD_DIM), lambda h: (0, 0)),
            pl.BlockSpec((HEAD_DIM, length), lambda h: (0, 0)),
            pl.BlockSpec((1, length), lambda h: (0, 0)),
        ],
        out_specs=[
            pl.BlockSpec((length, HEAD_DIM), lambda h: (0, h)),
            pl.BlockSpec((1, 1, length), lambda h: (h, 0, 0)),
        ],
        out_shape=[
            jax.ShapeDtypeStruct((length, width), bf16),
            jax.ShapeDtypeStruct((heads, 1, length), f32),
        ],
        compiler_params=pltpu.CompilerParams(vmem_limit_bytes=48 << 20),
        cost_estimate=pl.CostEstimate(
            flops=3 * heads * length * length * HEAD_DIM,
            bytes_accessed=8 * length * width,
            transcendentals=heads * length * length,
        ),
        name="attend",
    )(queries, keys, jnp.transpose(values), starts)


def attend_back_kernel(
    rows_of, q_ref, k_ref, kt_ref, v_ref, starts_ref, norm_ref, out_ref, grad_ref, dq_ref, dk_ref, dv_ref
):
    length = q_ref.shape[0]

    @pl.when(pl.program_id(0) == 0)
    def _():
        dk_ref[...] = jnp.zeros_like(dk_ref)
        dv_ref[...] = jnp.zeros_like(dv_ref)

    for low in range(0, length, rows_of):
        high = low + rows_of
        starts = starts_ref[:, low:high]
        queries = q_ref[low:high, :]
        grads = grad_ref[low:high, :]
        scores, allowed = transposed_scores(k_ref[:high, :], queries, starts, low, high, high)
        probs = jnp.where(allowed, jnp.exp(scores - norm_ref[0, :, low:high]), 0.0)
        grad_prob = dot_right_t(v_ref[:high, :], grads)
        weighed = jnp.transpose(grads.astype(f32) * out_ref[low:high, :].astype(f32))
        delta = jnp.sum(weighed, 0, keepdims=True)
        grad_score = (probs * (grad_prob - delta)).astype(bf16)
        dv_ref[:high, :] += dot_plain(probs.astype(bf16), grads)
        dk_ref[:high, :] += dot_plain(grad_score, queries)
        dq_ref[low:high, :] = jnp.transpose(dot_plain(kt_ref[:, :high], grad_score))


def attend_back(queries, keys, values, starts, norm, out, grads):
    length, width = queries.shape
    heads = width // HEAD_DIM
    by_head = pl.BlockSpec((length, HEAD_DIM), lambda h: (0, h))
    shared = pl.BlockSpec((length, HEAD_DIM), lambda h: (0, 0))
    return pl.pallas_call(
        functools.partial(attend_back_kernel, block_rows_of(length)),
        grid=(heads,),
        in_specs=[
            by_head,
            shared,
            pl.BlockSpec((HEAD_DIM, length), lambda h: (0, 0)),
            shared,
            pl.BlockSpec((1, length), lambda h: (0, 0)),
            pl.BlockSpec((1, 1, length), lambda h: (h, 0, 0)),
            by_head,
            by_head,
        ],
        out_specs=[by_head, shared, shared],
        out_shape=[
            jax.ShapeDtypeStruct((length, width), f32),
            jax.ShapeDtypeStruct((length, HEAD_DIM), f32),
            jax.ShapeDtypeStruct((length, HEAD_DIM), f32),
        ],
        compiler_params=pltpu.CompilerParams(vmem_limit_bytes=56 << 20),
        cost_estimate=pl.CostEstimate(
            flops=7 * heads * length * length * HEAD_DIM,
            bytes_accessed=16 * length * width,
            transcendentals=heads * length * length,
        ),
        name="attend_back",
    )(queries, keys, jnp.transpose(keys), values, starts, norm, out, grads)


def per_device(
    layer_input,
    output_grad,
    layer_keep,
    group_ids,
    exit_scale,
    doc_lengths,
    attention_gain,
    query_weight,
    key_weight,
    value_weight,
    output_weight,
    feedforward_gain,
    gate_weight,
    up_weight,
    down_weight,
):
    tokens, width = layer_input.shape[1:]
    ring = lax.axis_size("fsdp")
    planes = lax.axis_size("dp")
    place = lax.axis_index("fsdp")
    length = tokens * ring
    own_rows = query_weight.shape[0]
    heads = HEADS // ring
    own_width = heads * HEAD_DIM
    ff_own = gate_weight.shape[1]
    rows = layer_input[0].astype(f32)
    keep = layer_keep[0].astype(f32)

    inv_first = rms_scale(rows)
    normed = lax.all_gather((rows * inv_first).astype(bf16), "fsdp", axis=0, tiled=True)

    gain_mine = attention_gain.astype(f32)[:, None]
    sharers = ring // KV_HEADS
    cols = own_width + 2 * HEAD_DIM

    def spread(weight):
        heads_of = (weight.astype(f32) * gain_mine).astype(bf16).reshape(own_rows, KV_HEADS, 1, HEAD_DIM)
        return jnp.broadcast_to(heads_of, (own_rows, KV_HEADS, sharers, HEAD_DIM)).reshape(
            own_rows, ring, HEAD_DIM
        )

    query_scaled = (query_weight.astype(f32) * gain_mine).astype(bf16).reshape(own_rows, ring, own_width)
    sent = jnp.concatenate([query_scaled, spread(key_weight), spread(value_weight)], -1)
    sent = jnp.transpose(sent, (1, 0, 2)).reshape(ring * own_rows, cols)
    plane_cols = lax.all_to_all(sent, "fsdp", split_axis=0, concat_axis=0, tiled=True)
    project = jnp.concatenate(plane_gather(plane_cols), 0)

    picked = jnp.sum(
        jnp.where(jnp.arange(exit_scale.shape[0], dtype=jnp.int32) == group_ids[0], exit_scale, 0.0)
    )
    cotangent = output_grad[0].astype(f32) * picked
    direct = keep * cotangent
    direct_all = jnp.concatenate(plane_gather(direct.astype(bf16)), 0)

    gain_second = lax.all_gather(
        lax.all_gather(feedforward_gain, "fsdp", axis=0, tiled=False), "dp", axis=0, tiled=False
    ).reshape(width).astype(f32)

    output_full = lax.all_gather(output_weight, ("dp", "fsdp"), axis=0, tiled=True)
    gate_up = jnp.concatenate([gate_weight, up_weight], 1)
    gate_up = lax.all_gather(gate_up, "fsdp", axis=0, tiled=True)
    down_use = lax.all_gather(down_weight, "fsdp", axis=0, tiled=True)

    cosine, sine_part = rotary_tables(length)
    ends = jnp.sum(
        jnp.where(
            jnp.arange(doc_lengths.shape[1])[None, :] <= jnp.arange(doc_lengths.shape[1])[:, None],
            doc_lengths[0][None, :],
            0,
        ),
        1,
    )
    positions = jnp.arange(length, dtype=jnp.int32)
    starts = jnp.max(jnp.where(positions[None, :] >= ends[:, None], ends[:, None], 0), 0)[None, :]
    raw = dot_plain(normed, project)
    rotated = rotate(
        raw[:, : own_width + HEAD_DIM].reshape(length, heads + 1, HEAD_DIM), cosine, sine_part
    ).astype(bf16)
    queries = rotated[:, :heads].reshape(length, own_width)
    keys = rotated[:, heads]
    values = raw[:, own_width + HEAD_DIM :].astype(bf16)
    mixed, norm = attend(queries, keys, values, starts)
    attended_low = lax.all_to_all(mixed, "fsdp", split_axis=0, concat_axis=1, tiled=True)
    branch_attention = dot_plain(attended_low, output_full)
    middle = rows + branch_attention
    inv_second = rms_scale(middle)
    second_mine = (middle * inv_second * gain_second).astype(bf16)

    second_all = jnp.concatenate(plane_gather(second_mine), 0)
    gate_use, up_use = gate_up[:, :ff_own], gate_up[:, ff_own:]
    gate_pre = dot_plain(second_all, gate_use)
    upward = dot_plain(second_all, up_use)
    sigmoid_gate = 1.0 / (1.0 + jnp.exp(-gate_pre))
    silu_gate = gate_pre * sigmoid_gate
    hidden_low = (silu_gate * upward).astype(bf16)
    grad_hidden = dot_right_t(direct_all, down_use)
    grad_gate_low = (
        grad_hidden * upward * sigmoid_gate * (1.0 + gate_pre * (1.0 - sigmoid_gate))
    ).astype(bf16)
    grad_up_low = (grad_hidden * silu_gate).astype(bf16)
    grad_both = jnp.concatenate([grad_gate_low, grad_up_low], 1)
    second_terms = dot_right_t(grad_both, gate_up).astype(bf16).reshape(planes, tokens, width)
    grad_second = plane_scatter(second_terms)

    down_term = dot_left_t(hidden_low, direct_all).astype(bf16)
    gate_up_term = dot_left_t(second_all, grad_both).astype(bf16)
    down_grad = lax.psum_scatter(down_term, "fsdp", scatter_dimension=0, tiled=True).astype(f32)
    gate_up_grad = lax.psum_scatter(
        after(gate_up_term, down_term), "fsdp", scatter_dimension=0, tiled=True
    ).astype(f32)
    branch_terms = dot_plain(hidden_low, down_use).astype(bf16).reshape(planes, tokens, width)
    branch_terms = after(branch_terms, grad_second)
    branch_feed = plane_scatter(branch_terms)
    output = (rows + keep * (branch_attention + branch_feed)).astype(bf16)

    second_gain_term = jnp.sum(grad_second * middle * inv_second, 0)
    weighted = grad_second * gain_second
    grad_middle = inv_second * weighted - middle * inv_second**3 * jnp.mean(
        weighted * middle, -1, keepdims=True
    )
    grad_branch_low = (direct + grad_middle).astype(bf16)
    grad_attended_low = dot_right_t(grad_branch_low, output_full).astype(bf16)
    grad_heads = lax.all_to_all(grad_attended_low, "fsdp", split_axis=1, concat_axis=0, tiled=True)
    dq, dk, dv = attend_back(queries, keys, values, starts, norm, mixed, grad_heads)
    turned = rotate(
        (jnp.concatenate([dq, dk], 1) * score_scale).reshape(length, heads + 1, HEAD_DIM),
        cosine,
        -sine_part,
    ).astype(bf16)
    grad_cols = jnp.concatenate([turned.reshape(length, own_width + HEAD_DIM), dv.astype(bf16)], 1)
    normed_terms = dot_right_t(grad_cols, project).astype(bf16)
    weighted_first = lax.psum_scatter(normed_terms, "fsdp", scatter_dimension=0, tiled=True).astype(f32)
    grad_rows = inv_first * weighted_first - rows * inv_first**3 * jnp.mean(
        weighted_first * rows, -1, keepdims=True
    )
    input_grad = cotangent + grad_middle + grad_rows

    project_term = dot_left_t(normed, grad_cols).astype(bf16).reshape(planes, ring * own_rows, cols)
    project_plane = plane_scatter(project_term).astype(bf16)
    back = lax.all_to_all(project_plane, "fsdp", split_axis=0, concat_axis=0, tiled=True)
    back = back.reshape(ring, own_rows, cols).astype(f32)

    def collect(low):
        parts = back[:, :, low : low + HEAD_DIM].reshape(KV_HEADS, sharers, own_rows, HEAD_DIM)
        return jnp.transpose(jnp.sum(parts, 1), (1, 0, 2)).reshape(own_rows, KV_HEADS * HEAD_DIM)

    query_plain = jnp.transpose(back[:, :, :own_width], (1, 0, 2)).reshape(own_rows, width)
    key_plain = collect(own_width)
    value_plain = collect(own_width + HEAD_DIM)
    first_gain_grad = (
        jnp.sum(query_plain * query_weight.astype(f32), 1)
        + jnp.sum(key_plain * key_weight.astype(f32), 1)
        + jnp.sum(value_plain * value_weight.astype(f32), 1)
    )
    attended_by_owner = jnp.transpose(
        attended_low.reshape(tokens, planes, ring, own_rows), (0, 2, 1, 3)
    ).reshape(tokens, width)
    output_term = dot_left_t(attended_by_owner, grad_branch_low).astype(bf16)
    output_plane = lax.psum_scatter(output_term, "fsdp", scatter_dimension=0, tiled=True)
    output_grad_weight = plane_scatter(output_plane.reshape(planes, own_rows, width))
    second_gain_all = lax.psum(lax.psum(second_gain_term, "fsdp"), "dp")
    mine = (lax.axis_index("dp") * ring + place) * own_rows
    second_gain_grad = lax.dynamic_slice_in_dim(second_gain_all, mine, own_rows)
    return (
        output[None],
        input_grad[None],
        first_gain_grad,
        query_plain * gain_mine,
        key_plain * gain_mine,
        value_plain * gain_mine,
        output_grad_weight,
        second_gain_grad,
        gate_up_grad[:, :ff_own],
        gate_up_grad[:, ff_own:],
        down_grad,
    )


TO_CORE = (7, 3, 5, 1)
TO_CHIPS = (6, 2, 4, 0)
VMEM = pl.BlockSpec(memory_space=pltpu.VMEM)
SMEM = pl.BlockSpec(memory_space=pltpu.SMEM)
log2_e = math.log2(math.e)


def turn(block, cosine, sine, forward):
    rolled = pltpu.roll(block, HEAD_DIM // 2, 1)
    return block * cosine + rolled * sine if forward else block * cosine - rolled * sine


def masked_scores(keys, queries, starts, low):
    scores = dot_right_t(keys, queries) * (score_scale * log2_e)
    key_pos = lax.broadcasted_iota(jnp.int32, scores.shape, 0)
    query_pos = lax.broadcasted_iota(jnp.int32, scores.shape, 1) + low
    return scores, (key_pos <= query_pos) & (key_pos >= starts)


anywhere = pl.BlockSpec(memory_space=pl.ANY)


def whole_of(array):
    return pl.BlockSpec(array.shape, lambda i: (0,) * len(array.shape))


def front_kernel(at_ref, normed_ref, *refs):
    first_ref, refs = refs[0], refs[1:]
    down_ref, held_ref, sem, refs = refs[-4], refs[-2], refs[-1], (*refs[:-4], refs[-3])
    devices, tokens = normed_ref.shape[:2]
    chunk = first_ref.shape[1] - tokens
    copies = [
        pltpu.make_async_copy(
            first_ref.at[device, pl.ds(tokens, chunk)],
            held_ref.at[pl.ds(device * chunk, chunk)],
            sem.at[device],
        )
        for device in range(devices)
    ]
    for copy in copies:
        copy.start()
    out = pltpu.make_async_copy(held_ref, down_ref, sem.at[devices])

    def midway():
        for copy in copies:
            copy.wait()
        out.start()

    front_body(midway, at_ref, normed_ref, *refs)
    out.wait()


def front_body(midway, at_ref, normed_ref, *refs):
    columns_refs, refs = refs[:2], refs[2:]
    cos_ref, sin_ref, starts_ref, refs = refs[0], refs[1], refs[2], refs[3:]
    q_ref, k_ref, v_ref, mixed_ref, norm_ref, project_ref, gain_ref, vt_ref = refs
    place = at_ref[0]
    devices, tokens = normed_ref.shape[:2]
    length = devices * tokens
    core = place & 1
    group = place >> 1
    rows = columns_refs[0].shape[2] - 16
    q_width = q_ref.shape[1]
    q_all = 2 * q_width
    for owner in range(4):
        for bit in range(4):
            for side in range(2):
                block = columns_refs[side]
                device = 2 * (group ^ bit) + (core ^ side)
                here = pl.ds(pl.multiple_of((owner * 8 + device) * rows, rows), rows)
                for which in range(2):

                    @pl.when(core == which)
                    def _():
                        project_ref[here, :q_width] = block[owner, bit, :rows, which * q_width : (which + 1) * q_width]

                project_ref[here, q_width:] = block[owner, bit, :rows, q_all:]
                gain_ref[owner * 8 + device] = block[owner, bit, rows:, :HEAD_DIM]

    for device in range(devices):
        here = slice(device * tokens, (device + 1) * tokens)
        raw = dot_plain(normed_ref[device], project_ref[...])
        cosine, sine = cos_ref[here, :], sin_ref[here, :]
        for low in range(0, q_width, HEAD_DIM):
            q_ref[here, low : low + HEAD_DIM] = turn(
                raw[:, low : low + HEAD_DIM], cosine, sine, True
            ).astype(bf16)
        k_ref[here, :] = turn(raw[:, q_width : q_width + HEAD_DIM], cosine, sine, True).astype(bf16)
        v_ref[here, :] = raw[:, q_width + HEAD_DIM :].astype(bf16)
    midway()
    vt_ref[...] = jnp.transpose(v_ref[...].astype(f32)).astype(bf16)
    block = 256
    for head in range(q_width // HEAD_DIM):
        cols = slice(head * HEAD_DIM, (head + 1) * HEAD_DIM)
        for low in range(0, length, block):
            high = low + block
            scores, allowed = masked_scores(
                k_ref[:high, :], q_ref[low:high, cols], starts_ref[:, low:high], low
            )
            scores = jnp.where(allowed, scores, mask_fill)
            top = jnp.max(scores, 0, keepdims=True)
            expo = jnp.exp2(scores - top)
            total = jnp.sum(expo, 0, keepdims=True)
            probs = (expo * (1.0 / total)).astype(bf16)
            mixed_ref[low:high, cols] = jnp.transpose(dot_plain(vt_ref[:, :high], probs)).astype(bf16)
            norm_ref[head, :, low:high] = top + jnp.log2(total)


def front(at, first, tokens, columns, columns_other, cosine, sine, starts):
    length = 8 * tokens
    q_width = (columns.shape[3] - 2 * HEAD_DIM) // 2
    cols = q_width + 2 * HEAD_DIM
    width = 32 * (columns.shape[2] - 16)
    shapes = [
        jax.ShapeDtypeStruct((length, q_width), bf16),
        jax.ShapeDtypeStruct((length, HEAD_DIM), bf16),
        jax.ShapeDtypeStruct((length, HEAD_DIM), bf16),
        jax.ShapeDtypeStruct((length, q_width), bf16),
        jax.ShapeDtypeStruct((q_width // HEAD_DIM, 1, length), f32),
        jax.ShapeDtypeStruct((width, cols), bf16),
        jax.ShapeDtypeStruct((32, 16, HEAD_DIM), bf16),
    ]
    return pl.pallas_call(
        front_kernel,
        grid=(1,),
        in_specs=[SMEM, pl.BlockSpec((8, tokens, width), lambda i: (0, 0, 0)), anywhere]
        + [whole_of(x) for x in (columns, columns_other, cosine, sine, starts)],
        out_specs=[whole_of(x) for x in shapes] + [anywhere],
        out_shape=shapes + [jax.ShapeDtypeStruct((8 * (first.shape[1] - tokens), width), bf16)],
        scratch_shapes=[
            pltpu.VMEM((HEAD_DIM, length), bf16),
            pltpu.VMEM((8 * (first.shape[1] - tokens), width), bf16),
            pltpu.SemaphoreType.DMA((9,)),
        ],
        compiler_params=pltpu.CompilerParams(vmem_limit_bytes=52 << 20),
        cost_estimate=pl.CostEstimate(
            flops=2 * length * width * cols + 4 * length * length * q_width,
            bytes_accessed=2 * length * width + 4 * width * cols,
            transcendentals=length * length,
        ),
        name="front",
    )(at, first, first, columns, columns_other, cosine, sine, starts)


def back_kernel(tokens, at_ref, q_ref, k_ref, v_ref, mixed_ref, norm_ref, packed_ref, project_ref,
                cos_ref, sin_ref, starts_ref, core_ref, chips_ref, cols_ref, kt_ref, dk_ref, dv_ref,
                grad_ref):
    place = at_ref[0]
    length, q_width = q_ref.shape
    for device in range(8):
        grad_ref[device * tokens : (device + 1) * tokens, :] = packed_ref[device, :tokens, :q_width]
    block = 256
    kt_ref[...] = jnp.transpose(k_ref[...].astype(f32)).astype(bf16)
    dk_ref[...] = jnp.zeros_like(dk_ref)
    dv_ref[...] = jnp.zeros_like(dv_ref)
    for head in range(q_width // HEAD_DIM):
        cols = slice(head * HEAD_DIM, (head + 1) * HEAD_DIM)
        for low in range(0, length, block):
            high = low + block
            queries, grads = q_ref[low:high, cols], grad_ref[low:high, cols]
            scores, allowed = masked_scores(k_ref[:high, :], queries, starts_ref[:, low:high], low)
            probs = jnp.where(allowed, jnp.exp2(scores - norm_ref[head, :, low:high]), 0.0)
            grad_prob = dot_right_t(v_ref[:high, :], grads)
            weighed = jnp.transpose(grads.astype(f32) * mixed_ref[low:high, cols].astype(f32))
            grad_score = (probs * (grad_prob - jnp.sum(weighed, 0, keepdims=True))).astype(bf16)
            dv_ref[:high, :] += dot_plain(probs.astype(bf16), grads)
            dk_ref[:high, :] += dot_plain(grad_score, queries)
            dq = jnp.transpose(dot_plain(kt_ref[:, :high], grad_score)) * score_scale
            cols_ref[low:high, cols] = turn(
                dq, cos_ref[low:high, :], sin_ref[low:high, :], False
            ).astype(bf16)
    cols_ref[:, q_width : q_width + HEAD_DIM] = turn(
        dk_ref[...] * score_scale, cos_ref[...], sin_ref[...], False
    ).astype(bf16)
    cols_ref[:, q_width + HEAD_DIM :] = dv_ref[...].astype(bf16)
    for out_ref, bits in ((core_ref, TO_CORE), (chips_ref, TO_CHIPS)):
        for step, bit in enumerate(bits):
            here = pl.ds(pl.multiple_of((place ^ bit) * tokens, tokens), tokens)
            out_ref[step] = dot_right_t(cols_ref[here, :], project_ref[...]).astype(bf16)


def back(at, queries, keys, values, mixed, norm, grads, project, cosine, sine, starts):
    length, q_width = queries.shape
    width, cols = project.shape
    tokens = length // 8
    return pl.pallas_call(
        functools.partial(back_kernel, tokens),
        in_specs=[SMEM] + [VMEM] * 10,
        out_specs=[VMEM] * 3,
        out_shape=[
            jax.ShapeDtypeStruct((4, tokens, width), bf16),
            jax.ShapeDtypeStruct((4, tokens, width), bf16),
            jax.ShapeDtypeStruct((length, cols), bf16),
        ],
        scratch_shapes=[
            pltpu.VMEM((HEAD_DIM, length), bf16),
            pltpu.VMEM((length, HEAD_DIM), f32),
            pltpu.VMEM((length, HEAD_DIM), f32),
            pltpu.VMEM((length, q_width), bf16),
        ],
        compiler_params=pltpu.CompilerParams(vmem_limit_bytes=52 << 20),
        cost_estimate=pl.CostEstimate(
            flops=600 * length * width * cols + 7 * length * length * q_width,
            bytes_accessed=2 * length * width + 2 * width * cols,
            transcendentals=length * length,
        ),
        name="back",
    )(at, queries, keys, values, mixed, norm, grads, project, cosine, sine, starts)


def project_grad_kernel(first_ref, cols_ref, out_ref):
    normed = first_ref[...].reshape(cols_ref.shape[0], first_ref.shape[2])
    out_ref[...] = jnp.transpose(dot_left_t(cols_ref[...], normed)).astype(bf16)


def project_grad(first, grad_cols):
    length, cols = grad_cols.shape
    width = first.shape[2]
    part = 512
    return pl.pallas_call(
        project_grad_kernel,
        grid=(width // part,),
        in_specs=[
            pl.BlockSpec((8, length // 8, part), lambda i: (0, 0, i)),
            pl.BlockSpec((length, cols), lambda i: (0, 0)),
        ],
        out_specs=pl.BlockSpec((part, cols), lambda i: (i, 0)),
        out_shape=jax.ShapeDtypeStruct((width, cols), bf16),
        compiler_params=pltpu.CompilerParams(vmem_limit_bytes=52 << 20),
        cost_estimate=pl.CostEstimate(
            flops=20 * length * width * cols, bytes_accessed=2 * length * width, transcendentals=0
        ),
        name="project_grad",
    )(first, grad_cols)


def output_grad_kernel(at_ref, packed_ref, attended_ref, out_ref):
    own = packed_ref.shape[2] // 2
    rows = out_ref.shape[1] - 16
    tokens = packed_ref.shape[1] - 16
    total = None
    gain = None
    for device in range(8):
        term = dot_left_t(
            packed_ref[device, :tokens, own:], attended_ref[device * tokens : (device + 1) * tokens, :]
        )
        extra = jnp.sum(packed_ref[device, tokens:, own:].astype(f32), 0, keepdims=True)
        total = term if total is None else total + term
        gain = extra if gain is None else gain + extra
    turned = jnp.transpose(total).astype(bf16)
    first = lax.broadcasted_iota(jnp.int32, (16, own), 0) == 0
    gain_rows = jnp.where(first, jnp.broadcast_to(gain, (16, own)), 0.0)
    for owner in range(4):
        out_ref[owner, :rows, :] = turned[owner * rows : (owner + 1) * rows, :]
        here = jnp.where(at_ref[0] // 2 == owner, 1.0, 0.0)
        out_ref[owner, rows:, :] = (gain_rows * here).astype(bf16)


def output_grad_term(at, packed, attended):
    length, width = attended.shape
    own = packed.shape[2] // 2
    return pl.pallas_call(
        output_grad_kernel,
        in_specs=[SMEM] + [VMEM] * 2,
        out_specs=VMEM,
        out_shape=jax.ShapeDtypeStruct((4, width // 4 + 16, own), bf16),
        compiler_params=pltpu.CompilerParams(vmem_limit_bytes=52 << 20),
        cost_estimate=pl.CostEstimate(
            flops=60 * length * own * width, bytes_accessed=2 * length * width, transcendentals=0
        ),
        name="output_grad_term",
    )(at, packed, attended)


def place_blocks(plane, blocks, out_ref):
    tokens = blocks[0].shape[0]
    for block, move in zip(blocks, LINE):
        owner = plane + move if move != 3 else 3 - plane
        valid = (owner >= 0) & (owner <= 3) if move != 3 else (plane == 0) | (plane == 3)

        @pl.when(valid)
        def _():
            out_ref[pl.ds(pl.multiple_of(owner * tokens, tokens), tokens), :] = block[...]


def feed_kernel(units, count, n_count, at_ref, *refs):
    d_refs, n_refs, refs = refs[:4], refs[4 : 4 + n_count], refs[4 + n_count :]
    both_ref, down_ref, rows_ref, refs = *refs[:3], refs[3 + count :]
    second_ref, direct_ref, hidden_ref, grads_ref, term_ref, held_ref = refs
    step = pl.program_id(0)

    @pl.when(step == 0)
    def _():
        tokens = d_refs[0].shape[0]
        for slot in range(4):
            owner = (at_ref[1] - slot) & 3
            direct_ref[pl.ds(pl.multiple_of(owner * tokens, tokens), tokens), :] = d_refs[slot][...]
        if n_count == 6:
            place_blocks(at_ref[1], n_refs, second_ref)
        else:
            second_ref[...] = n_refs[0][...].reshape(second_ref.shape)

    @pl.when(step < units)
    def _():
        raw = dot_plain(second_ref[...], both_ref[...])
        half = raw.shape[1] // 2
        gate, upward = raw[:, :half], raw[:, half:]
        sig = 1.0 / (1.0 + jnp.exp(-gate))
        silu = gate * sig
        hidden_ref[...] = (silu * upward).astype(bf16)
        grad_hidden = dot_right_t(direct_ref[...], down_ref[...])
        grad_gate = (grad_hidden * upward * sig * (1.0 + gate * (1.0 - sig))).astype(bf16)
        grads = jnp.concatenate([grad_gate, (grad_hidden * silu).astype(bf16)], 1)
        grads_ref[...] = grads
        held_ref[step] = grads

    @pl.when(step >= units)
    def _():
        total = None
        for unit in range(units):
            cols = slice(unit * held_ref.shape[2], (unit + 1) * held_ref.shape[2])
            part = dot_right_t(held_ref[unit], rows_ref[:, cols])
            total = part if total is None else total + part
        term_ref[...] = total.astype(bf16).reshape(term_ref.shape)


def feed(at, part_at, parts_of, seconds, directs, both, down, so_far):
    tokens, width = seconds[0].shape[-2:]
    some = 4 * tokens
    ff = down.shape[0]
    n_count = len(seconds)
    gathered = pl.BlockSpec((4, tokens, width), lambda i: (0, 0, 0))
    single = pl.BlockSpec((tokens, width), lambda i: (0, 0))
    unit, part = 128, 256
    units, parts = ff // unit, width // part
    so_far = so_far or []
    total = parts_of * some
    outs = pl.pallas_call(
        functools.partial(feed_kernel, units, len(so_far), n_count),
        grid=(units + parts,),
        in_specs=[
            SMEM,
            *[pl.BlockSpec((tokens, width), lambda i: (part_at, 0))] * 4,
            *[single if n_count == 6 else gathered] * n_count,
            pl.BlockSpec((width, 2 * unit), lambda i: (0, jnp.minimum(i, units - 1))),
            pl.BlockSpec((unit, width), lambda i: (jnp.minimum(i, units - 1), 0)),
            pl.BlockSpec((part, 2 * ff), lambda i: (jnp.maximum(i - units, 0), 0)),
        ]
        + [pl.BlockSpec(memory_space=pl.ANY)] * len(so_far),
        out_specs=[
            pl.BlockSpec((some, width), lambda i: (part_at, 0)),
            pl.BlockSpec((some, width), lambda i: (part_at, 0)),
            pl.BlockSpec((some, unit), lambda i: (part_at, jnp.minimum(i, units - 1))),
            pl.BlockSpec((some, 2 * unit), lambda i: (part_at, jnp.minimum(i, units - 1))),
            pl.BlockSpec((4, tokens, part), lambda i: (0, 0, jnp.maximum(i - units, 0))),
        ],
        out_shape=[
            jax.ShapeDtypeStruct((total, width), bf16),
            jax.ShapeDtypeStruct((total, width), bf16),
            jax.ShapeDtypeStruct((total, ff), bf16),
            jax.ShapeDtypeStruct((total, 2 * ff), bf16),
            jax.ShapeDtypeStruct((4, tokens, width), bf16),
        ],
        scratch_shapes=[pltpu.VMEM((units, some, 2 * unit), bf16)],
        input_output_aliases={8 + n_count + i: i for i in range(len(so_far))},
        compiler_params=pltpu.CompilerParams(vmem_limit_bytes=52 << 20),
        cost_estimate=pl.CostEstimate(
            flops=10 * some * width * ff,
            bytes_accessed=10 * width * ff,
            transcendentals=some * ff,
        ),
        name="feed",
    )(at, *directs, *seconds, both, down, both, *so_far)
    return outs[:4], outs[4]


def branch_kernel(hidden_ref, down_ref, out_ref):
    out_ref[...] = dot_plain(hidden_ref[...], down_ref[...]).astype(bf16).reshape(out_ref.shape)


def branch(hidden, down, parts):
    rows, ff = hidden.shape
    width = down.shape[1]
    tokens = rows // (4 * parts)
    return pl.pallas_call(
        branch_kernel,
        grid=(parts, 4),
        in_specs=[
            pl.BlockSpec((4 * tokens, ff), lambda h, i: (h, 0)),
            pl.BlockSpec((ff, width // 4), lambda h, i: (0, i)),
        ],
        out_specs=pl.BlockSpec((4, tokens, width // 4), lambda h, i: (0, h, i)),
        out_shape=jax.ShapeDtypeStruct((4, parts * tokens, width), bf16),
        compiler_params=pltpu.CompilerParams(vmem_limit_bytes=52 << 20),
        cost_estimate=pl.CostEstimate(flops=1 << 20, bytes_accessed=1 << 16, transcendentals=0),
        name="branch",
    )(hidden, down)


def split_kernel(both_ref, gate_ref, up_ref):
    for low in range(0, gate_ref.shape[1], 128):
        gate_ref[:, low : low + 128] = both_ref[:, 2 * low : 2 * low + 128].astype(f32)
        up_ref[:, low : low + 128] = both_ref[:, 2 * low + 128 : 2 * low + 256].astype(f32)


def split(both):
    rows, cols = both.shape
    out = jax.ShapeDtypeStruct((rows, cols // 2), f32)
    part = pl.BlockSpec((64, cols // 2), lambda i: (i, 0))
    return pl.pallas_call(
        split_kernel,
        grid=(rows // 64,),
        in_specs=[pl.BlockSpec((64, cols), lambda i: (i, 0))],
        out_specs=[part, part],
        out_shape=[out, out],
        name="split",
    )(both)


def finish_kernel(final_ref, gain_ref, qw_ref, kw_ref, vw_ref, q_ref, k_ref, v_ref, o_ref, first_ref, second_ref):
    rows = q_ref.shape[0]
    own = q_ref.shape[1] // 8
    gain = gain_ref[...]
    first = None
    second = None
    for device in range(8):
        block = final_ref[device, :rows, :].astype(f32)
        cols = slice(device * own, (device + 1) * own)
        head = slice(device // 2 * HEAD_DIM, (device // 2 + 1) * HEAD_DIM)
        out_ref, weight_ref = ((k_ref, kw_ref), (v_ref, vw_ref))[device % 2]
        query, shared = block[:, :own], block[:, own : own + HEAD_DIM]
        q_ref[:, cols] = query * gain
        out_ref[:, head] = shared * gain
        o_ref[:, cols] = block[:, own + HEAD_DIM :]
        term = jnp.sum(query * qw_ref[:, cols].astype(f32), 1, keepdims=True) + jnp.sum(
            shared * weight_ref[:, head].astype(f32), 1, keepdims=True
        )
        extra = jnp.sum(final_ref[device, rows:, :HEAD_DIM].astype(f32), 0, keepdims=True)
        first = term if first is None else first + term
        second = extra if second is None else second + extra
    first_ref[...] = first
    second_ref[...] = second


def finish(final, gain, query_weight, key_weight, value_weight):
    def like(weight):
        return jax.ShapeDtypeStruct(weight.shape, f32)

    rows = query_weight.shape[0]
    return pl.pallas_call(
        finish_kernel,
        in_specs=[VMEM] * 5,
        out_specs=[VMEM] * 6,
        out_shape=[
            like(query_weight),
            like(key_weight),
            like(value_weight),
            like(query_weight),
            jax.ShapeDtypeStruct((rows, 1), f32),
            jax.ShapeDtypeStruct((1, HEAD_DIM), f32),
        ],
        compiler_params=pltpu.CompilerParams(vmem_limit_bytes=32 << 20),
        name="finish",
    )(final, gain, query_weight, key_weight, value_weight)


def middle_back_kernel(low_ref, high_ref, middle_ref, inv_ref, gain_ref, direct_ref, weight_ref,
                       packed_ref, grad_ref, branch_ref):
    tokens, width = grad_ref.shape
    half = tokens // 2
    own = weight_ref.shape[0] // 2
    step = pl.program_id(0)

    @pl.when(step == 0)
    def _():
        for first, ref in ((0, low_ref), (half, high_ref)):
            here = slice(first, first + half)
            total = ref[0].astype(f32)
            for plane in (1, 2, 3):
                total = total + ref[plane].astype(f32)
            middle, inv = middle_ref[here, :], inv_ref[here, :]
            weighted = total * gain_ref[...]
            grad = inv * weighted - middle * inv**3 * jnp.mean(weighted * middle, -1, keepdims=True)
            grad_ref[here, :] = grad
            branch_ref[here, :] = (direct_ref[here, :] + grad).astype(bf16)
            term = jnp.sum(total * middle * inv, 0, keepdims=True)
            gain_term = term if first == 0 else gain_term + term
        gain_high = gain_term.astype(bf16).astype(f32)
        row = lax.broadcasted_iota(jnp.int32, (16, width), 0)
        branch_ref[tokens:, :] = jnp.where(
            row == 0, gain_high, jnp.where(row == 1, gain_term - gain_high, 0.0)
        ).astype(bf16)

    grads = dot_right_t(branch_ref[:tokens, :], weight_ref[...]).astype(bf16)
    for which in range(2):
        packed_ref[which, :tokens, :own] = grads[:, which * own : (which + 1) * own]
        packed_ref[which, tokens:, :own] = jnp.zeros((16, own), bf16)
        at_col = pl.multiple_of((2 * step + which) * own, own)
        packed_ref[which, :, own:] = branch_ref[:, pl.ds(at_col, own)]


def middle_back(low, high, middle, inv, gain, direct, weight):
    tokens, width = middle.shape
    own = width // 8
    whole = pl.BlockSpec((4, tokens // 2, width), lambda i: (0, 0, 0))
    rows = pl.BlockSpec((tokens, width), lambda i: (0, 0))
    return pl.pallas_call(
        middle_back_kernel,
        grid=(4,),
        in_specs=[
            whole,
            whole,
            rows,
            pl.BlockSpec((tokens, 1), lambda i: (0, 0)),
            pl.BlockSpec((1, width), lambda i: (0, 0)),
            rows,
            pl.BlockSpec((2 * own, width), lambda i: (i, 0)),
        ],
        out_specs=[pl.BlockSpec((2, tokens + 16, 2 * own), lambda i: (i, 0, 0)), rows],
        out_shape=[
            jax.ShapeDtypeStruct((8, tokens + 16, 2 * own), bf16),
            jax.ShapeDtypeStruct((tokens, width), f32),
        ],
        scratch_shapes=[pltpu.VMEM((tokens + 16, width), bf16)],
        compiler_params=pltpu.CompilerParams(vmem_limit_bytes=48 << 20),
        cost_estimate=pl.CostEstimate(
            flops=2 * tokens * width * width, bytes_accessed=3 * width * width, transcendentals=0
        ),
        name="middle_back",
    )(low, high, middle, inv, gain, direct, weight)


def middle_kernel(parts_ref, weight_ref, rows_ref, gain_ref, attended_ref, branch_ref, middle_ref, inv_ref,
                  low_ref, high_ref, total_ref):
    step = pl.program_id(0)
    own = parts_ref.shape[2]
    attended_ref[:, :own] = parts_ref[0]
    attended_ref[:, own:] = parts_ref[1]
    term = dot_plain(attended_ref[...], weight_ref[...])

    @pl.when(step == 0)
    def _():
        total_ref[...] = term

    @pl.when(step > 0)
    def _():
        total_ref[...] += term

    @pl.when(step == pl.num_programs(0) - 1)
    def _():
        half = low_ref.shape[0]
        branch = total_ref[...]
        middle = rows_ref[...].astype(f32) + branch
        inv = rms_scale(middle)
        branch_ref[...] = branch
        middle_ref[...] = middle
        inv_ref[...] = inv
        second = (middle * inv * gain_ref[...]).astype(bf16)
        low_ref[...] = second[:half]
        high_ref[...] = second[half:]


def middle_forward(parts, weight, rows, gain):
    devices, tokens, own = parts.shape
    width = weight.shape[1]
    half = pl.BlockSpec((tokens // 2, width), lambda i: (0, 0))
    whole = pl.BlockSpec((tokens, width), lambda i: (0, 0))
    return pl.pallas_call(
        middle_kernel,
        grid=(devices // 2,),
        in_specs=[
            pl.BlockSpec((2, tokens, own), lambda i: (i, 0, 0)),
            pl.BlockSpec((2 * own, width), lambda i: (i, 0)),
            whole,
            pl.BlockSpec((1, width), lambda i: (0, 0)),
        ],
        out_specs=[
            pl.BlockSpec((tokens, 2 * own), lambda i: (0, i)),
            whole,
            whole,
            pl.BlockSpec((tokens, 1), lambda i: (0, 0)),
            half,
            half,
        ],
        out_shape=[
            jax.ShapeDtypeStruct((tokens, devices * own), bf16),
            jax.ShapeDtypeStruct((tokens, width), f32),
            jax.ShapeDtypeStruct((tokens, width), f32),
            jax.ShapeDtypeStruct((tokens, 1), f32),
            jax.ShapeDtypeStruct((tokens // 2, width), bf16),
            jax.ShapeDtypeStruct((tokens // 2, width), bf16),
        ],
        scratch_shapes=[pltpu.VMEM((tokens, width), f32)],
        compiler_params=pltpu.CompilerParams(vmem_limit_bytes=48 << 20),
        cost_estimate=pl.CostEstimate(
            flops=2 * tokens * width * width, bytes_accessed=3 * width * width, transcendentals=0
        ),
        name="middle_forward",
    )(parts, weight, rows, gain)


def fast_device(
    layer_input,
    output_grad,
    layer_keep,
    group_ids,
    exit_scale,
    doc_lengths,
    attention_gain,
    query_weight,
    key_weight,
    value_weight,
    output_weight,
    feedforward_gain,
    gate_weight,
    up_weight,
    down_weight,
):
    tokens, width = layer_input.shape[1:]
    place, plane = lax.axis_index("fsdp"), lax.axis_index("dp")
    at = jnp.stack([place, plane]).astype(jnp.int32)
    length = tokens * 8
    own_rows = query_weight.shape[0]
    q_width = HEADS // 8 * HEAD_DIM
    cols = q_width + 2 * HEAD_DIM
    ff_own = gate_weight.shape[1]
    half = tokens // 2
    rows = layer_input[0].astype(f32)
    keep = layer_keep[0].astype(f32)

    both_mine = jnp.stack(
        [gate_weight.reshape(-1, ff_own // 128, 128), up_weight.reshape(-1, ff_own // 128, 128)], 2
    ).reshape(-1, 2 * ff_own)
    inv_first = rms_scale(rows)
    normed = (rows * inv_first).astype(bf16)
    first = lax.all_gather(jnp.concatenate([normed, down_weight], 0), "fsdp", axis=0, tiled=False)
    gain_mine = attention_gain.astype(f32)[:, None]

    def by_chip(weight):
        scaled = (weight.astype(f32) * gain_mine).astype(bf16)
        return scaled.reshape(own_rows, 4, weight.shape[1] // 4)

    sent = jnp.concatenate([by_chip(query_weight), by_chip(key_weight), by_chip(value_weight)], -1)
    sent = jnp.transpose(sent, (1, 0, 2))
    wide = sent.shape[2]
    gain_rows = jnp.pad(feedforward_gain[None, :], ((0, 15), (0, wide - own_rows)))
    group = place // 2

    def to_chip(bit):
        block = lax.dynamic_index_in_dim(sent, group ^ bit, 0, keepdims=False)
        return jnp.concatenate([block, gain_rows], 0)

    picked = jnp.sum(
        jnp.where(jnp.arange(exit_scale.shape[0], dtype=jnp.int32) == group_ids[0], exit_scale, 0.0)
    )
    cotangent = output_grad[0].astype(f32) * picked
    direct = keep * cotangent
    direct_low = direct.astype(bf16)
    direct_1 = shift(direct_low, 1)
    columns = jnp.stack([to_chip(0)] + [flip(to_chip(bit), 2 * bit) for bit in (1, 2, 3)])
    output_plane = gather_planes(after(output_weight, columns, direct_1))
    columns = gather_planes(after(columns, output_plane))
    columns_other = flip(columns, 1)
    output_full = lax.all_gather(output_plane, "fsdp", axis=1, tiled=True).reshape(width, width)
    both = lax.all_gather(after(both_mine, columns), "fsdp", axis=0, tiled=True)
    half_dim = HEAD_DIM // 2
    frequency = rope_base ** (-(2.0 * np.arange(HEAD_DIM // 2, dtype=np.float32)) / HEAD_DIM)
    angles = np.arange(length, dtype=np.float32)[:, None] * frequency.astype(np.float32)[None, :]
    cosine = jnp.asarray(np.concatenate([np.cos(angles), np.cos(angles)], 1).astype(np.float32))
    sine = jnp.asarray(np.concatenate([-np.sin(angles), np.sin(angles)], 1).astype(np.float32))
    order = jnp.arange(doc_lengths.shape[1])
    ends = jnp.sum(jnp.where(order[None, :] <= order[:, None], doc_lengths[0][None, :], 0), 1)
    positions = jnp.arange(length, dtype=jnp.int32)
    starts = jnp.max(jnp.where(positions[None, :] >= ends[:, None], ends[:, None], 0), 0)[None, :]

    direct_2 = shift(after(direct_low, columns), 2)
    queries, keys, values, mixed, norm, project, gains, down_use = front(
        at, first, tokens, columns, columns_other, cosine, sine, starts
    )
    gain_second = gains[:, 0, :own_rows].reshape(width).astype(f32)

    parts = lax.all_to_all(mixed.reshape(8, tokens, q_width), "fsdp", split_axis=0, concat_axis=0)
    direct_3 = shift(after(direct_low, columns), 3)
    parts = after(parts, direct_2)
    attended_low, branch_attention, middle, inv_second, second_low, second_high = middle_forward(
        parts, output_full, layer_input[0], gain_second[None, :]
    )
    directs = [direct_low, direct_1, direct_2, direct_3]
    second_half = after(second_low, direct_3)
    second_near = line_first(second_half)
    seconds_low = [second_half, *second_near, *line_second(*second_near)]
    attended_all = lax.all_gather(after(attended_low, *seconds_low), "fsdp", axis=0, tiled=True)
    seconds_high = gather_planes(after(second_high, *seconds_low))

    stacked, terms_low = feed(at, 0, 2, seconds_low, directs, both, down_use, None)
    stacked, terms_high = feed(at, 1, 2, [seconds_high], directs, both, down_use, stacked)
    second_all, direct_all, hidden_all, grads_all = stacked
    got_low = swap_planes(terms_low)

    branch_terms = branch(hidden_all, down_use, 2)
    down_term = dot_left_t(after(hidden_all, got_low), direct_all).astype(bf16)
    both_term = dot_left_t(second_all, grads_all).astype(bf16)
    got_high = after(swap_planes(after(terms_high, got_low)), branch_terms, both_term)
    down_grad = lax.psum_scatter(down_term, "fsdp", scatter_dimension=0, tiled=True).astype(f32)
    both_grad = lax.psum_scatter(both_term, "fsdp", scatter_dimension=0, tiled=True)

    to_send, grad_middle = middle_back(
        got_low, got_high, middle, inv_second, gain_second[None, :], direct, output_full
    )
    packed = lax.all_to_all(to_send, "fsdp", split_axis=0, concat_axis=0)

    def ahead(step):
        return lax.dynamic_index_in_dim(branch_terms, jnp.clip(step, 0, 3), 0, keepdims=False)

    branch_up2 = lax.ppermute(after(ahead(plane + 2), to_send), "dp", UP[:2])
    branch_down2 = lax.ppermute(after(ahead(plane - 2), to_send), "dp", DOWN[1:])
    branch_far = lax.ppermute(after(ahead(3 - plane), to_send), "dp", [(3, 1), (0, 2)])
    output_term = output_grad_term(at, packed, attended_all)
    output_got = swap_planes(output_term)
    packed = after(packed, output_term)
    core_terms, chip_terms, grad_cols = back(
        at, queries, keys, values, mixed, norm, packed, project, cosine, sine, starts
    )
    core_terms, branch_up2, branch_down2, branch_far = after_all(
        (core_terms, branch_up2, branch_down2, branch_far)
    )
    other = flip(core_terms, 1)
    project_term = project_grad(first, grad_cols)
    other = after(other, project_term)
    sums = [add_low(chip_terms[i], other[i]) for i in range(3)]
    far, near_x, near_y = flip(sums[0], 6), flip(sums[1], 2), flip(sums[2], 4)
    core = place % 2
    keys_term, values_term = project_term[:, q_width : q_width + HEAD_DIM], project_term[:, q_width + HEAD_DIM :]
    kept = jnp.where(core == 0, keys_term, values_term)
    kept = add_low(kept, flip(jnp.where(core == 0, values_term, keys_term), 1))
    project_term = jnp.concatenate([project_term[:, :q_width], kept], 1)
    kept_cols = q_width + HEAD_DIM
    project_got = swap_planes(after(project_term.reshape(4, width // 4, kept_cols), output_got))
    zero = jnp.zeros((), bf16)
    branch_up2, branch_down2, branch_far = after_all((branch_up2, branch_down2, branch_far), *sums)
    sent_up = (
        ahead(plane + 1).astype(f32)
        + branch_up2.astype(f32)
        + jnp.where(plane == 2, branch_far, zero).astype(f32)
    ).astype(bf16)
    sent_down = (
        ahead(plane - 1).astype(f32)
        + branch_down2.astype(f32)
        + jnp.where(plane == 1, branch_far, zero).astype(f32)
    ).astype(bf16)
    branch_up1 = lax.ppermute(sent_up, "dp", UP)
    branch_down1 = lax.ppermute(sent_down, "dp", DOWN)
    branch_feed = ahead(plane).astype(f32) + branch_up1.astype(f32) + branch_down1.astype(f32)
    project_plane = jnp.sum(project_got.astype(f32), 0).astype(bf16)
    output_plane_sum = jnp.sum(output_got.astype(f32), 0).astype(bf16)
    both_plane = jnp.concatenate([project_plane, output_plane_sum[: 8 * own_rows]], 1)
    gain_four = output_plane_sum[8 * own_rows].reshape(4, own_rows)
    low_half = place % 2 == 0
    gain_eight = jnp.concatenate(
        [jnp.where(low_half, gain_four, 0), jnp.where(low_half, 0, gain_four)], 0
    )
    gain_eight = jnp.pad(gain_eight[:, None, :], ((0, 0), (0, 15), (0, kept_cols + q_width - own_rows)))
    final = jnp.concatenate([both_plane.reshape(8, own_rows, kept_cols + q_width), gain_eight], 1)
    gate_grad, up_grad = split(both_grad)
    final = lax.all_to_all(after(final, far, near_x, near_y, sent_up, sent_down), "fsdp", split_axis=0, concat_axis=0)
    weighted_first = (
        chip_terms[3].astype(f32)
        + other[3].astype(f32)
        + far.astype(f32)
        + near_x.astype(f32)
        + near_y.astype(f32)
    )
    grad_rows = inv_first * weighted_first - rows * inv_first**3 * jnp.mean(
        weighted_first * rows, -1, keepdims=True
    )
    input_grad = cotangent + grad_middle + grad_rows

    output = (rows + keep * (branch_attention + branch_feed)).astype(bf16)

    final = after(final, branch_up1, branch_down1, gate_grad)
    query_grad, key_grad, value_grad, output_sum, first_gain, second_gain = finish(
        final, gain_mine, query_weight, key_weight, value_weight
    )
    return (
        output[None],
        input_grad[None],
        first_gain[:, 0],
        query_grad,
        key_grad,
        value_grad,
        output_sum,
        second_gain[0, :own_rows],
        gate_grad,
        up_grad,
        down_grad,
    )


def solution(mesh):
    both = ("dp", "fsdp")
    fast = (mesh.shape["dp"], mesh.shape["fsdp"]) == (4, 8)
    return jax.shard_map(
        fast_device if fast else per_device,
        mesh=mesh,
        in_specs=(
            P("dp", "fsdp", None),
            P("dp", "fsdp", None),
            P("dp"),
            P("dp"),
            P(),
            P("dp", None),
            P(both),
            P(both, None),
            P(both, None),
            P(both, None),
            P(both, None),
            P(both),
            P("fsdp", "dp"),
            P("fsdp", "dp"),
            P(both, None),
        ),
        out_specs=(
            P("dp", "fsdp", None),
            P("dp", "fsdp", None),
            P(both),
            P(both, None),
            P(both, None),
            P(both, None),
            P(both, None),
            P(both),
            P("fsdp", "dp"),
            P("fsdp", "dp"),
            P(both, None),
        ),
        check_vma=False,
    )
```
